32 devices in a mesh: req: 16 (over z, x, core), tp: 2 (over y).
Axes of the slice: x: 2, y: 2, z: 4, core: 2. Of those that a mesh axis runs over, the one named last changes fastest.
Arguments:
- queries: bfloat16 [512, 4096], P('req', 'tp'), may hold values from -12 to 12
- keys_values: bfloat16 [512, 1024], P('req', 'tp'), may hold values from -12 to 12
- segments: int32 [512], P('req'), may hold values from 0 to 2, as said below
- sink_logits: float32 [64], P('tp'), may hold values from 0 to 4
- out_weight: bfloat16 [4096, 2880], P('tp'), may hold values from -0.09375 to 0.09375
- out_bias: bfloat16 [2880], replicated, may hold values from -3 to 3
- residual: bfloat16 [512, 2880], P(('req', 'tp')), may hold values from -6 to 6
- norm_gain: bfloat16 [2880], replicated, may hold values from 0.5 to 1.5
- route_ids: int32 [512, 4], P(('req', 'tp')), may hold values from 0 to 15, all different within a row; in each aligned block of 16 rows (0 to 15, 16 to 31, ...) at most 8 rows name the same one
- route_logits: float32 [512, 4], P(('req', 'tp')), may hold values from -6 to 6
- gate_weight: bfloat16 [16, 2880, 2880], P('req', None, 'tp'), may hold values from -0.3125 to 0.3125
- gate_bias: bfloat16 [16, 2880], P('req', 'tp'), may hold values from -3 to 3
- up_weight: bfloat16 [16, 2880, 2880], P('req', None, 'tp'), may hold values from -0.3125 to 0.3125
- up_bias: bfloat16 [16, 2880], P('req', 'tp'), may hold values from -3 to 3
- down_weight: bfloat16 [16, 2880, 2880], P('req', 'tp'), may hold values from -0.0546875 to 0.0546875
- down_bias: bfloat16 [16, 2880], replicated, may hold values from -3 to 3
- page_table: int32 [16, 2], P('req'), may hold values from 0 to 1, each once within a row
Outputs:
- mixed_out: bfloat16 [512, 2880], P(('req', 'tp'))
- kv_cache: bfloat16 [32, 16, 1024], P('req', None, 'tp')
The draws below stay inside these ranges and needn't reach their ends.
Inputs may be any that keep to these rules, and one draw needn't show every extreme that they name: `segments`: within each group of 32 tokens the numbers start at 0, never fall and rise by at most one from token to token; every group holds exactly 3 packed requests, of uneven lengths. `route_ids`: each row names 4 different experts. Among the 16 rows of one device no expert is named by more than 8 rows, a bound that some block reaches. `page_table`: each row names every page of its group once.
All inputs are finite; a program needn't handle non-finite values.
Results may differ from the reference program's by a relative error of at most 0.018.
Values may be sent and summed in bfloat16 or wider, within the bound.
No kernel may reach another device: no remote copies, remote signals or barrier semaphores. Data moves between devices by JAX's collectives and lax.ppermute only.
A program may use at most 128 MiB of HBM per device.

```python
import math
import jax
import jax.numpy as jnp
import numpy as np
from jax import lax

D = 2880
FF = 2880
Q_HEADS = 64
KV_HEADS = 8
HEAD = 64
TOP = 4
PAGE_LEN = 16
TOK_DEV = 16
TOK_REQ = 32
TOKENS = 512
EXPERTS = 16
CAP = 8
PAGES = 2
N_REQ = 16
N_TP = 2


def seg_table(key):
    groups = TOKENS // TOK_REQ
    cuts = 2
    slots = jnp.broadcast_to(jnp.arange(TOK_REQ, dtype=jnp.int32)[None, :], (groups, TOK_REQ))
    shuffled = jax.random.permutation(jax.random.fold_in(key, 11), slots, axis=1, independent=True)
    later_cols = jnp.arange(TOK_REQ, dtype=jnp.int32)[None, :] > 0
    boundary = (shuffled < cuts) & later_cols
    extra = (shuffled == cuts) & later_cols
    zero_cut = jnp.any(shuffled[:, :1] < cuts, axis=1, keepdims=True)
    boundary = boundary | extra & zero_cut
    return jnp.cumsum(boundary.astype(jnp.int32), axis=1).astype(jnp.int32).reshape(TOKENS)


def draw_segments(key, part):
    return seg_table(key)


def attention_inputs(key):
    query_width = Q_HEADS * HEAD
    pair_width = KV_HEADS * 2 * HEAD
    queries = jnp.clip(jax.random.normal(jax.random.fold_in(key, 21), (TOKENS, query_width)), -6.0, 6.0)
    keyvals = jnp.clip(jax.random.normal(jax.random.fold_in(key, 22), (TOKENS, pair_width)), -6.0, 6.0)
    return (queries, keyvals)


def draw_queries(key, part):
    return attention_inputs(key)[0].astype(jnp.bfloat16)


def draw_keys_values(key, part):
    return attention_inputs(key)[1].astype(jnp.bfloat16)


def levels(key, extent, cuts, least, largest):
    def one(dim, blocks):
        heights = jax.random.uniform(jax.random.fold_in(jax.random.fold_in(key, 6), dim), (blocks,), jnp.float32, least / len(cuts), largest / len(cuts))
        return jnp.repeat(jnp.exp(heights), extent[dim] // blocks).reshape((-1,) + (1,) * (len(extent) - dim - 1))

    loudness = one(*cuts[0])
    for cut in cuts[1:]:
        loudness = loudness * one(*cut)
    return loudness


def deal_out(stream_key, own, number, rows, number_of, top, reach, skew):
    order = jax.random.permutation(stream_key, number_of)
    heavy_load, ordinary = shares(number_of, rows * top, reach, skew, True), shares(number_of, rows * top, reach, skew, False)
    places = jnp.arange(number_of)

    def named(sizes, rotation):
        used = int((sizes > 0).sum())
        fixed = max(1, used // 4)
        moved = fixed + (places - fixed + rotation * (used - fixed)) % max(1, number_of - fixed)
        return jnp.zeros((number_of,), jnp.int32).at[order[jnp.where(places < fixed, places, moved)]].set(jnp.asarray(sizes, jnp.int32))

    sizes = jnp.where(number % 4 == 0, named(heavy_load, number // 4), named(ordinary, number - number // 4 - 1))
    mixed = jax.random.permutation(jax.random.fold_in(own, 3), number_of)
    giver, receiver = mixed[0:number_of // 2 * 2:2], mixed[1:number_of // 2 * 2:2]
    margin = jnp.minimum(sizes[giver] - 1, reach - sizes[receiver]) // 2
    margin = jnp.where((giver == order[0]) | (receiver == order[0]) | (sizes[receiver] == 0), 0, jnp.maximum(margin, 0))
    moved = jax.random.randint(jax.random.fold_in(own, 4), (number_of // 2,), 0, 1 << 20) % (margin + 1)
    sizes = sizes.at[giver].add(-moved).at[receiver].add(moved)
    labels = jnp.searchsorted(jnp.cumsum(sizes), jnp.arange(rows * top), side="right").astype(jnp.int32)
    grid = labels.reshape(top, rows).T
    grid = grid[jax.random.permutation(jax.random.fold_in(own, 1), rows)]
    rotation = jax.random.randint(jax.random.fold_in(own, 2), (rows, 1), 0, top)
    return jnp.take_along_axis(grid, (jnp.arange(top)[None, :] + rotation) % top, axis=1)


def shares(amount, total, bound, slope, full):
    weights = [(1 << 20) // math.isqrt(grade ** slope) + 1 for grade in range(1, amount + 1)]
    largest = bound if full else min(bound, max(-(-total // amount), total * weights[0] // sum(weights)))
    least = 1 if total - largest >= amount - 1 else 0
    counts, rest = [largest] + [least] * (amount - 1), total - largest - least * (amount - 1)
    while rest > 0:
        candidates = [i for i in range(1, amount) if counts[i] < largest] or [i for i in range(1, amount) if counts[i] < bound]
        mass, remaining = sum([weights[i] for i in candidates]), rest
        for i in candidates:
            addition = min(bound - counts[i], max(1, remaining * weights[i] // mass), rest)
            counts[i] = counts[i] + addition
            rest = rest - addition
    return np.array(counts)


def normal_values(key, shape, deviation, limit, cuts=(), held_as=jnp.bfloat16):
    values = jax.random.normal(key, shape, jnp.float32) * deviation
    if len(cuts) > 0:
        values = levels(key, shape, cuts, -0.22, 0.18) * values
    return jnp.clip(values, min=-limit, max=limit).astype(held_as)


def setup_inputs(seed: int = 0) -> dict:
    seeds = jax.random.split(jax.random.key(seed), 18)
    queries = draw_queries(jax.random.fold_in(seeds[17], 71), 0)
    keys_values = draw_keys_values(jax.random.fold_in(seeds[17], 71), 0)
    segments = draw_segments(jax.random.fold_in(seeds[17], 71), 0)
    sink_logits = jnp.clip(4.0 * jax.random.uniform(seeds[3], (Q_HEADS,), jnp.float32) ** levels(seeds[3], (Q_HEADS,), ((0, 2),), -0.2, 0.2), 0.0, 4.0)
    out_weight = normal_values(seeds[4], (Q_HEADS * HEAD, D), (Q_HEADS * HEAD) ** -0.5, 0.09375, ((0, 2),))
    out_bias = normal_values(seeds[5], (D,), 0.5, 3.0)
    residual = normal_values(seeds[6], (TOKENS, D), 1.0, 6.0, ((0, 32),))
    norm_gain = jnp.clip(1.0 + 0.1 * jax.random.normal(seeds[7], (D,), jnp.float32), 0.5, 1.5).astype(jnp.bfloat16)
    route_ids_keys = jax.random.split(jax.random.fold_in(seeds[8], 1), TOKENS // TOK_DEV)
    route_ids_turns = jax.random.permutation(jax.random.fold_in(seeds[8], 3), TOKENS // TOK_DEV)
    route_ids = jax.vmap(lambda own, number: deal_out(jax.random.fold_in(seeds[8], 2), own, number, TOK_DEV, EXPERTS, TOP, CAP, 2))(route_ids_keys, route_ids_turns).reshape((TOKENS, TOP))
    route_logits = normal_values(seeds[9], (TOKENS, TOP), 1.5, 6.0, ((0, 32),), jnp.float32)
    gate_weight = normal_values(seeds[10], (EXPERTS, D, FF), (D // 8) ** -0.5, 0.3125, ((0, 16), (2, 2)))
    gate_bias = normal_values(seeds[11], (EXPERTS, FF), 0.5, 3.0, ((0, 16), (1, 2)))
    up_weight = normal_values(seeds[12], (EXPERTS, D, FF), (D // 8) ** -0.5, 0.3125, ((0, 16), (2, 2)))
    up_bias = normal_values(seeds[13], (EXPERTS, FF), 0.5, 3.0, ((0, 16), (1, 2)))
    down_weight = normal_values(seeds[14], (EXPERTS, FF, D), (4 * FF) ** -0.5, 0.0546875, ((0, 16), (1, 2)))
    down_bias = normal_values(seeds[15], (EXPERTS, D), 0.5, 3.0)
    page_table = jax.vmap(lambda own: jax.random.permutation(own, PAGES))(jax.random.split(seeds[16], N_REQ)).reshape((N_REQ, PAGES)).astype(jnp.int32)
    return {"queries": queries, "keys_values": keys_values, "segments": segments, "sink_logits": sink_logits, "out_weight": out_weight, "out_bias": out_bias, "residual": residual, "norm_gain": norm_gain, "route_ids": route_ids, "route_logits": route_logits, "gate_weight": gate_weight, "gate_bias": gate_bias, "up_weight": up_weight, "up_bias": up_bias, "down_weight": down_weight, "down_bias": down_bias, "page_table": page_table}


rope_base = 150000.0
norm_eps = 1e-05
swiglu_limit = 7.0
glu_alpha = 1.702

def seg_positions(segment_ids):
    length = segment_ids.shape[0]
    indices = jnp.arange(length, dtype=jnp.int32)
    change = jnp.concatenate([jnp.ones((1,), dtype=bool), segment_ids[1:] != segment_ids[:-1]])
    starts = lax.cummax(jnp.where(change, indices, 0).astype(jnp.int32), axis=0)
    return indices - starts

def rotate(values, positions):
    half_dim = values.shape[-1] // 2
    inverse = rope_base ** (-jnp.arange(half_dim, dtype=jnp.float32) / half_dim)
    angles = positions.astype(jnp.float32)[:, None] * inverse[None, :]
    cosine = jnp.cos(angles)[:, None, :]
    sine_col = jnp.sin(angles)[:, None, :]
    first_half = values[..., :half_dim]
    second_half = values[..., half_dim:]
    return jnp.concatenate([first_half * cosine - second_half * sine_col, second_half * cosine + first_half * sine_col], axis=-1)

def attend_group(queries, keys_values, segment_ids, sink_logits):
    length = queries.shape[0]
    kv_heads = keys_values.shape[1] // (2 * HEAD)
    q_heads = queries.shape[1] // HEAD
    group_size = q_heads // kv_heads
    positions = seg_positions(segment_ids)
    q_rot = rotate(queries.astype(jnp.float32).reshape(length, q_heads, HEAD), positions).astype(jnp.bfloat16)
    q_rot = q_rot.reshape(length, kv_heads, group_size, HEAD)
    key_part = keys_values.reshape(length, kv_heads, 2, HEAD)
    k_rot = rotate(key_part[:, :, 0].astype(jnp.float32), positions).astype(jnp.bfloat16)
    values = key_part[:, :, 1]
    scores = jnp.einsum('qkgd,skd->kgqs', q_rot.astype(jnp.float32), k_rot.astype(jnp.float32)) * HEAD ** (-0.5)
    indices = jnp.arange(length, dtype=jnp.int32)
    visible = (segment_ids[:, None] == segment_ids[None, :]) & (indices[None, :] <= indices[:, None])
    scores = jnp.where(visible, scores, -jnp.inf)
    sink_col = sink_logits.reshape(kv_heads, group_size)[:, :, None]
    highest = jnp.maximum(lax.optimization_barrier(jnp.max(scores, axis=-1)), sink_col)
    expo_terms = jnp.exp(scores - highest[..., None])
    denominator = lax.optimization_barrier(jnp.sum(expo_terms, axis=-1)) + jnp.exp(sink_col - highest)
    probabilities = (expo_terms / denominator[..., None]).astype(jnp.bfloat16)
    attended = jnp.einsum('kgqs,skd->qkgd', probabilities.astype(jnp.float32), values.astype(jnp.float32))
    attended = attended.astype(jnp.bfloat16).reshape(length, q_heads * HEAD)
    cached = jnp.stack([k_rot, values], axis=2).reshape(length, kv_heads * 2 * HEAD)
    return (attended, cached)

def reference(queries, keys_values, segments, sink_logits, out_weight, out_bias, residual, norm_gain, route_ids, route_logits, gate_weight, gate_bias, up_weight, up_bias, down_weight, down_bias, page_table):

    def one_group(pieces):
        return attend_group(pieces[0], pieces[1], pieces[2], sink_logits)
    attended, cached = lax.map(one_group, (queries.reshape(N_REQ, TOK_REQ, -1), keys_values.reshape(N_REQ, TOK_REQ, -1), segments.reshape(N_REQ, TOK_REQ)))
    attended = attended.reshape(TOKENS, -1)
    projected = jnp.dot(attended, out_weight, preferred_element_type=jnp.float32)
    hidden = (residual.astype(jnp.float32) + projected + out_bias.astype(jnp.float32)).astype(jnp.bfloat16)
    stream = hidden.astype(jnp.float32)
    normed = (stream * lax.rsqrt(lax.optimization_barrier(jnp.mean(stream * stream, axis=-1, keepdims=True)) + norm_eps) * norm_gain.astype(jnp.float32)).astype(jnp.bfloat16)
    route_weights = jax.nn.softmax(route_logits.astype(jnp.float32), axis=-1)
    capacity = N_REQ * N_TP * CAP

    def expert_step(carry, pieces):
        w_gate, b_gate, w_up, b_up, w_down, b_down, expert = pieces
        hit = route_ids == expert
        chosen = jnp.any(hit, axis=1)
        share = lax.optimization_barrier(jnp.sum(jnp.where(hit, route_weights, 0.0), axis=1))
        order = jnp.cumsum(chosen.astype(jnp.int32)) - 1
        chosen_count = jnp.sum(chosen.astype(jnp.int32))
        target = jnp.where(chosen, order, capacity).astype(jnp.int32)
        member = jnp.zeros((capacity,), jnp.int32).at[target].set(jnp.arange(TOKENS, dtype=jnp.int32), mode='drop')
        valid = jnp.arange(capacity, dtype=jnp.int32) < chosen_count
        picked = normed[member]
        gate_act = jnp.dot(picked, w_gate, preferred_element_type=jnp.float32) + b_gate.astype(jnp.float32)
        up_act = jnp.dot(picked, w_up, preferred_element_type=jnp.float32) + b_up.astype(jnp.float32)
        gate_act = jnp.minimum(gate_act, swiglu_limit)
        up_act = jnp.clip(up_act, -swiglu_limit, swiglu_limit)
        active = (gate_act * jax.nn.sigmoid(glu_alpha * gate_act) * (up_act + 1.0)).astype(jnp.bfloat16)
        partial_value = jnp.einsum('rtf,tfd->trd', active.reshape(capacity, N_TP, -1).astype(jnp.float32), w_down.reshape(N_TP, -1, D).astype(jnp.float32))
        rounded = lax.optimization_barrier(partial_value.astype(jnp.bfloat16))
        expert_out = lax.optimization_barrier(jnp.sum(rounded.astype(jnp.float32), axis=0)) + b_down.astype(jnp.float32)
        scale = jnp.where(valid, share[member], 0.0)
        return (carry.at[member].add(scale[:, None] * expert_out), None)
    expert_mix, _ = lax.scan(expert_step, jnp.zeros((TOKENS, D), jnp.float32), (gate_weight, gate_bias, up_weight, up_bias, down_weight, down_bias, jnp.arange(EXPERTS, dtype=jnp.int32)))
    mixed_out = (stream + expert_mix).astype(jnp.bfloat16)
    blocks = cached.reshape(N_REQ, PAGES, PAGE_LEN, -1)

    def place_pages(table, block_set):
        return jnp.zeros_like(block_set).at[table].set(block_set)
    page_pool = jax.vmap(place_pages)(page_table, blocks).reshape(N_REQ * PAGES, PAGE_LEN, -1)
    return (mixed_out, page_pool)
```

```python
import functools

import jax
import jax.numpy as jnp
from jax import lax
from jax.experimental import pallas as pl
from jax.experimental.pallas import tpu as pltpu
from jax.sharding import PartitionSpec as P

HEAD = 64
PAGE_LEN = 16
LANES = 128


rope_base = 150000.0
norm_eps = 1e-05
swiglu_limit = 7.0
glu_alpha = 1.702


def seg_positions(segment_ids):
    length = segment_ids.shape[0]
    indices = jnp.arange(length, dtype=jnp.int32)
    change = jnp.concatenate([jnp.ones((1,), dtype=bool), segment_ids[1:] != segment_ids[:-1]])
    starts = lax.cummax(jnp.where(change, indices, 0), axis=0)
    return indices - starts


def rotate(values, positions):
    half_dim = values.shape[-1] // 2
    inverse = rope_base ** (-jnp.arange(half_dim, dtype=jnp.float32) / half_dim)
    angles = positions.astype(jnp.float32)[:, None] * inverse[None, :]
    cosine = jnp.cos(angles)[:, None, :]
    sine_col = jnp.sin(angles)[:, None, :]
    first_half = values[..., :half_dim]
    second_half = values[..., half_dim:]
    return jnp.concatenate(
        [
            first_half * cosine - second_half * sine_col,
            second_half * cosine + first_half * sine_col,
        ],
        axis=-1,
    )


def attend_group(queries, keys_values, segment_ids, sink_logits):
    length = queries.shape[0]
    kv_heads = keys_values.shape[1] // (2 * HEAD)
    q_heads = queries.shape[1] // HEAD
    group_size = q_heads // kv_heads
    positions = seg_positions(segment_ids)
    q_rot = rotate(queries.astype(jnp.float32).reshape(length, q_heads, HEAD), positions).astype(
        jnp.bfloat16
    )
    q_rot = q_rot.reshape(length, kv_heads, group_size, HEAD)
    key_part = keys_values.reshape(length, kv_heads, 2, HEAD)
    k_rot = rotate(key_part[:, :, 0].astype(jnp.float32), positions).astype(jnp.bfloat16)
    values = key_part[:, :, 1]
    scores = jnp.einsum(
        "qkgd,skd->kgqs", q_rot, k_rot, preferred_element_type=jnp.float32
    ) * HEAD ** (-0.5)
    indices = jnp.arange(length, dtype=jnp.int32)
    visible = (segment_ids[:, None] == segment_ids[None, :]) & (
        indices[None, :] <= indices[:, None]
    )
    scores = jnp.where(visible, scores, -jnp.inf)
    sink_col = sink_logits.reshape(kv_heads, group_size)[:, :, None]
    highest = jnp.maximum(jnp.max(scores, axis=-1), sink_col)
    expo_terms = jnp.exp(scores - highest[..., None])
    denominator = jnp.sum(expo_terms, axis=-1) + jnp.exp(sink_col - highest)
    probabilities = (expo_terms / denominator[..., None]).astype(jnp.bfloat16)
    attended = jnp.einsum(
        "kgqs,skd->qkgd", probabilities, values, preferred_element_type=jnp.float32
    )
    attended = attended.astype(jnp.bfloat16).reshape(length, q_heads * HEAD)
    cached = jnp.stack([k_rot, values], axis=2).reshape(length, kv_heads * 2 * HEAD)
    return (attended, cached)


def slot_index(routes, experts, capacity):
    blocks, row_count, route_width = routes.shape
    flat_ids = routes.reshape(blocks, row_count * route_width)
    onehot = (flat_ids[:, :, None] == jnp.arange(experts, dtype=jnp.int32)[None, None, :]).astype(
        jnp.int32
    )
    earlier = jnp.cumsum(onehot, axis=1) - onehot
    position = jnp.sum(earlier * onehot, axis=2)
    block_ids = jnp.arange(blocks, dtype=jnp.int32)[:, None]
    slot_ids = flat_ids * (blocks * capacity) + block_ids * capacity + position
    return slot_ids.reshape(blocks * row_count, route_width).astype(jnp.int32)


def dispatch(tokens, slot_ids, slot_total):
    row_count = tokens.shape[0]
    owners = jnp.broadcast_to(jnp.arange(row_count, dtype=jnp.int32)[:, None], slot_ids.shape)
    member = (
        jnp.full((slot_total,), row_count, jnp.int32)
        .at[slot_ids.reshape(-1)]
        .set(owners.reshape(-1))
    )
    padded = jnp.concatenate([tokens, jnp.zeros((1, tokens.shape[1]), tokens.dtype)], axis=0)
    return padded[member]


def slot_limit(tok_count, route_width, experts):
    return max(2, 2 * tok_count * route_width // experts)


def body(
    queries,
    keys_values,
    segments,
    sink_logits,
    out_weight,
    out_bias,
    residual,
    norm_gain,
    route_ids,
    route_logits,
    gate_weight,
    gate_bias,
    up_weight,
    up_bias,
    down_weight,
    down_bias,
    page_table,
):
    attended, cached = attend_group(queries, keys_values, segments, sink_logits)
    projected = lax.psum_scatter(
        jnp.dot(attended, out_weight, preferred_element_type=jnp.float32).astype(jnp.bfloat16),
        "tp",
        scatter_dimension=0,
        tiled=True,
    ).astype(jnp.float32)
    hidden = (residual.astype(jnp.float32) + projected + out_bias.astype(jnp.float32)).astype(
        jnp.bfloat16
    )
    stream = hidden.astype(jnp.float32)
    normed = (
        stream
        * lax.rsqrt(jnp.mean(stream * stream, axis=-1, keepdims=True) + norm_eps)
        * norm_gain.astype(jnp.float32)
    ).astype(jnp.bfloat16)
    route_weights = jax.nn.softmax(route_logits, axis=-1)
    tok_count, route_width = route_ids.shape
    experts = down_bias.shape[0]
    model_width = residual.shape[1]
    capacity = slot_limit(tok_count, route_width, experts)
    own_slots = slot_index(route_ids[None], experts, capacity)
    group_rows, group_routes = (
        lax.all_gather(normed, "tp", axis=0, tiled=True),
        lax.all_gather(route_ids, "tp", axis=0, tiled=True),
    )
    tp_count = group_rows.shape[0] // tok_count
    all_slots = slot_index(
        group_routes.reshape(tp_count, tok_count, route_width), experts, capacity
    )
    dispatched = dispatch(group_rows, all_slots, experts * tp_count * capacity).reshape(
        experts, tp_count, capacity, model_width
    )
    received = lax.all_to_all(dispatched, "req", split_axis=0, concat_axis=0, tiled=True)
    slot_shape = received.shape
    flat_rows = received.reshape(-1, model_width)
    gate_act = jnp.dot(flat_rows, gate_weight[0], preferred_element_type=jnp.float32) + gate_bias[
        0
    ].astype(jnp.float32)
    up_act = jnp.dot(flat_rows, up_weight[0], preferred_element_type=jnp.float32) + up_bias[
        0
    ].astype(jnp.float32)
    gate_act = jnp.minimum(gate_act, swiglu_limit)
    up_act = jnp.clip(up_act, -swiglu_limit, swiglu_limit)
    active = (gate_act * jax.nn.sigmoid(glu_alpha * gate_act) * (up_act + 1.0)).astype(jnp.bfloat16)
    partial_value = jnp.dot(active, down_weight[0], preferred_element_type=jnp.float32).reshape(
        slot_shape
    )
    summed = lax.psum_scatter(
        partial_value.astype(jnp.bfloat16), "tp", scatter_dimension=1, tiled=True
    ).astype(jnp.float32)
    returned = lax.all_to_all(
        summed.astype(jnp.bfloat16), "req", split_axis=0, concat_axis=0, tiled=True
    ).astype(summed.dtype)
    returned = returned.reshape(experts * capacity, model_width)
    slot_onehot = (
        own_slots[:, :, None] == jnp.arange(experts * capacity, dtype=jnp.int32)[None, None, :]
    ).astype(jnp.float32)
    combiner = jnp.einsum("rk,rks->rs", route_weights, slot_onehot, precision=lax.Precision.HIGHEST)
    expert_onehot = (
        route_ids[:, :, None] == jnp.arange(experts, dtype=jnp.int32)[None, None, :]
    ).astype(jnp.float32)
    dense_weights = jnp.einsum(
        "rk,rke->re", route_weights, expert_onehot, precision=lax.Precision.HIGHEST
    )
    expert_mix = jnp.dot(
        combiner, returned, precision=lax.Precision.HIGHEST, preferred_element_type=jnp.float32
    )
    expert_mix = expert_mix + jnp.dot(
        dense_weights,
        down_bias.astype(jnp.float32),
        precision=lax.Precision.HIGHEST,
        preferred_element_type=jnp.float32,
    )
    mixed_out = (stream + expert_mix).astype(jnp.bfloat16)
    blocks = cached.reshape(-1, PAGE_LEN, cached.shape[1])
    page_pool = jnp.zeros_like(blocks).at[page_table[0]].set(blocks)
    return (mixed_out, page_pool)


def mid_kernel(
    own_ref,
    got_ref,
    residual_ref,
    out_bias_ref,
    gain_ref,
    ids_ref,
    logits_ref,
    down_bias_ref,
    base_ref,
    rows_ref,
):
    width = residual_ref.shape[1]
    experts = down_bias_ref.shape[0]
    hidden = (
        residual_ref[...].astype(jnp.float32)
        + own_ref[...].astype(jnp.float32)
        + got_ref[...].astype(jnp.float32)
        + out_bias_ref[...].astype(jnp.float32)
    ).astype(jnp.bfloat16)
    stream = hidden.astype(jnp.float32)
    normed = (
        stream
        * lax.rsqrt(jnp.mean(stream * stream, axis=-1, keepdims=True) + norm_eps)
        * gain_ref[...].astype(jnp.float32)
    ).astype(jnp.bfloat16)
    logits = logits_ref[...]
    expo = jnp.exp(logits - jnp.max(logits, axis=-1, keepdims=True))
    weights = expo / jnp.sum(expo, axis=-1, keepdims=True)
    high = weights.astype(jnp.bfloat16).astype(jnp.float32)
    low = (weights - high).astype(jnp.bfloat16).astype(jnp.float32)
    ids = ids_ref[...]
    lanes = lax.broadcasted_iota(jnp.int32, (ids.shape[0], LANES), 1)
    high_cols = jnp.zeros(lanes.shape, jnp.float32)
    low_cols = jnp.zeros(lanes.shape, jnp.float32)
    first = width % LANES
    for k in range(ids.shape[1]):
        at = ids[:, k : k + 1] + first
        high_cols = high_cols + jnp.where(lanes == at, high[:, k : k + 1], 0.0)
        low_cols = low_cols + jnp.where(lanes == at + experts, low[:, k : k + 1], 0.0)
    high_dense = high_cols[:, first : first + experts].astype(jnp.bfloat16)
    low_dense = low_cols[:, first + experts : first + 2 * experts].astype(jnp.bfloat16)
    bias = down_bias_ref[...]
    base_ref[...] = (
        stream
        + jnp.dot(high_dense, bias, preferred_element_type=jnp.float32)
        + jnp.dot(low_dense, bias, preferred_element_type=jnp.float32)
    )
    rows_ref[:, :width] = normed
    rows_ref[:, width:] = (high_cols + low_cols)[:, first:].astype(jnp.bfloat16)


def tiles(total, step):
    return [(start, min(step, total - start)) for start in range(0, total, step)]


def expert_kernel(parts, expert_ref, *refs):
    pieces, refs = refs[:parts], refs[parts:]
    gate_hbm, up_hbm, down_hbm, gate_bias_ref, up_bias_ref = refs[:5]
    outs, refs = refs[5 : 5 + parts], refs[5 + parts :]
    rows, picked, gate_w, up_w, down_w, active, spread, sems = refs
    piece = pieces[0].shape[0]
    total = rows.shape[0]
    slots = picked.shape[0]
    width = down_w.shape[1]
    copies = [
        pltpu.make_async_copy(p, rows.at[pl.ds(i * piece, piece)], sems.at[i])
        for i, p in enumerate(pieces)
    ]
    weights = [
        pltpu.make_async_copy(src, dst, sems.at[parts + i])
        for i, (src, dst) in enumerate(
            ((gate_hbm, gate_w), (up_hbm, up_w), (down_hbm, down_w))
        )
    ]
    for copy in copies + weights:
        copy.start()
    for copy in copies:
        copy.wait()

    expert = expert_ref[0]
    experts = (rows.shape[1] - width) // 4
    lane = lax.broadcasted_iota(jnp.int32, (16, LANES), 1)
    which = lax.broadcasted_iota(jnp.int32, (16, LANES), 0)
    choose = jnp.where(
        (lane == width % LANES + expert + which * experts) & (which < 2), 1.0, 0.0
    ).astype(jnp.bfloat16)
    found = lax.dot_general(
        choose,
        rows[:, rows.shape[1] - LANES :],
        (((1,), (1,)), ((), ())),
        preferred_element_type=jnp.float32,
    )
    share = found[0:1] + found[1:2]
    chosen = share > 0.0
    earlier = jnp.where(
        lax.broadcasted_iota(jnp.int32, (total, total), 0)
        <= lax.broadcasted_iota(jnp.int32, (total, total), 1),
        1.0,
        0.0,
    ).astype(jnp.bfloat16)
    marks = jnp.broadcast_to(jnp.where(chosen, 1.0, 0.0), (16, total)).astype(jnp.bfloat16)
    count = jnp.dot(marks, earlier, preferred_element_type=jnp.float32)[0:1]
    slot = jnp.where(chosen, count - 1.0, -1.0).astype(jnp.int32)
    hit = lax.broadcasted_iota(jnp.int32, (slots, total), 0) == slot
    pick_f32 = jnp.where(hit, 1.0, 0.0)
    pick = pick_f32.astype(jnp.bfloat16)
    slot_share = jnp.sum(jnp.where(hit, share, 0.0), axis=1, keepdims=True)
    spread[...] = pick_f32.T.astype(jnp.bfloat16)
    for start, size in tiles(width, 512):
        picked[:, start : start + size] = jnp.dot(
            pick, rows[:, start : start + size], preferred_element_type=jnp.float32
        ).astype(jnp.bfloat16)

    weights[0].wait()
    weights[1].wait()
    for start, size in tiles(gate_w.shape[1], 256):
        cols = slice(start, start + size)
        gate = jnp.dot(
            picked[...], gate_w[:, cols], preferred_element_type=jnp.float32
        ) + gate_bias_ref[:, cols].astype(jnp.float32)
        up = jnp.dot(
            picked[...], up_w[:, cols], preferred_element_type=jnp.float32
        ) + up_bias_ref[:, cols].astype(jnp.float32)
        gate = jnp.minimum(gate, swiglu_limit)
        up = jnp.clip(up, -swiglu_limit, swiglu_limit)
        active[:, cols] = (
            gate * (1.0 / (1.0 + jnp.exp(-glu_alpha * gate))) * (up + 1.0)
        ).astype(jnp.bfloat16)
    weights[2].wait()
    for start, size in tiles(width, 256):
        cols = slice(start, start + size)
        value = jnp.dot(active[...], down_w[:, cols], preferred_element_type=jnp.float32)
        scaled = (value * slot_share).astype(jnp.bfloat16)
        spread_rows = jnp.dot(spread[...], scaled, preferred_element_type=jnp.float32).astype(
            jnp.bfloat16
        )
        for i, out in enumerate(outs):
            out[:, cols] = spread_rows[i * piece : (i + 1) * piece]


def vmem():
    return pl.BlockSpec(memory_space=pltpu.VMEM)


def anywhere():
    return pl.BlockSpec(memory_space=pl.ANY)


def run_expert(expert, pieces, gate_weight, gate_bias, up_weight, up_bias, down_weight, slots):
    parts = len(pieces)
    piece, padded = pieces[0].shape
    hidden_units, width = down_weight.shape
    total = parts * piece
    return pl.pallas_call(
        functools.partial(expert_kernel, parts),
        out_shape=[jax.ShapeDtypeStruct((piece, width), jnp.bfloat16)] * parts,
        in_specs=[pl.BlockSpec(memory_space=pltpu.SMEM)]
        + [anywhere()] * (parts + 3)
        + [vmem()] * 2,
        out_specs=[vmem()] * parts,
        scratch_shapes=[
            pltpu.VMEM((total, padded), jnp.bfloat16),
            pltpu.VMEM((slots, width), jnp.bfloat16),
            pltpu.VMEM(gate_weight.shape, jnp.bfloat16),
            pltpu.VMEM(up_weight.shape, jnp.bfloat16),
            pltpu.VMEM(down_weight.shape, jnp.bfloat16),
            pltpu.VMEM((slots, hidden_units), jnp.bfloat16),
            pltpu.VMEM((total, slots), jnp.bfloat16),
            pltpu.SemaphoreType.DMA((parts + 3,)),
        ],
        compiler_params=pltpu.CompilerParams(vmem_limit_bytes=52 * 2**20),
        cost_estimate=pl.CostEstimate(
            flops=2 * slots * width * (3 * hidden_units + 2 * total),
            bytes_accessed=6 * width * hidden_units,
            transcendentals=slots * hidden_units,
        ),
        name="expert",
    )(expert, *pieces, gate_weight, up_weight, down_weight, gate_bias, up_bias)


AXES = ("req", "tp")


def moved(array, n_req, step):
    outer, mid, core, tp = step
    pairs = []
    for source in range(2 * n_req):
        req, side = divmod(source, 2)
        place = (req // 4 ^ outer) * 4 + (req // 2 % 2 ^ mid) * 2 + (req % 2 ^ core)
        pairs.append((source, place * 2 + (side ^ tp)))
    return lax.ppermute(array, AXES, pairs)


def crossed(array, n_req, by_core):
    pairs = []
    for source in range(2 * n_req):
        req, side = divmod(source, 2)
        if req % 2 == by_core:
            pairs.append((source, (req ^ 2) * 2 + side))
        else:
            pairs.append((source, req * 2 + (side ^ 1)))
    return lax.ppermute(array, AXES, pairs)


def gather_rows(rows, n_req):
    outer = n_req // 4
    line = jnp.concatenate([rows] + [moved(rows, n_req, (k, 0, 0, 0)) for k in range(1, outer)])
    first = crossed(line, n_req, 0)
    second = crossed(line, n_req, 1)
    both = crossed(first, n_req, 1)
    own = [line, first, second, both]
    return own + [moved(piece, n_req, (0, 0, 1, 0)) for piece in own]


def add_rows(left, right):
    return (left.astype(jnp.float32) + right.astype(jnp.float32)).astype(jnp.bfloat16)


def scatter_rows(sums, n_req):
    own, other = sums[:4], sums[4:]
    line, first, second, both = [
        add_rows(mine, moved(theirs, n_req, (0, 0, 1, 0))) for mine, theirs in zip(own, other)
    ]
    first = add_rows(first, crossed(both, n_req, 1))
    line = add_rows(line, crossed(second, n_req, 1))
    line = add_rows(line, crossed(first, n_req, 0))
    outer = n_req // 4
    count = line.shape[0] // outer
    blocks = [line[k * count : (k + 1) * count] for k in range(outer)]
    return [blocks[0]] + [
        moved(block, n_req, (k, 0, 0, 0)) for k, block in enumerate(blocks) if k > 0
    ]


def gathered_body(
    n_req,
    queries,
    keys_values,
    segments,
    sink_logits,
    out_weight,
    out_bias,
    residual,
    norm_gain,
    route_ids,
    route_logits,
    gate_weight,
    gate_bias,
    up_weight,
    up_bias,
    down_weight,
    down_bias,
    page_table,
):
    attended, cached = attend_group(queries, keys_values, segments, sink_logits)
    tok_count, width = residual.shape
    partial = jnp.dot(attended, out_weight, preferred_element_type=jnp.float32).astype(jnp.bfloat16)
    side = lax.axis_index("tp")
    own = lax.dynamic_slice_in_dim(partial, side * tok_count, tok_count)
    other = lax.dynamic_slice_in_dim(partial, (1 - side) * tok_count, tok_count)
    got = moved(other, n_req, (0, 0, 0, 1))
    experts = down_bias.shape[0]
    base, rows = pl.pallas_call(
        mid_kernel,
        out_shape=[
            jax.ShapeDtypeStruct((tok_count, width), jnp.float32),
            jax.ShapeDtypeStruct((tok_count, width + 4 * experts), jnp.bfloat16),
        ],
        in_specs=[vmem()] * 8,
        out_specs=[vmem()] * 2,
        name="norm_rows",
    )(
        own,
        got,
        residual,
        out_bias[None],
        norm_gain[None],
        route_ids,
        route_logits,
        down_bias,
    )
    pieces = gather_rows(rows, n_req)
    slots = 2 * n_req * slot_limit(tok_count, route_ids.shape[1], experts)
    sums = run_expert(
        lax.axis_index("req")[None],
        pieces,
        gate_weight[0],
        gate_bias,
        up_weight[0],
        up_bias,
        down_weight[0],
        slots,
    )
    mixed = base
    for part in scatter_rows(sums, n_req):
        mixed = mixed + part.astype(jnp.float32)
    blocks = cached.reshape(-1, PAGE_LEN, cached.shape[1])
    page_pool = jnp.zeros_like(blocks).at[page_table[0]].set(blocks)
    return (mixed.astype(jnp.bfloat16), page_pool)


def solution(mesh):
    in_specs = (
        P("req", "tp"),
        P("req", "tp"),
        P("req"),
        P("tp"),
        P("tp", None),
        P(),
        P(("req", "tp"), None),
        P(),
        P(("req", "tp"), None),
        P(("req", "tp"), None),
        P("req", None, "tp"),
        P("req", "tp"),
        P("req", None, "tp"),
        P("req", "tp"),
        P("req", "tp", None),
        P(),
        P("req", None),
    )
    out_specs = (P(("req", "tp"), None), P("req", None, "tp"))
    n_req, n_tp = mesh.shape["req"], mesh.shape["tp"]
    chosen = functools.partial(gathered_body, n_req) if (n_req, n_tp) == (16, 2) else body
    return jax.shard_map(chosen, mesh=mesh, in_specs=in_specs, out_specs=out_specs, check_vma=False)
```

```python
import functools

import jax
import jax.numpy as jnp
import numpy as np
from jax import lax
from jax.experimental import pallas as pl
from jax.experimental.pallas import tpu as pltpu
from jax.sharding import PartitionSpec as P

HEAD = 64
PAGE_LEN = 16
LANES = 128


rope_base = 150000.0
norm_eps = 1e-05
swiglu_limit = 7.0
glu_alpha = 1.702


def seg_positions(segment_ids):
    length = segment_ids.shape[0]
    indices = jnp.arange(length, dtype=jnp.int32)
    change = jnp.concatenate([jnp.ones((1,), dtype=bool), segment_ids[1:] != segment_ids[:-1]])
    starts = lax.cummax(jnp.where(change, indices, 0), axis=0)
    return indices - starts


def rotate(values, positions):
    half_dim = values.shape[-1] // 2
    inverse = rope_base ** (-jnp.arange(half_dim, dtype=jnp.float32) / half_dim)
    angles = positions.astype(jnp.float32)[:, None] * inverse[None, :]
    cosine = jnp.cos(angles)[:, None, :]
    sine_col = jnp.sin(angles)[:, None, :]
    first_half = values[..., :half_dim]
    second_half = values[..., half_dim:]
    return jnp.concatenate(
        [
            first_half * cosine - second_half * sine_col,
            second_half * cosine + first_half * sine_col,
        ],
        axis=-1,
    )


def attend_group(queries, keys_values, segment_ids, sink_logits):
    length = queries.shape[0]
    kv_heads = keys_values.shape[1] // (2 * HEAD)
    q_heads = queries.shape[1] // HEAD
    group_size = q_heads // kv_heads
    positions = seg_positions(segment_ids)
    q_rot = rotate(queries.astype(jnp.float32).reshape(length, q_heads, HEAD), positions).astype(
        jnp.bfloat16
    )
    q_rot = q_rot.reshape(length, kv_heads, group_size, HEAD)
    key_part = keys_values.reshape(length, kv_heads, 2, HEAD)
    k_rot = rotate(key_part[:, :, 0].astype(jnp.float32), positions).astype(jnp.bfloat16)
    values = key_part[:, :, 1]
    scores = jnp.einsum(
        "qkgd,skd->kgqs", q_rot, k_rot, preferred_element_type=jnp.float32
    ) * HEAD ** (-0.5)
    indices = jnp.arange(length, dtype=jnp.int32)
    visible = (segment_ids[:, None] == segment_ids[None, :]) & (
        indices[None, :] <= indices[:, None]
    )
    scores = jnp.where(visible, scores, -jnp.inf)
    sink_col = sink_logits.reshape(kv_heads, group_size)[:, :, None]
    highest = jnp.maximum(jnp.max(scores, axis=-1), sink_col)
    expo_terms = jnp.exp(scores - highest[..., None])
    denominator = jnp.sum(expo_terms, axis=-1) + jnp.exp(sink_col - highest)
    probabilities = (expo_terms / denominator[..., None]).astype(jnp.bfloat16)
    attended = jnp.einsum(
        "kgqs,skd->qkgd", probabilities, values, preferred_element_type=jnp.float32
    )
    attended = attended.astype(jnp.bfloat16).reshape(length, q_heads * HEAD)
    cached = jnp.stack([k_rot, values], axis=2).reshape(length, kv_heads * 2 * HEAD)
    return (attended, cached)


def slot_index(routes, experts, capacity):
    blocks, row_count, route_width = routes.shape
    flat_ids = routes.reshape(blocks, row_count * route_width)
    onehot = (flat_ids[:, :, None] == jnp.arange(experts, dtype=jnp.int32)[None, None, :]).astype(
        jnp.int32
    )
    earlier = jnp.cumsum(onehot, axis=1) - onehot
    position = jnp.sum(earlier * onehot, axis=2)
    block_ids = jnp.arange(blocks, dtype=jnp.int32)[:, None]
    slot_ids = flat_ids * (blocks * capacity) + block_ids * capacity + position
    return slot_ids.reshape(blocks * row_count, route_width).astype(jnp.int32)


def dispatch(tokens, slot_ids, slot_total):
    row_count = tokens.shape[0]
    owners = jnp.broadcast_to(jnp.arange(row_count, dtype=jnp.int32)[:, None], slot_ids.shape)
    member = (
        jnp.full((slot_total,), row_count, jnp.int32)
        .at[slot_ids.reshape(-1)]
        .set(owners.reshape(-1))
    )
    padded = jnp.concatenate([tokens, jnp.zeros((1, tokens.shape[1]), tokens.dtype)], axis=0)
    return padded[member]


def slot_limit(tok_count, route_width, experts):
    return max(2, 2 * tok_count * route_width // experts)


def body(
    queries,
    keys_values,
    segments,
    sink_logits,
    out_weight,
    out_bias,
    residual,
    norm_gain,
    route_ids,
    route_logits,
    gate_weight,
    gate_bias,
    up_weight,
    up_bias,
    down_weight,
    down_bias,
    page_table,
):
    attended, cached = attend_group(queries, keys_values, segments, sink_logits)
    projected = lax.psum_scatter(
        jnp.dot(attended, out_weight, preferred_element_type=jnp.float32).astype(jnp.bfloat16),
        "tp",
        scatter_dimension=0,
        tiled=True,
    ).astype(jnp.float32)
    hidden = (residual.astype(jnp.float32) + projected + out_bias.astype(jnp.float32)).astype(
        jnp.bfloat16
    )
    stream = hidden.astype(jnp.float32)
    normed = (
        stream
        * lax.rsqrt(jnp.mean(stream * stream, axis=-1, keepdims=True) + norm_eps)
        * norm_gain.astype(jnp.float32)
    ).astype(jnp.bfloat16)
    route_weights = jax.nn.softmax(route_logits, axis=-1)
    tok_count, route_width = route_ids.shape
    experts = down_bias.shape[0]
    model_width = residual.shape[1]
    capacity = slot_limit(tok_count, route_width, experts)
    own_slots = slot_index(route_ids[None], experts, capacity)
    group_rows, group_routes = (
        lax.all_gather(normed, "tp", axis=0, tiled=True),
        lax.all_gather(route_ids, "tp", axis=0, tiled=True),
    )
    tp_count = group_rows.shape[0] // tok_count
    all_slots = slot_index(
        group_routes.reshape(tp_count, tok_count, route_width), experts, capacity
    )
    dispatched = dispatch(group_rows, all_slots, experts * tp_count * capacity).reshape(
        experts, tp_count, capacity, model_width
    )
    received = lax.all_to_all(dispatched, "req", split_axis=0, concat_axis=0, tiled=True)
    slot_shape = received.shape
    flat_rows = received.reshape(-1, model_width)
    gate_act = jnp.dot(flat_rows, gate_weight[0], preferred_element_type=jnp.float32) + gate_bias[
        0
    ].astype(jnp.float32)
    up_act = jnp.dot(flat_rows, up_weight[0], preferred_element_type=jnp.float32) + up_bias[
        0
    ].astype(jnp.float32)
    gate_act = jnp.minimum(gate_act, swiglu_limit)
    up_act = jnp.clip(up_act, -swiglu_limit, swiglu_limit)
    active = (gate_act * jax.nn.sigmoid(glu_alpha * gate_act) * (up_act + 1.0)).astype(jnp.bfloat16)
    partial_value = jnp.dot(active, down_weight[0], preferred_element_type=jnp.float32).reshape(
        slot_shape
    )
    summed = lax.psum_scatter(
        partial_value.astype(jnp.bfloat16), "tp", scatter_dimension=1, tiled=True
    ).astype(jnp.float32)
    returned = lax.all_to_all(
        summed.astype(jnp.bfloat16), "req", split_axis=0, concat_axis=0, tiled=True
    ).astype(summed.dtype)
    returned = returned.reshape(experts * capacity, model_width)
    slot_onehot = (
        own_slots[:, :, None] == jnp.arange(experts * capacity, dtype=jnp.int32)[None, None, :]
    ).astype(jnp.float32)
    combiner = jnp.einsum("rk,rks->rs", route_weights, slot_onehot, precision=lax.Precision.HIGHEST)
    expert_onehot = (
        route_ids[:, :, None] == jnp.arange(experts, dtype=jnp.int32)[None, None, :]
    ).astype(jnp.float32)
    dense_weights = jnp.einsum(
        "rk,rke->re", route_weights, expert_onehot, precision=lax.Precision.HIGHEST
    )
    expert_mix = jnp.dot(
        combiner, returned, precision=lax.Precision.HIGHEST, preferred_element_type=jnp.float32
    )
    expert_mix = expert_mix + jnp.dot(
        dense_weights,
        down_bias.astype(jnp.float32),
        precision=lax.Precision.HIGHEST,
        preferred_element_type=jnp.float32,
    )
    mixed_out = (stream + expert_mix).astype(jnp.bfloat16)
    blocks = cached.reshape(-1, PAGE_LEN, cached.shape[1])
    page_pool = jnp.zeros_like(blocks).at[page_table[0]].set(blocks)
    return (mixed_out, page_pool)


def mid_kernel(
    own_ref,
    got_ref,
    residual_ref,
    out_bias_ref,
    gain_ref,
    ids_ref,
    logits_ref,
    down_bias_ref,
    base_ref,
    rows_ref,
):
    width = residual_ref.shape[1]
    experts = down_bias_ref.shape[0]
    hidden = (
        residual_ref[...].astype(jnp.float32)
        + own_ref[...].astype(jnp.float32)
        + got_ref[...].astype(jnp.float32)
        + out_bias_ref[...].astype(jnp.float32)
    ).astype(jnp.bfloat16)
    stream = hidden.astype(jnp.float32)
    normed = (
        stream
        * lax.rsqrt(jnp.mean(stream * stream, axis=-1, keepdims=True) + norm_eps)
        * gain_ref[...].astype(jnp.float32)
    ).astype(jnp.bfloat16)
    logits = logits_ref[...]
    expo = jnp.exp(logits - jnp.max(logits, axis=-1, keepdims=True))
    weights = expo / jnp.sum(expo, axis=-1, keepdims=True)
    high = weights.astype(jnp.bfloat16).astype(jnp.float32)
    low = (weights - high).astype(jnp.bfloat16).astype(jnp.float32)
    ids = ids_ref[...]
    lanes = lax.broadcasted_iota(jnp.int32, (ids.shape[0], LANES), 1)
    high_cols = jnp.zeros(lanes.shape, jnp.float32)
    low_cols = jnp.zeros(lanes.shape, jnp.float32)
    first = width % LANES
    for k in range(ids.shape[1]):
        at = ids[:, k : k + 1] + first
        high_cols = high_cols + jnp.where(lanes == at, high[:, k : k + 1], 0.0)
        low_cols = low_cols + jnp.where(lanes == at + experts, low[:, k : k + 1], 0.0)
    high_dense = high_cols[:, first : first + experts].astype(jnp.bfloat16)
    low_dense = low_cols[:, first + experts : first + 2 * experts].astype(jnp.bfloat16)
    bias = down_bias_ref[...]
    base_ref[...] = (
        stream
        + jnp.dot(high_dense, bias, preferred_element_type=jnp.float32)
        + jnp.dot(low_dense, bias, preferred_element_type=jnp.float32)
    )
    rows_ref[:, :width] = normed
    rows_ref[:, width:] = (high_cols + low_cols)[:, first:].astype(jnp.bfloat16)


def tiles(total, step):
    return [(start, min(step, total - start)) for start in range(0, total, step)]


def expert_kernel(parts, step, expert_ref, *refs):
    pieces, refs = refs[:parts], refs[parts:]
    gate_hbm, up_hbm, down_hbm, gate_bias_ref, up_bias_ref = refs[:5]
    outs, refs = refs[5 : 5 + parts], refs[5 + parts :]
    rows, picked, gate_up, down_w, active, spread, sems = refs
    piece = pieces[0].shape[0]
    total = rows.shape[0]
    slots = picked.shape[0]
    units, width = down_w.shape
    row_copies = [
        pltpu.make_async_copy(p, rows.at[pl.ds(i * piece, piece)], sems.at[i])
        for i, p in enumerate(pieces)
    ]
    chunks = tiles(units, step)
    up_copies = []
    for i, (start, size) in enumerate(chunks):
        for side, source in enumerate((gate_hbm, up_hbm)):
            up_copies.append(
                pltpu.make_async_copy(
                    source.at[pl.ds(start, size)],
                    gate_up.at[pl.ds(2 * start + side * size, size)],
                    sems.at[parts + 2 * i + side],
                )
            )
    blocks = tiles(width, 2 * step)
    down_copies = [
        pltpu.make_async_copy(
            down_hbm.at[:, pl.ds(start, size)],
            down_w.at[:, pl.ds(start, size)],
            sems.at[parts + 2 * len(chunks) + i],
        )
        for i, (start, size) in enumerate(blocks)
    ]
    for copy in row_copies + up_copies + down_copies:
        copy.start()
    up_bias = jnp.broadcast_to(up_bias_ref[...].astype(jnp.float32), (8, units)).T
    gate_bias = jnp.broadcast_to(gate_bias_ref[...].astype(jnp.float32), (8, units)).T
    earlier = jnp.where(
        lax.broadcasted_iota(jnp.int32, (total, total), 0)
        <= lax.broadcasted_iota(jnp.int32, (total, total), 1),
        1.0,
        0.0,
    ).astype(jnp.bfloat16)
    for copy in row_copies:
        copy.wait()

    expert = expert_ref[0]
    experts = (rows.shape[1] - width) // 4
    lane = lax.broadcasted_iota(jnp.int32, (16, LANES), 1)
    which = lax.broadcasted_iota(jnp.int32, (16, LANES), 0)
    choose = jnp.where(
        (lane == width % LANES + expert + which * experts) & (which < 2), 1.0, 0.0
    ).astype(jnp.bfloat16)
    found = lax.dot_general(
        choose,
        rows[:, rows.shape[1] - LANES :],
        (((1,), (1,)), ((), ())),
        preferred_element_type=jnp.float32,
    )
    share = found[0:1] + found[1:2]
    chosen = share > 0.0
    marks = jnp.broadcast_to(jnp.where(chosen, 1.0, 0.0), (16, total)).astype(jnp.bfloat16)
    count = jnp.dot(marks, earlier, preferred_element_type=jnp.float32)[0:1]
    slot = jnp.where(chosen, count - 1.0, -1.0).astype(jnp.int32)
    hit = lax.broadcasted_iota(jnp.int32, (slots, total), 0) == slot
    pick_f32 = jnp.where(hit, 1.0, 0.0)
    pick = pick_f32.astype(jnp.bfloat16)
    slot_share = jnp.sum(jnp.where(hit, share, 0.0), axis=1, keepdims=True)
    spread[...] = pick_f32.T.astype(jnp.bfloat16)
    for start, size in tiles(width, 512):
        picked[:, start : start + size] = jnp.dot(
            pick, rows[:, start : start + size], preferred_element_type=jnp.float32
        ).astype(jnp.bfloat16)

    for i, (start, size) in enumerate(chunks):
        up_copies[2 * i].wait()
        up_copies[2 * i + 1].wait()
        both = lax.dot_general(
            gate_up[2 * start : 2 * (start + size)],
            picked[...],
            (((1,), (1,)), ((), ())),
            preferred_element_type=jnp.float32,
        )
        gate = jnp.minimum(both[:size] + gate_bias[start : start + size, 0:1], swiglu_limit)
        up = jnp.clip(both[size:] + up_bias[start : start + size, 0:1], -swiglu_limit, swiglu_limit)
        value = gate * (1.0 / (1.0 + jnp.exp(-glu_alpha * gate))) * (up + 1.0)
        active[:, start : start + size] = value.T.astype(jnp.bfloat16)
    for i, (start, size) in enumerate(blocks):
        down_copies[i].wait()
        cols = slice(start, start + size)
        value = jnp.dot(active[...], down_w[:, cols], preferred_element_type=jnp.float32)
        scaled = (value * slot_share).astype(jnp.bfloat16)
        spread_rows = jnp.dot(spread[...], scaled, preferred_element_type=jnp.float32).astype(
            jnp.bfloat16
        )
        for k, out in enumerate(outs):
            out[:, cols] = spread_rows[k * piece : (k + 1) * piece]


def attention_kernel(
    side_ref,
    pages_ref,
    sink_ref,
    queries_ref,
    keys_values_ref,
    segments_ref,
    inverse_ref,
    weight_hbm,
    own_ref,
    other_ref,
    cache_ref,
    weight,
    attended,
    sems,
):
    length, query_width = queries_ref.shape
    width = weight.shape[0]
    kv_heads = keys_values_ref.shape[1] // LANES
    group_tiles = query_width // LANES // kv_heads
    chunks = tiles(width, 512)
    copies = [
        pltpu.make_async_copy(
            weight_hbm.at[pl.ds(start, size)], weight.at[pl.ds(start, size)], sems.at[i]
        )
        for i, (start, size) in enumerate(chunks)
    ]
    for copy in copies:
        copy.start()
    named = jnp.broadcast_to(segments_ref[...].astype(jnp.float32), (length, length))
    visible = (named == named.T) & (
        lax.broadcasted_iota(jnp.int32, (length, length), 1)
        <= lax.broadcasted_iota(jnp.int32, (length, length), 0)
    )
    positions = jnp.sum(jnp.where(visible, 1.0, 0.0), axis=1, keepdims=True) - 1.0
    angles = positions * inverse_ref[...]
    lane = lax.broadcasted_iota(jnp.int32, (length, LANES), 1)
    lower = lane % HEAD < HEAD // 2
    cosine = jnp.cos(angles)
    sine = jnp.sin(angles)
    sine = jnp.where(lower, -sine, sine)
    left = lane < HEAD

    def turned(tile):
        swapped = jnp.where(
            lower, pltpu.roll(tile, LANES - HEAD // 2, 1), pltpu.roll(tile, HEAD // 2, 1)
        )
        return tile * cosine + swapped * sine

    seen = jnp.concatenate([visible] * (2 * group_tiles), axis=0)
    for k in range(kv_heads):
        raw = keys_values_ref[:, k * LANES : (k + 1) * LANES].astype(jnp.float32)
        pair = jnp.where(left, turned(raw), raw).astype(jnp.bfloat16)
        for b in range(cache_ref.shape[0]):
            cache_ref[pages_ref[0, b], :, k * LANES : (k + 1) * LANES] = pair[
                b * PAGE_LEN : (b + 1) * PAGE_LEN
            ]
        heads = []
        sinks = []
        for t in range(k * group_tiles, (k + 1) * group_tiles):
            tile = turned(queries_ref[:, t * LANES : (t + 1) * LANES].astype(jnp.float32))
            heads.append(jnp.where(left, tile, 0.0))
            heads.append(jnp.where(left, pltpu.roll(tile, HEAD, 1), 0.0))
            sinks.append(jnp.full((length, 1), sink_ref[2 * t], jnp.float32))
            sinks.append(jnp.full((length, 1), sink_ref[2 * t + 1], jnp.float32))
        sink = jnp.concatenate(sinks, axis=0)
        scores = lax.dot_general(
            jnp.concatenate(heads, axis=0).astype(jnp.bfloat16),
            pair,
            (((1,), (1,)), ((), ())),
            preferred_element_type=jnp.float32,
        ) * HEAD ** (-0.5)
        scores = jnp.where(seen, scores, -1e30)
        highest = jnp.maximum(jnp.max(scores, axis=-1, keepdims=True), sink)
        expo = jnp.where(seen, jnp.exp(scores - highest), 0.0)
        denominator = jnp.sum(expo, axis=-1, keepdims=True) + jnp.exp(sink - highest)
        probabilities = (expo / denominator).astype(jnp.bfloat16)
        mixed = jnp.dot(probabilities, pair, preferred_element_type=jnp.float32)
        for t in range(group_tiles):
            even = mixed[2 * t * length : (2 * t + 1) * length]
            odd = mixed[(2 * t + 1) * length : (2 * t + 2) * length]
            start = (k * group_tiles + t) * LANES
            attended[:, start : start + LANES] = jnp.where(
                left, pltpu.roll(even, HEAD, 1), odd
            ).astype(jnp.bfloat16)
    first_side = side_ref[0] == 0
    half = own_ref.shape[0]
    for i, (start, size) in enumerate(chunks):
        copies[i].wait()
        projected = lax.dot_general(
            attended[...],
            weight[start : start + size],
            (((1,), (1,)), ((), ())),
            preferred_element_type=jnp.float32,
        )
        top, bottom = projected[:half], projected[half:]
        own_ref[:, start : start + size] = jnp.where(first_side, top, bottom)
        other_ref[:, start : start + size] = jnp.where(first_side, bottom, top).astype(jnp.bfloat16)


def run_attention(side, page_table, sink_logits, queries, keys_values, segments, out_weight):
    length, query_width = queries.shape
    width = out_weight.shape[1]
    half = length // 2
    inverse = np.float32(rope_base) ** (
        -(np.arange(LANES) % (HEAD // 2)).astype(np.float32) / np.float32(HEAD // 2)
    )
    smem = pl.BlockSpec(memory_space=pltpu.SMEM)
    return pl.pallas_call(
        attention_kernel,
        out_shape=[
            jax.ShapeDtypeStruct((half, width), jnp.float32),
            jax.ShapeDtypeStruct((half, width), jnp.bfloat16),
            jax.ShapeDtypeStruct(
                (length // PAGE_LEN, PAGE_LEN, keys_values.shape[1]), jnp.bfloat16
            ),
        ],
        in_specs=[smem] * 3 + [vmem()] * 4 + [anywhere()],
        out_specs=[vmem()] * 3,
        scratch_shapes=[
            pltpu.VMEM((width, query_width), jnp.bfloat16),
            pltpu.VMEM((length, query_width), jnp.bfloat16),
            pltpu.SemaphoreType.DMA((len(tiles(width, 512)),)),
        ],
        compiler_params=pltpu.CompilerParams(vmem_limit_bytes=24 * 2**20),
        name="attention",
    )(
        side,
        page_table,
        sink_logits,
        queries,
        keys_values,
        segments[None],
        jnp.asarray(inverse.astype(np.float32))[None],
        out_weight.T,
    )


def vmem():
    return pl.BlockSpec(memory_space=pltpu.VMEM)


def anywhere():
    return pl.BlockSpec(memory_space=pl.ANY)


def run_expert(expert, pieces, gate_weight, gate_bias, up_weight, up_bias, down_weight, slots):
    parts = len(pieces)
    piece, padded = pieces[0].shape
    hidden_units, width = down_weight.shape
    total = parts * piece
    step = 256
    copies = parts + 2 * len(tiles(hidden_units, step)) + len(tiles(width, 2 * step))
    return pl.pallas_call(
        functools.partial(expert_kernel, parts, step),
        out_shape=[jax.ShapeDtypeStruct((piece, width), jnp.bfloat16)] * parts,
        in_specs=[pl.BlockSpec(memory_space=pltpu.SMEM)]
        + [anywhere()] * (parts + 3)
        + [vmem()] * 2,
        out_specs=[vmem()] * parts,
        scratch_shapes=[
            pltpu.VMEM((total, padded), jnp.bfloat16),
            pltpu.VMEM((slots, width), jnp.bfloat16),
            pltpu.VMEM((2 * hidden_units, width), jnp.bfloat16),
            pltpu.VMEM(down_weight.shape, jnp.bfloat16),
            pltpu.VMEM((slots, hidden_units), jnp.bfloat16),
            pltpu.VMEM((total, slots), jnp.bfloat16),
            pltpu.SemaphoreType.DMA((copies,)),
        ],
        compiler_params=pltpu.CompilerParams(vmem_limit_bytes=52 * 2**20),
        cost_estimate=pl.CostEstimate(
            flops=2 * slots * width * (3 * hidden_units + 2 * total),
            bytes_accessed=6 * width * hidden_units,
            transcendentals=slots * hidden_units,
        ),
        name="expert",
    )(expert, *pieces, gate_weight.T, up_weight.T, down_weight, gate_bias, up_bias)


AXES = ("req", "tp")


def moved(array, n_req, step):
    outer, mid, core, tp = step
    pairs = []
    for source in range(2 * n_req):
        req, side = divmod(source, 2)
        place = (req // 4 ^ outer) * 4 + (req // 2 % 2 ^ mid) * 2 + (req % 2 ^ core)
        pairs.append((source, place * 2 + (side ^ tp)))
    return lax.ppermute(array, AXES, pairs)


def crossed(array, n_req, by_core):
    pairs = []
    for source in range(2 * n_req):
        req, side = divmod(source, 2)
        if req % 2 == by_core:
            pairs.append((source, (req ^ 2) * 2 + side))
        else:
            pairs.append((source, req * 2 + (side ^ 1)))
    return lax.ppermute(array, AXES, pairs)


def gather_rows(rows, n_req):
    outer = n_req // 4
    line = jnp.concatenate([rows] + [moved(rows, n_req, (k, 0, 0, 0)) for k in range(1, outer)])
    first = crossed(line, n_req, 0)
    second = crossed(line, n_req, 1)
    both = crossed(first, n_req, 1)
    own = [line, first, second, both]
    return own + [moved(piece, n_req, (0, 0, 1, 0)) for piece in own]


def add_rows(left, right):
    return (left.astype(jnp.float32) + right.astype(jnp.float32)).astype(jnp.bfloat16)


def scatter_rows(sums, n_req):
    own, other = sums[:4], sums[4:]
    line, first, second, both = [
        add_rows(mine, moved(theirs, n_req, (0, 0, 1, 0))) for mine, theirs in zip(own, other)
    ]
    first = add_rows(first, crossed(both, n_req, 1))
    line = add_rows(line, crossed(second, n_req, 1))
    line = add_rows(line, crossed(first, n_req, 0))
    outer = n_req // 4
    count = line.shape[0] // outer
    blocks = [line[k * count : (k + 1) * count] for k in range(outer)]
    return [blocks[0]] + [
        moved(block, n_req, (k, 0, 0, 0)) for k, block in enumerate(blocks) if k > 0
    ]


def gathered_body(
    n_req,
    queries,
    keys_values,
    segments,
    sink_logits,
    out_weight,
    out_bias,
    residual,
    norm_gain,
    route_ids,
    route_logits,
    gate_weight,
    gate_bias,
    up_weight,
    up_bias,
    down_weight,
    down_bias,
    page_table,
):
    tok_count, width = residual.shape
    side = lax.axis_index("tp")[None]
    own, other, page_pool = run_attention(
        side, page_table, sink_logits, queries, keys_values, segments, out_weight
    )
    got = moved(other, n_req, (0, 0, 0, 1))
    experts = down_bias.shape[0]
    base, rows = pl.pallas_call(
        mid_kernel,
        out_shape=[
            jax.ShapeDtypeStruct((tok_count, width), jnp.float32),
            jax.ShapeDtypeStruct((tok_count, width + 4 * experts), jnp.bfloat16),
        ],
        in_specs=[vmem()] * 8,
        out_specs=[vmem()] * 2,
        name="norm_rows",
    )(
        own,
        got,
        residual,
        out_bias[None],
        norm_gain[None],
        route_ids,
        route_logits,
        down_bias,
    )
    pieces = gather_rows(rows, n_req)
    slots = 2 * n_req * slot_limit(tok_count, route_ids.shape[1], experts)
    sums = run_expert(
        lax.axis_index("req")[None],
        pieces,
        gate_weight[0],
        gate_bias,
        up_weight[0],
        up_bias,
        down_weight[0],
        slots,
    )
    mixed = base
    for part in scatter_rows(sums, n_req):
        mixed = mixed + part.astype(jnp.float32)
    return (mixed.astype(jnp.bfloat16), page_pool)


def solution(mesh):
    in_specs = (
        P("req", "tp"),
        P("req", "tp"),
        P("req"),
        P("tp"),
        P("tp", None),
        P(),
        P(("req", "tp"), None),
        P(),
        P(("req", "tp"), None),
        P(("req", "tp"), None),
        P("req", None, "tp"),
        P("req", "tp"),
        P("req", None, "tp"),
        P("req", "tp"),
        P("req", "tp", None),
        P(),
        P("req", None),
    )
    out_specs = (P(("req", "tp"), None), P("req", None, "tp"))
    n_req, n_tp = mesh.shape["req"], mesh.shape["tp"]
    chosen = functools.partial(gathered_body, n_req) if (n_req, n_tp) == (16, 2) else body
    return jax.shard_map(chosen, mesh=mesh, in_specs=in_specs, out_specs=out_specs, check_vma=False)
```

```python
import functools

import jax
import jax.numpy as jnp
import numpy as np
from jax import lax
from jax.experimental import pallas as pl
from jax.experimental.pallas import tpu as pltpu
from jax.sharding import PartitionSpec as P

HEAD = 64
PAGE_LEN = 16
LANES = 128
VMEM_LIMIT = 60 * 2**20
LOAD_ROWS = 480


rope_base = 150000.0
norm_eps = 1e-05
swiglu_limit = 7.0
glu_alpha = 1.702


def seg_positions(segment_ids):
    length = segment_ids.shape[0]
    indices = jnp.arange(length, dtype=jnp.int32)
    change = jnp.concatenate([jnp.ones((1,), dtype=bool), segment_ids[1:] != segment_ids[:-1]])
    starts = lax.cummax(jnp.where(change, indices, 0), axis=0)
    return indices - starts


def rotate(values, positions):
    half_dim = values.shape[-1] // 2
    inverse = rope_base ** (-jnp.arange(half_dim, dtype=jnp.float32) / half_dim)
    angles = positions.astype(jnp.float32)[:, None] * inverse[None, :]
    cosine = jnp.cos(angles)[:, None, :]
    sine_col = jnp.sin(angles)[:, None, :]
    first_half = values[..., :half_dim]
    second_half = values[..., half_dim:]
    return jnp.concatenate(
        [
            first_half * cosine - second_half * sine_col,
            second_half * cosine + first_half * sine_col,
        ],
        axis=-1,
    )


def attend_group(queries, keys_values, segment_ids, sink_logits):
    length = queries.shape[0]
    kv_heads = keys_values.shape[1] // (2 * HEAD)
    q_heads = queries.shape[1] // HEAD
    group_size = q_heads // kv_heads
    positions = seg_positions(segment_ids)
    q_rot = rotate(queries.astype(jnp.float32).reshape(length, q_heads, HEAD), positions).astype(
        jnp.bfloat16
    )
    q_rot = q_rot.reshape(length, kv_heads, group_size, HEAD)
    key_part = keys_values.reshape(length, kv_heads, 2, HEAD)
    k_rot = rotate(key_part[:, :, 0].astype(jnp.float32), positions).astype(jnp.bfloat16)
    values = key_part[:, :, 1]
    scores = jnp.einsum(
        "qkgd,skd->kgqs", q_rot, k_rot, preferred_element_type=jnp.float32
    ) * HEAD ** (-0.5)
    indices = jnp.arange(length, dtype=jnp.int32)
    visible = (segment_ids[:, None] == segment_ids[None, :]) & (
        indices[None, :] <= indices[:, None]
    )
    scores = jnp.where(visible, scores, -jnp.inf)
    sink_col = sink_logits.reshape(kv_heads, group_size)[:, :, None]
    highest = jnp.maximum(jnp.max(scores, axis=-1), sink_col)
    expo_terms = jnp.exp(scores - highest[..., None])
    denominator = jnp.sum(expo_terms, axis=-1) + jnp.exp(sink_col - highest)
    probabilities = (expo_terms / denominator[..., None]).astype(jnp.bfloat16)
    attended = jnp.einsum(
        "kgqs,skd->qkgd", probabilities, values, preferred_element_type=jnp.float32
    )
    attended = attended.astype(jnp.bfloat16).reshape(length, q_heads * HEAD)
    cached = jnp.stack([k_rot, values], axis=2).reshape(length, kv_heads * 2 * HEAD)
    return (attended, cached)


def slot_index(routes, experts, capacity):
    blocks, row_count, route_width = routes.shape
    flat_ids = routes.reshape(blocks, row_count * route_width)
    onehot = (flat_ids[:, :, None] == jnp.arange(experts, dtype=jnp.int32)[None, None, :]).astype(
        jnp.int32
    )
    earlier = jnp.cumsum(onehot, axis=1) - onehot
    position = jnp.sum(earlier * onehot, axis=2)
    block_ids = jnp.arange(blocks, dtype=jnp.int32)[:, None]
    slot_ids = flat_ids * (blocks * capacity) + block_ids * capacity + position
    return slot_ids.reshape(blocks * row_count, route_width).astype(jnp.int32)


def dispatch(tokens, slot_ids, slot_total):
    row_count = tokens.shape[0]
    owners = jnp.broadcast_to(jnp.arange(row_count, dtype=jnp.int32)[:, None], slot_ids.shape)
    member = (
        jnp.full((slot_total,), row_count, jnp.int32)
        .at[slot_ids.reshape(-1)]
        .set(owners.reshape(-1))
    )
    padded = jnp.concatenate([tokens, jnp.zeros((1, tokens.shape[1]), tokens.dtype)], axis=0)
    return padded[member]


def slot_limit(tok_count, route_width, experts):
    return max(2, 2 * tok_count * route_width // experts)


def body(
    queries,
    keys_values,
    segments,
    sink_logits,
    out_weight,
    out_bias,
    residual,
    norm_gain,
    route_ids,
    route_logits,
    gate_weight,
    gate_bias,
    up_weight,
    up_bias,
    down_weight,
    down_bias,
    page_table,
):
    attended, cached = attend_group(queries, keys_values, segments, sink_logits)
    projected = lax.psum_scatter(
        jnp.dot(attended, out_weight, preferred_element_type=jnp.float32).astype(jnp.bfloat16),
        "tp",
        scatter_dimension=0,
        tiled=True,
    ).astype(jnp.float32)
    hidden = (residual.astype(jnp.float32) + projected + out_bias.astype(jnp.float32)).astype(
        jnp.bfloat16
    )
    stream = hidden.astype(jnp.float32)
    normed = (
        stream
        * lax.rsqrt(jnp.mean(stream * stream, axis=-1, keepdims=True) + norm_eps)
        * norm_gain.astype(jnp.float32)
    ).astype(jnp.bfloat16)
    route_weights = jax.nn.softmax(route_logits, axis=-1)
    tok_count, route_width = route_ids.shape
    experts = down_bias.shape[0]
    model_width = residual.shape[1]
    capacity = slot_limit(tok_count, route_width, experts)
    own_slots = slot_index(route_ids[None], experts, capacity)
    group_rows, group_routes = (
        lax.all_gather(normed, "tp", axis=0, tiled=True),
        lax.all_gather(route_ids, "tp", axis=0, tiled=True),
    )
    tp_count = group_rows.shape[0] // tok_count
    all_slots = slot_index(
        group_routes.reshape(tp_count, tok_count, route_width), experts, capacity
    )
    dispatched = dispatch(group_rows, all_slots, experts * tp_count * capacity).reshape(
        experts, tp_count, capacity, model_width
    )
    received = lax.all_to_all(dispatched, "req", split_axis=0, concat_axis=0, tiled=True)
    slot_shape = received.shape
    flat_rows = received.reshape(-1, model_width)
    gate_act = jnp.dot(flat_rows, gate_weight[0], preferred_element_type=jnp.float32) + gate_bias[
        0
    ].astype(jnp.float32)
    up_act = jnp.dot(flat_rows, up_weight[0], preferred_element_type=jnp.float32) + up_bias[
        0
    ].astype(jnp.float32)
    gate_act = jnp.minimum(gate_act, swiglu_limit)
    up_act = jnp.clip(up_act, -swiglu_limit, swiglu_limit)
    active = (gate_act * jax.nn.sigmoid(glu_alpha * gate_act) * (up_act + 1.0)).astype(jnp.bfloat16)
    partial_value = jnp.dot(active, down_weight[0], preferred_element_type=jnp.float32).reshape(
        slot_shape
    )
    summed = lax.psum_scatter(
        partial_value.astype(jnp.bfloat16), "tp", scatter_dimension=1, tiled=True
    ).astype(jnp.float32)
    returned = lax.all_to_all(
        summed.astype(jnp.bfloat16), "req", split_axis=0, concat_axis=0, tiled=True
    ).astype(summed.dtype)
    returned = returned.reshape(experts * capacity, model_width)
    slot_onehot = (
        own_slots[:, :, None] == jnp.arange(experts * capacity, dtype=jnp.int32)[None, None, :]
    ).astype(jnp.float32)
    combiner = jnp.einsum("rk,rks->rs", route_weights, slot_onehot, precision=lax.Precision.HIGHEST)
    expert_onehot = (
        route_ids[:, :, None] == jnp.arange(experts, dtype=jnp.int32)[None, None, :]
    ).astype(jnp.float32)
    dense_weights = jnp.einsum(
        "rk,rke->re", route_weights, expert_onehot, precision=lax.Precision.HIGHEST
    )
    expert_mix = jnp.dot(
        combiner, returned, precision=lax.Precision.HIGHEST, preferred_element_type=jnp.float32
    )
    expert_mix = expert_mix + jnp.dot(
        dense_weights,
        down_bias.astype(jnp.float32),
        precision=lax.Precision.HIGHEST,
        preferred_element_type=jnp.float32,
    )
    mixed_out = (stream + expert_mix).astype(jnp.bfloat16)
    blocks = cached.reshape(-1, PAGE_LEN, cached.shape[1])
    page_pool = jnp.zeros_like(blocks).at[page_table[0]].set(blocks)
    return (mixed_out, page_pool)


def mid_kernel(
    own_ref,
    got_ref,
    residual_ref,
    out_bias_ref,
    gain_ref,
    ids_ref,
    logits_ref,
    down_bias_ref,
    base_ref,
    rows_ref,
):
    width = residual_ref.shape[1]
    experts = down_bias_ref.shape[0]
    hidden = (
        residual_ref[...].astype(jnp.float32)
        + own_ref[...].astype(jnp.float32)
        + got_ref[...].astype(jnp.float32)
        + out_bias_ref[...].astype(jnp.float32)
    ).astype(jnp.bfloat16)
    stream = hidden.astype(jnp.float32)
    normed = (
        stream
        * lax.rsqrt(jnp.mean(stream * stream, axis=-1, keepdims=True) + norm_eps)
        * gain_ref[...].astype(jnp.float32)
    ).astype(jnp.bfloat16)
    logits = logits_ref[...]
    expo = jnp.exp(logits - jnp.max(logits, axis=0, keepdims=True))
    weights = expo / jnp.sum(expo, axis=0, keepdims=True)
    high = weights.astype(jnp.bfloat16).astype(jnp.float32)
    low = (weights - high).astype(jnp.bfloat16).astype(jnp.float32)
    ids = ids_ref[...]
    column = lax.broadcasted_iota(jnp.int32, (LANES, ids.shape[1]), 0)
    high_cols = jnp.zeros(column.shape, jnp.float32)
    low_cols = jnp.zeros(column.shape, jnp.float32)
    first = width % LANES
    for k in range(ids.shape[0]):
        at = ids[k : k + 1] + first
        high_cols = high_cols + jnp.where(column == at, high[k : k + 1], 0.0)
        low_cols = low_cols + jnp.where(column == at + experts, low[k : k + 1], 0.0)
    high_cols = high_cols.T
    low_cols = low_cols.T
    high_dense = high_cols[:, first : first + experts].astype(jnp.bfloat16)
    low_dense = low_cols[:, first + experts : first + 2 * experts].astype(jnp.bfloat16)
    bias = down_bias_ref[...]
    base_ref[...] = (
        stream
        + jnp.dot(high_dense, bias, preferred_element_type=jnp.float32)
        + jnp.dot(low_dense, bias, preferred_element_type=jnp.float32)
    )
    rows_ref[:, :width] = normed
    rows_ref[:, width:] = (high_cols + low_cols)[:, first:].astype(jnp.bfloat16)


def tiles(total, step):
    return [(start, min(step, total - start)) for start in range(0, total, step)]


def by_rows(left, right):
    return lax.dot_general(
        left, right, (((1,), (1,)), ((), ())), preferred_element_type=jnp.float32
    )


def load_kernel(parts, *refs):
    sources, targets, sign, sems = refs[:parts], refs[parts : 2 * parts], refs[-2], refs[-1]
    copies = []
    for source, target in zip(sources, targets):
        for start, size in tiles(source.shape[0], LOAD_ROWS):
            here = pl.ds(start, size)
            copies.append(
                pltpu.make_async_copy(source.at[here], target.at[here], sems.at[len(copies)])
            )
    for copy in copies:
        copy.start()
    for copy in copies:
        copy.wait()
    sign[...] = targets[0][: sign.shape[0], : sign.shape[1]]


def load(weights, reserve):
    parts = len(weights)
    copies = sum(len(tiles(weight.shape[0], LOAD_ROWS)) for weight in weights)
    return pl.pallas_call(
        functools.partial(load_kernel, parts),
        out_shape=[jax.ShapeDtypeStruct(weight.shape, weight.dtype) for weight in weights]
        + [jax.ShapeDtypeStruct((16, LANES), weights[0].dtype)],
        in_specs=[anywhere()] * parts,
        out_specs=[vmem()] * (parts + 1),
        scratch_shapes=[pltpu.SemaphoreType.DMA((copies,))],
        compiler_params=pltpu.CompilerParams(vmem_limit_bytes=reserve),
        cost_estimate=pl.CostEstimate(
            flops=0, bytes_accessed=4 * sum(w.size for w in weights), transcendentals=0
        ),
        name="load",
    )(*weights)


def expert_kernel(parts, block, limit, step, expert_ref, *refs):
    pieces, refs = refs[:parts], refs[parts:]
    gate_w, up_w, down_w, gate_bias_ref, up_bias_ref = refs[:5]
    outs, (picked, active) = refs[7 : 7 + parts], refs[7 + parts :]
    piece, padded = pieces[0].shape
    total = parts * piece
    units, width = down_w.shape
    group = 2 * piece
    group_slots = group // block * limit
    up_bias = jnp.broadcast_to(up_bias_ref[...].astype(jnp.float32), (8, units)).T
    gate_bias = jnp.broadcast_to(gate_bias_ref[...].astype(jnp.float32), (8, units)).T

    expert = expert_ref[0]
    experts = (padded - width) // 4
    lane = lax.broadcasted_iota(jnp.int32, (16, LANES), 1)
    which = lax.broadcasted_iota(jnp.int32, (16, LANES), 0)
    choose = jnp.where(
        (lane == width % LANES + expert + which * experts) & (which < 2), 1.0, 0.0
    ).astype(jnp.bfloat16)
    found = by_rows(
        choose, jnp.concatenate([p[:, padded - LANES :] for p in pieces], axis=0)
    )
    share = jnp.broadcast_to(found[0:1] + found[1:2], (8, total))
    chosen = share > 0.0
    token = lax.broadcasted_iota(jnp.int32, (8, total), 1)
    count = jnp.where(chosen, 1, 0)
    reach = 1
    while reach < block:
        count = count + jnp.where(token % block >= reach, pltpu.roll(count, reach, 1), 0)
        reach *= 2
    slot = jnp.where(chosen, token // block * limit + count - 1, -1)
    spreads, shares = [], []
    for g in range(total // group):
        here = slice(g * group, (g + 1) * group)
        hit = (
            lax.broadcasted_iota(jnp.int32, (group_slots, group), 0) + g * group_slots
            == slot[0:1, here]
        )
        shares.append(jnp.sum(jnp.where(hit, share[0:1, here], 0.0), axis=1, keepdims=True))
        pick = jnp.where(hit, 1.0, 0.0)
        spreads.append(pick.T.astype(jnp.bfloat16))
        pick = pick.astype(jnp.bfloat16)
        for start, size in tiles(width, 2 * step):
            cols = slice(start, start + size)
            both = jnp.concatenate([pieces[2 * g][:, cols], pieces[2 * g + 1][:, cols]], axis=0)
            picked[g * group_slots : (g + 1) * group_slots, cols] = jnp.dot(
                pick, both, preferred_element_type=jnp.float32
            ).astype(jnp.bfloat16)
    slot_share = jnp.concatenate(shares, axis=0)

    for start, size in tiles(units, step):
        here = slice(start, start + size)
        gate = by_rows(gate_w[here], picked[...])
        up = by_rows(up_w[here], picked[...])
        gate = jnp.minimum(gate + gate_bias[here, 0:1], swiglu_limit)
        up = jnp.clip(up + up_bias[here, 0:1], -swiglu_limit, swiglu_limit)
        value = gate * (1.0 / (1.0 + jnp.exp(-glu_alpha * gate))) * (up + 1.0)
        active[:, here] = value.T.astype(jnp.bfloat16)
    for start, size in tiles(width, 2 * step):
        cols = slice(start, start + size)
        value = jnp.dot(active[...], down_w[:, cols], preferred_element_type=jnp.float32)
        scaled = (value * slot_share).astype(jnp.bfloat16)
        for g, spread in enumerate(spreads):
            sums = jnp.dot(
                spread,
                scaled[g * group_slots : (g + 1) * group_slots],
                preferred_element_type=jnp.float32,
            ).astype(jnp.bfloat16)
            outs[2 * g][:, cols] = sums[:piece]
            outs[2 * g + 1][:, cols] = sums[piece:]


def attention_kernel(
    side_ref,
    expert_in_ref,
    pages_ref,
    sink_ref,
    queries_ref,
    keys_values_ref,
    segments_ref,
    inverse_ref,
    weight_hbm,
    own_ref,
    other_ref,
    cache_ref,
    expert_ref,
    weight,
    attended,
    sems,
):
    expert_ref[0] = expert_in_ref[0]
    length, query_width = queries_ref.shape
    width = weight.shape[0]
    kv_heads = keys_values_ref.shape[1] // LANES
    group_tiles = query_width // LANES // kv_heads
    chunks = tiles(width, 512)
    copies = [
        pltpu.make_async_copy(
            weight_hbm.at[pl.ds(start, size)], weight.at[pl.ds(start, size)], sems.at[i]
        )
        for i, (start, size) in enumerate(chunks)
    ]
    for copy in copies[:2]:
        copy.start()
    named = jnp.broadcast_to(segments_ref[...].astype(jnp.float32), (length, length))
    visible = (named == named.T) & (
        lax.broadcasted_iota(jnp.int32, (length, length), 1)
        <= lax.broadcasted_iota(jnp.int32, (length, length), 0)
    )
    positions = jnp.sum(jnp.where(visible, 1.0, 0.0), axis=1, keepdims=True) - 1.0
    angles = positions * inverse_ref[...]
    lane = lax.broadcasted_iota(jnp.int32, (length, LANES), 1)
    lower = lane % HEAD < HEAD // 2
    cosine = jnp.cos(angles)
    sine = jnp.sin(angles)
    sine = jnp.where(lower, -sine, sine)
    left = lane < HEAD

    def turned(tile):
        swapped = jnp.where(
            lower, pltpu.roll(tile, LANES - HEAD // 2, 1), pltpu.roll(tile, HEAD // 2, 1)
        )
        return tile * cosine + swapped * sine

    seen = jnp.concatenate([visible] * (2 * group_tiles), axis=0)
    for k in range(kv_heads):
        raw = keys_values_ref[:, k * LANES : (k + 1) * LANES].astype(jnp.float32)
        pair = jnp.where(left, turned(raw), raw).astype(jnp.bfloat16)
        for b in range(cache_ref.shape[0]):
            cache_ref[pages_ref[0, b], :, k * LANES : (k + 1) * LANES] = pair[
                b * PAGE_LEN : (b + 1) * PAGE_LEN
            ]
        heads = []
        sinks = []
        for t in range(k * group_tiles, (k + 1) * group_tiles):
            tile = turned(queries_ref[:, t * LANES : (t + 1) * LANES].astype(jnp.float32))
            heads.append(jnp.where(left, tile, 0.0))
            heads.append(jnp.where(left, pltpu.roll(tile, HEAD, 1), 0.0))
            sinks.append(jnp.full((length, 1), sink_ref[2 * t], jnp.float32))
            sinks.append(jnp.full((length, 1), sink_ref[2 * t + 1], jnp.float32))
        sink = jnp.concatenate(sinks, axis=0)
        scores = lax.dot_general(
            jnp.concatenate(heads, axis=0).astype(jnp.bfloat16),
            pair,
            (((1,), (1,)), ((), ())),
            preferred_element_type=jnp.float32,
        ) * HEAD ** (-0.5)
        scores = jnp.where(seen, scores, -1e30)
        highest = jnp.maximum(jnp.max(scores, axis=-1, keepdims=True), sink)
        expo = jnp.where(seen, jnp.exp(scores - highest), 0.0)
        denominator = jnp.sum(expo, axis=-1, keepdims=True) + jnp.exp(sink - highest)
        probabilities = (expo / denominator).astype(jnp.bfloat16)
        mixed = jnp.dot(probabilities, pair, preferred_element_type=jnp.float32)
        for t in range(group_tiles):
            even = mixed[2 * t * length : (2 * t + 1) * length]
            odd = mixed[(2 * t + 1) * length : (2 * t + 2) * length]
            start = (k * group_tiles + t) * LANES
            attended[:, start : start + LANES] = jnp.where(
                left, pltpu.roll(even, HEAD, 1), odd
            ).astype(jnp.bfloat16)
    first_side = side_ref[0] == 0
    half = own_ref.shape[0]
    for i, (start, size) in enumerate(chunks):
        copies[i].wait()
        if i + 2 < len(copies):
            copies[i + 2].start()
        projected = by_rows(attended[...], weight[start : start + size])
        top, bottom = projected[:half], projected[half:]
        own_ref[:, start : start + size] = jnp.where(first_side, top, bottom)
        other_ref[:, start : start + size] = jnp.where(first_side, bottom, top).astype(jnp.bfloat16)


def run_attention(side, expert, page_table, sink_logits, queries, keys_values, segments, out_weight):
    length, query_width = queries.shape
    width = out_weight.shape[1]
    half = length // 2
    inverse = np.float32(rope_base) ** (
        -(np.arange(LANES) % (HEAD // 2)).astype(np.float32) / np.float32(HEAD // 2)
    )
    smem = pl.BlockSpec(memory_space=pltpu.SMEM)
    return pl.pallas_call(
        attention_kernel,
        out_shape=[
            jax.ShapeDtypeStruct((half, width), jnp.float32),
            jax.ShapeDtypeStruct((half, width), jnp.bfloat16),
            jax.ShapeDtypeStruct(
                (length // PAGE_LEN, PAGE_LEN, keys_values.shape[1]), jnp.bfloat16
            ),
            jax.ShapeDtypeStruct((1,), jnp.int32),
        ],
        in_specs=[smem] * 4 + [vmem()] * 4 + [anywhere()],
        out_specs=[vmem()] * 3 + [smem],
        scratch_shapes=[
            pltpu.VMEM((width, query_width), jnp.bfloat16),
            pltpu.VMEM((length, query_width), jnp.bfloat16),
            pltpu.SemaphoreType.DMA((len(tiles(width, 512)),)),
        ],
        compiler_params=pltpu.CompilerParams(vmem_limit_bytes=VMEM_LIMIT),
        name="attention",
    )(
        side,
        expert,
        page_table,
        sink_logits,
        queries,
        keys_values,
        segments[None],
        jnp.asarray(inverse.astype(np.float32))[None],
        out_weight.T,
    )


def vmem():
    return pl.BlockSpec(memory_space=pltpu.VMEM)


def anywhere():
    return pl.BlockSpec(memory_space=pl.ANY)


def run_expert(
    expert, pieces, gate_rows, gate_bias, up_rows, up_bias, down_weight, sign, late_sign, block, limit
):
    parts = len(pieces)
    piece, padded = pieces[0].shape
    hidden_units, width = down_weight.shape
    slots = parts * piece // block * limit
    return pl.pallas_call(
        functools.partial(expert_kernel, parts, block, limit, 256),
        out_shape=[jax.ShapeDtypeStruct((piece, width), jnp.bfloat16)] * parts,
        in_specs=[pl.BlockSpec(memory_space=pltpu.SMEM)] + [vmem()] * (parts + 5)
        + [anywhere()] * 2,
        out_specs=[vmem()] * parts,
        scratch_shapes=[
            pltpu.VMEM((slots, width), jnp.bfloat16),
            pltpu.VMEM((slots, hidden_units), jnp.bfloat16),
        ],
        compiler_params=pltpu.CompilerParams(vmem_limit_bytes=8 * 2**20),
        cost_estimate=pl.CostEstimate(
            flops=6 * slots * width * hidden_units,
            bytes_accessed=6 * width * hidden_units,
            transcendentals=slots * hidden_units,
        ),
        name="expert",
    )(expert, *pieces, gate_rows, up_rows, down_weight, gate_bias, up_bias, sign, late_sign)


AXES = ("req", "tp")


def moved(array, n_req, step):
    outer, mid, core, tp = step
    pairs = []
    for source in range(2 * n_req):
        req, side = divmod(source, 2)
        place = (req // 4 ^ outer) * 4 + (req // 2 % 2 ^ mid) * 2 + (req % 2 ^ core)
        pairs.append((source, place * 2 + (side ^ tp)))
    return lax.ppermute(array, AXES, pairs)


def crossed(array, n_req, by_core):
    pairs = []
    for source in range(2 * n_req):
        req, side = divmod(source, 2)
        if req % 2 == by_core:
            pairs.append((source, (req ^ 2) * 2 + side))
        else:
            pairs.append((source, req * 2 + (side ^ 1)))
    return lax.ppermute(array, AXES, pairs)


def gather_rows(rows, n_req, sign, late_sign):
    outer = n_req // 4
    line = jnp.concatenate([rows] + [moved(rows, n_req, (k, 0, 0, 0)) for k in range(1, outer)])
    first = crossed(line, n_req, 0)
    second = crossed(line, n_req, 1)
    sent, sign = lax.optimization_barrier((first, sign))
    both = crossed(sent, n_req, 1)
    own = [line, first, second, both]
    sent, late_sign = lax.optimization_barrier((both, late_sign))
    pieces = own + [moved(piece, n_req, (0, 0, 1, 0)) for piece in (line, first, second, sent)]
    return pieces, sign, late_sign


def add_rows(left, right):
    return (left.astype(jnp.float32) + right.astype(jnp.float32)).astype(jnp.bfloat16)


def scatter_rows(sums, n_req):
    own, other = sums[:4], sums[4:]
    line, first, second, both = [
        add_rows(mine, moved(theirs, n_req, (0, 0, 1, 0))) for mine, theirs in zip(own, other)
    ]
    first = add_rows(first, crossed(both, n_req, 1))
    line = add_rows(line, crossed(second, n_req, 1))
    line = add_rows(line, crossed(first, n_req, 0))
    outer = n_req // 4
    count = line.shape[0] // outer
    blocks = [line[k * count : (k + 1) * count] for k in range(outer)]
    return [blocks[0]] + [
        moved(block, n_req, (k, 0, 0, 0)) for k, block in enumerate(blocks) if k > 0
    ]


def gathered_body(
    n_req,
    queries,
    keys_values,
    segments,
    sink_logits,
    out_weight,
    out_bias,
    residual,
    norm_gain,
    route_ids,
    route_logits,
    gate_weight,
    gate_bias,
    up_weight,
    up_bias,
    down_weight,
    down_bias,
    page_table,
):
    tok_count, width = residual.shape
    side = lax.axis_index("tp")[None]
    expert = lax.axis_index("req")[None]
    own, other, page_pool, expert = run_attention(
        side, expert, page_table, sink_logits, queries, keys_values, segments, out_weight
    )
    got = moved(other, n_req, (0, 0, 0, 1))
    experts = down_bias.shape[0]
    base, rows = pl.pallas_call(
        mid_kernel,
        out_shape=[
            jax.ShapeDtypeStruct((tok_count, width), jnp.float32),
            jax.ShapeDtypeStruct((tok_count, width + 4 * experts), jnp.bfloat16),
        ],
        in_specs=[vmem()] * 8,
        out_specs=[vmem()] * 2,
        name="norm_rows",
    )(
        own,
        got,
        residual,
        out_bias[None],
        norm_gain[None],
        route_ids.T,
        route_logits.T,
        down_bias,
    )
    gate, up, sign = load([gate_weight[0].T, up_weight[0].T], 36 * 2**20)
    down, late_sign = load([down_weight[0]], 2 * 2**20)
    pieces, sign, late_sign = gather_rows(rows, n_req, sign, late_sign)
    sums = run_expert(
        expert,
        pieces,
        gate,
        gate_bias,
        up,
        up_bias,
        down,
        sign,
        late_sign,
        tok_count,
        slot_limit(tok_count, route_ids.shape[1], experts),
    )
    mixed = base
    for part in scatter_rows(sums, n_req):
        mixed = mixed + part.astype(jnp.float32)
    return (mixed.astype(jnp.bfloat16), page_pool)


def solution(mesh):
    in_specs = (
        P("req", "tp"),
        P("req", "tp"),
        P("req"),
        P("tp"),
        P("tp", None),
        P(),
        P(("req", "tp"), None),
        P(),
        P(("req", "tp"), None),
        P(("req", "tp"), None),
        P("req", None, "tp"),
        P("req", "tp"),
        P("req", None, "tp"),
        P("req", "tp"),
        P("req", "tp", None),
        P(),
        P("req", None),
    )
    out_specs = (P(("req", "tp"), None), P("req", None, "tp"))
    n_req, n_tp = mesh.shape["req"], mesh.shape["tp"]
    chosen = functools.partial(gathered_body, n_req) if (n_req, n_tp) == (16, 2) else body
    return jax.shard_map(chosen, mesh=mesh, in_specs=in_specs, out_specs=out_specs, check_vma=False)
```

```python
import functools

import jax
import jax.numpy as jnp
import numpy as np
from jax import lax
from jax.experimental import pallas as pl
from jax.experimental.pallas import tpu as pltpu
from jax.sharding import PartitionSpec as P

HEAD = 64
PAGE_LEN = 16
LANES = 128
DOWN_STEP = 512
VMEM_LIMIT = 60 * 2**20
LOAD_ROWS = 480


rope_base = 150000.0
norm_eps = 1e-05
swiglu_limit = 7.0
glu_alpha = 1.702


def seg_positions(segment_ids):
    length = segment_ids.shape[0]
    indices = jnp.arange(length, dtype=jnp.int32)
    change = jnp.concatenate([jnp.ones((1,), dtype=bool), segment_ids[1:] != segment_ids[:-1]])
    starts = lax.cummax(jnp.where(change, indices, 0), axis=0)
    return indices - starts


def rotate(values, positions):
    half_dim = values.shape[-1] // 2
    inverse = rope_base ** (-jnp.arange(half_dim, dtype=jnp.float32) / half_dim)
    angles = positions.astype(jnp.float32)[:, None] * inverse[None, :]
    cosine = jnp.cos(angles)[:, None, :]
    sine_col = jnp.sin(angles)[:, None, :]
    first_half = values[..., :half_dim]
    second_half = values[..., half_dim:]
    return jnp.concatenate(
        [
            first_half * cosine - second_half * sine_col,
            second_half * cosine + first_half * sine_col,
        ],
        axis=-1,
    )


def attend_group(queries, keys_values, segment_ids, sink_logits):
    length = queries.shape[0]
    kv_heads = keys_values.shape[1] // (2 * HEAD)
    q_heads = queries.shape[1] // HEAD
    group_size = q_heads // kv_heads
    positions = seg_positions(segment_ids)
    q_rot = rotate(queries.astype(jnp.float32).reshape(length, q_heads, HEAD), positions).astype(
        jnp.bfloat16
    )
    q_rot = q_rot.reshape(length, kv_heads, group_size, HEAD)
    key_part = keys_values.reshape(length, kv_heads, 2, HEAD)
    k_rot = rotate(key_part[:, :, 0].astype(jnp.float32), positions).astype(jnp.bfloat16)
    values = key_part[:, :, 1]
    scores = jnp.einsum(
        "qkgd,skd->kgqs", q_rot, k_rot, preferred_element_type=jnp.float32
    ) * HEAD ** (-0.5)
    indices = jnp.arange(length, dtype=jnp.int32)
    visible = (segment_ids[:, None] == segment_ids[None, :]) & (
        indices[None, :] <= indices[:, None]
    )
    scores = jnp.where(visible, scores, -jnp.inf)
    sink_col = sink_logits.reshape(kv_heads, group_size)[:, :, None]
    highest = jnp.maximum(jnp.max(scores, axis=-1), sink_col)
    expo_terms = jnp.exp(scores - highest[..., None])
    denominator = jnp.sum(expo_terms, axis=-1) + jnp.exp(sink_col - highest)
    probabilities = (expo_terms / denominator[..., None]).astype(jnp.bfloat16)
    attended = jnp.einsum(
        "kgqs,skd->qkgd", probabilities, values, preferred_element_type=jnp.float32
    )
    attended = attended.astype(jnp.bfloat16).reshape(length, q_heads * HEAD)
    cached = jnp.stack([k_rot, values], axis=2).reshape(length, kv_heads * 2 * HEAD)
    return (attended, cached)


def slot_index(routes, experts, capacity):
    blocks, row_count, route_width = routes.shape
    flat_ids = routes.reshape(blocks, row_count * route_width)
    onehot = (flat_ids[:, :, None] == jnp.arange(experts, dtype=jnp.int32)[None, None, :]).astype(
        jnp.int32
    )
    earlier = jnp.cumsum(onehot, axis=1) - onehot
    position = jnp.sum(earlier * onehot, axis=2)
    block_ids = jnp.arange(blocks, dtype=jnp.int32)[:, None]
    slot_ids = flat_ids * (blocks * capacity) + block_ids * capacity + position
    return slot_ids.reshape(blocks * row_count, route_width).astype(jnp.int32)


def dispatch(tokens, slot_ids, slot_total):
    row_count = tokens.shape[0]
    owners = jnp.broadcast_to(jnp.arange(row_count, dtype=jnp.int32)[:, None], slot_ids.shape)
    member = (
        jnp.full((slot_total,), row_count, jnp.int32)
        .at[slot_ids.reshape(-1)]
        .set(owners.reshape(-1))
    )
    padded = jnp.concatenate([tokens, jnp.zeros((1, tokens.shape[1]), tokens.dtype)], axis=0)
    return padded[member]


def slot_limit(tok_count, route_width, experts):
    return max(2, 2 * tok_count * route_width // experts)


def body(
    queries,
    keys_values,
    segments,
    sink_logits,
    out_weight,
    out_bias,
    residual,
    norm_gain,
    route_ids,
    route_logits,
    gate_weight,
    gate_bias,
    up_weight,
    up_bias,
    down_weight,
    down_bias,
    page_table,
):
    attended, cached = attend_group(queries, keys_values, segments, sink_logits)
    projected = lax.psum_scatter(
        jnp.dot(attended, out_weight, preferred_element_type=jnp.float32).astype(jnp.bfloat16),
        "tp",
        scatter_dimension=0,
        tiled=True,
    ).astype(jnp.float32)
    hidden = (residual.astype(jnp.float32) + projected + out_bias.astype(jnp.float32)).astype(
        jnp.bfloat16
    )
    stream = hidden.astype(jnp.float32)
    normed = (
        stream
        * lax.rsqrt(jnp.mean(stream * stream, axis=-1, keepdims=True) + norm_eps)
        * norm_gain.astype(jnp.float32)
    ).astype(jnp.bfloat16)
    route_weights = jax.nn.softmax(route_logits, axis=-1)
    tok_count, route_width = route_ids.shape
    experts = down_bias.shape[0]
    model_width = residual.shape[1]
    capacity = slot_limit(tok_count, route_width, experts)
    own_slots = slot_index(route_ids[None], experts, capacity)
    group_rows, group_routes = (
        lax.all_gather(normed, "tp", axis=0, tiled=True),
        lax.all_gather(route_ids, "tp", axis=0, tiled=True),
    )
    tp_count = group_rows.shape[0] // tok_count
    all_slots = slot_index(
        group_routes.reshape(tp_count, tok_count, route_width), experts, capacity
    )
    dispatched = dispatch(group_rows, all_slots, experts * tp_count * capacity).reshape(
        experts, tp_count, capacity, model_width
    )
    received = lax.all_to_all(dispatched, "req", split_axis=0, concat_axis=0, tiled=True)
    slot_shape = received.shape
    flat_rows = received.reshape(-1, model_width)
    gate_act = jnp.dot(flat_rows, gate_weight[0], preferred_element_type=jnp.float32) + gate_bias[
        0
    ].astype(jnp.float32)
    up_act = jnp.dot(flat_rows, up_weight[0], preferred_element_type=jnp.float32) + up_bias[
        0
    ].astype(jnp.float32)
    gate_act = jnp.minimum(gate_act, swiglu_limit)
    up_act = jnp.clip(up_act, -swiglu_limit, swiglu_limit)
    active = (gate_act * jax.nn.sigmoid(glu_alpha * gate_act) * (up_act + 1.0)).astype(jnp.bfloat16)
    partial_value = jnp.dot(active, down_weight[0], preferred_element_type=jnp.float32).reshape(
        slot_shape
    )
    summed = lax.psum_scatter(
        partial_value.astype(jnp.bfloat16), "tp", scatter_dimension=1, tiled=True
    ).astype(jnp.float32)
    returned = lax.all_to_all(
        summed.astype(jnp.bfloat16), "req", split_axis=0, concat_axis=0, tiled=True
    ).astype(summed.dtype)
    returned = returned.reshape(experts * capacity, model_width)
    slot_onehot = (
        own_slots[:, :, None] == jnp.arange(experts * capacity, dtype=jnp.int32)[None, None, :]
    ).astype(jnp.float32)
    combiner = jnp.einsum("rk,rks->rs", route_weights, slot_onehot, precision=lax.Precision.HIGHEST)
    expert_onehot = (
        route_ids[:, :, None] == jnp.arange(experts, dtype=jnp.int32)[None, None, :]
    ).astype(jnp.float32)
    dense_weights = jnp.einsum(
        "rk,rke->re", route_weights, expert_onehot, precision=lax.Precision.HIGHEST
    )
    expert_mix = jnp.dot(
        combiner, returned, precision=lax.Precision.HIGHEST, preferred_element_type=jnp.float32
    )
    expert_mix = expert_mix + jnp.dot(
        dense_weights,
        down_bias.astype(jnp.float32),
        precision=lax.Precision.HIGHEST,
        preferred_element_type=jnp.float32,
    )
    mixed_out = (stream + expert_mix).astype(jnp.bfloat16)
    blocks = cached.reshape(-1, PAGE_LEN, cached.shape[1])
    page_pool = jnp.zeros_like(blocks).at[page_table[0]].set(blocks)
    return (mixed_out, page_pool)


def mid_kernel(
    own_ref,
    got_ref,
    residual_ref,
    out_bias_ref,
    gain_ref,
    ids_ref,
    logits_ref,
    down_bias_ref,
    base_ref,
    rows_ref,
):
    width = residual_ref.shape[1]
    experts = down_bias_ref.shape[0]
    hidden = (
        residual_ref[...].astype(jnp.float32)
        + own_ref[...].astype(jnp.float32)
        + got_ref[...].astype(jnp.float32)
        + out_bias_ref[...].astype(jnp.float32)
    ).astype(jnp.bfloat16)
    stream = hidden.astype(jnp.float32)
    normed = (
        stream
        * lax.rsqrt(jnp.mean(stream * stream, axis=-1, keepdims=True) + norm_eps)
        * gain_ref[...].astype(jnp.float32)
    ).astype(jnp.bfloat16)
    logits = logits_ref[...]
    expo = jnp.exp(logits - jnp.max(logits, axis=0, keepdims=True))
    weights = expo / jnp.sum(expo, axis=0, keepdims=True)
    high = weights.astype(jnp.bfloat16).astype(jnp.float32)
    low = (weights - high).astype(jnp.bfloat16).astype(jnp.float32)
    ids = ids_ref[...]
    column = lax.broadcasted_iota(jnp.int32, (LANES, ids.shape[1]), 0)
    high_cols = jnp.zeros(column.shape, jnp.float32)
    low_cols = jnp.zeros(column.shape, jnp.float32)
    first = width % LANES
    for k in range(ids.shape[0]):
        at = ids[k : k + 1] + first
        high_cols = high_cols + jnp.where(column == at, high[k : k + 1], 0.0)
        low_cols = low_cols + jnp.where(column == at + experts, low[k : k + 1], 0.0)
    high_cols = high_cols.T
    low_cols = low_cols.T
    high_dense = high_cols[:, first : first + experts].astype(jnp.bfloat16)
    low_dense = low_cols[:, first + experts : first + 2 * experts].astype(jnp.bfloat16)
    bias = down_bias_ref[...]
    base_ref[...] = (
        stream
        + jnp.dot(high_dense, bias, preferred_element_type=jnp.float32)
        + jnp.dot(low_dense, bias, preferred_element_type=jnp.float32)
    )
    rows_ref[:, :width] = normed
    rows_ref[:, width:] = (high_cols + low_cols)[:, first:].astype(jnp.bfloat16)


def tiles(total, step):
    return [(start, min(step, total - start)) for start in range(0, total, step)]


def by_rows(left, right):
    return lax.dot_general(
        left, right, (((1,), (1,)), ((), ())), preferred_element_type=jnp.float32
    )


def load_kernel(source, target, sign, sems):
    copies = []
    for i, (start, size) in enumerate(tiles(source.shape[0], LOAD_ROWS)):
        here = pl.ds(start, size)
        copies.append(pltpu.make_async_copy(source.at[here], target.at[here], sems.at[i]))
    for copy in copies:
        copy.start()
    for copy in copies:
        copy.wait()
    sign[...] = target[: sign.shape[0], : sign.shape[1]]


def load(weight, reserve):
    return pl.pallas_call(
        load_kernel,
        out_shape=[
            jax.ShapeDtypeStruct(weight.shape, weight.dtype),
            jax.ShapeDtypeStruct((16, LANES), weight.dtype),
        ],
        in_specs=[anywhere()],
        out_specs=[vmem()] * 2,
        scratch_shapes=[pltpu.SemaphoreType.DMA((len(tiles(weight.shape[0], LOAD_ROWS)),))],
        compiler_params=pltpu.CompilerParams(vmem_limit_bytes=reserve),
        cost_estimate=pl.CostEstimate(
            flops=0, bytes_accessed=4 * weight.size, transcendentals=0
        ),
        name="load",
    )(weight)


def expert_kernel(parts, block, limit, step, expert_ref, *refs):
    pieces, refs = refs[:parts], refs[parts:]
    gate_w, up_w, down_w, gate_bias_ref, up_bias_ref = refs[:5]
    outs, (picked, active) = refs[8 : 8 + parts], refs[8 + parts :]
    piece, padded = pieces[0].shape
    total = parts * piece
    units, width = down_w.shape
    group = 2 * piece
    group_slots = group // block * limit
    up_bias = jnp.broadcast_to(up_bias_ref[...].astype(jnp.float32), (8, units)).T
    gate_bias = jnp.broadcast_to(gate_bias_ref[...].astype(jnp.float32), (8, units)).T

    expert = expert_ref[0]
    experts = (padded - width) // 4
    lane = lax.broadcasted_iota(jnp.int32, (16, LANES), 1)
    which = lax.broadcasted_iota(jnp.int32, (16, LANES), 0)
    choose = jnp.where(
        (lane == width % LANES + expert + which * experts) & (which < 2), 1.0, 0.0
    ).astype(jnp.bfloat16)
    found = by_rows(
        choose, jnp.concatenate([p[:, padded - LANES :] for p in pieces], axis=0)
    )
    share = jnp.broadcast_to(found[0:1] + found[1:2], (8, total))
    chosen = share > 0.0
    token = lax.broadcasted_iota(jnp.int32, (8, total), 1)
    count = jnp.where(chosen, 1, 0)
    reach = 1
    while reach < block:
        count = count + jnp.where(token % block >= reach, pltpu.roll(count, reach, 1), 0)
        reach *= 2
    slot = jnp.where(chosen, token // block * limit + count - 1, -1)
    spreads, shares = [], []
    for g in range(total // group):
        here = slice(g * group, (g + 1) * group)
        hit = (
            lax.broadcasted_iota(jnp.int32, (group_slots, group), 0) + g * group_slots
            == slot[0:1, here]
        )
        shares.append(jnp.sum(jnp.where(hit, share[0:1, here], 0.0), axis=1, keepdims=True))
        pick = jnp.where(hit, 1.0, 0.0)
        spreads.append(pick.T.astype(jnp.bfloat16))
        pick = pick.astype(jnp.bfloat16)
        for start, size in tiles(width, 2 * step):
            cols = slice(start, start + size)
            both = jnp.concatenate([pieces[2 * g][:, cols], pieces[2 * g + 1][:, cols]], axis=0)
            picked[g * group_slots : (g + 1) * group_slots, cols] = jnp.dot(
                pick, both, preferred_element_type=jnp.float32
            ).astype(jnp.bfloat16)
    slot_share = jnp.concatenate(shares, axis=0)

    def activate(start, size, gate, up):
        here = slice(start, start + size)
        gate = jnp.minimum(gate + gate_bias[here, 0:1], swiglu_limit)
        up = jnp.clip(up + up_bias[here, 0:1], -swiglu_limit, swiglu_limit)
        value = gate * (1.0 / (1.0 + jnp.exp(-glu_alpha * gate))) * (up + 1.0)
        active[:, here] = value.T.astype(jnp.bfloat16)

    def give(start, size, value):
        cols = slice(start, start + size)
        scaled = (value * slot_share).astype(jnp.bfloat16)
        for g, spread in enumerate(spreads):
            sums = jnp.dot(
                spread,
                scaled[g * group_slots : (g + 1) * group_slots],
                preferred_element_type=jnp.float32,
            ).astype(jnp.bfloat16)
            outs[2 * g][:, cols] = sums[:piece]
            outs[2 * g + 1][:, cols] = sums[piece:]

    last = None
    for start, size in tiles(units, step):
        here = slice(start, start + size)
        gate = by_rows(gate_w[here], picked[...])
        up = by_rows(up_w[here], picked[...])
        if last is not None:
            activate(*last)
        last = (start, size, gate, up)
    activate(*last)
    last = None
    for start, size in tiles(width, DOWN_STEP):
        cols = slice(start, start + size)
        value = jnp.dot(active[...], down_w[:, cols], preferred_element_type=jnp.float32)
        if last is not None:
            give(*last)
        last = (start, size, value)
    give(*last)


def attention_kernel(
    side_ref,
    expert_in_ref,
    pages_ref,
    sink_ref,
    queries_ref,
    keys_values_ref,
    segments_ref,
    inverse_ref,
    weight_hbm,
    own_ref,
    other_ref,
    cache_ref,
    expert_ref,
    weight,
    attended,
    sems,
):
    expert_ref[0] = expert_in_ref[0]
    length, query_width = queries_ref.shape
    width = weight.shape[0]
    kv_heads = keys_values_ref.shape[1] // LANES
    group_tiles = query_width // LANES // kv_heads
    chunks = tiles(width, 512)
    copies = [
        pltpu.make_async_copy(
            weight_hbm.at[pl.ds(start, size)], weight.at[pl.ds(start, size)], sems.at[i]
        )
        for i, (start, size) in enumerate(chunks)
    ]
    for copy in copies[:2]:
        copy.start()
    named = jnp.broadcast_to(segments_ref[...].astype(jnp.float32), (length, length))
    visible = (named == named.T) & (
        lax.broadcasted_iota(jnp.int32, (length, length), 1)
        <= lax.broadcasted_iota(jnp.int32, (length, length), 0)
    )
    positions = jnp.sum(jnp.where(visible, 1.0, 0.0), axis=1, keepdims=True) - 1.0
    angles = positions * inverse_ref[...]
    lane = lax.broadcasted_iota(jnp.int32, (length, LANES), 1)
    lower = lane % HEAD < HEAD // 2
    cosine = jnp.cos(angles)
    sine = jnp.sin(angles)
    sine = jnp.where(lower, -sine, sine)
    left = lane < HEAD

    def turned(tile):
        swapped = jnp.where(
            lower, pltpu.roll(tile, LANES - HEAD // 2, 1), pltpu.roll(tile, HEAD // 2, 1)
        )
        return tile * cosine + swapped * sine

    seen = jnp.concatenate([visible] * (2 * group_tiles), axis=0)
    for k in range(kv_heads):
        raw = keys_values_ref[:, k * LANES : (k + 1) * LANES].astype(jnp.float32)
        pair = jnp.where(left, turned(raw), raw).astype(jnp.bfloat16)
        for b in range(cache_ref.shape[0]):
            cache_ref[pages_ref[0, b], :, k * LANES : (k + 1) * LANES] = pair[
                b * PAGE_LEN : (b + 1) * PAGE_LEN
            ]
        heads = []
        sinks = []
        for t in range(k * group_tiles, (k + 1) * group_tiles):
            tile = turned(queries_ref[:, t * LANES : (t + 1) * LANES].astype(jnp.float32))
            heads.append(jnp.where(left, tile, 0.0))
            heads.append(jnp.where(left, pltpu.roll(tile, HEAD, 1), 0.0))
            sinks.append(jnp.full((length, 1), sink_ref[2 * t], jnp.float32))
            sinks.append(jnp.full((length, 1), sink_ref[2 * t + 1], jnp.float32))
        sink = jnp.concatenate(sinks, axis=0)
        scores = lax.dot_general(
            jnp.concatenate(heads, axis=0).astype(jnp.bfloat16),
            pair,
            (((1,), (1,)), ((), ())),
            preferred_element_type=jnp.float32,
        ) * HEAD ** (-0.5)
        scores = jnp.where(seen, scores, -1e30)
        highest = jnp.maximum(jnp.max(scores, axis=-1, keepdims=True), sink)
        expo = jnp.where(seen, jnp.exp(scores - highest), 0.0)
        denominator = jnp.sum(expo, axis=-1, keepdims=True) + jnp.exp(sink - highest)
        probabilities = (expo / denominator).astype(jnp.bfloat16)
        mixed = jnp.dot(probabilities, pair, preferred_element_type=jnp.float32)
        for t in range(group_tiles):
            even = mixed[2 * t * length : (2 * t + 1) * length]
            odd = mixed[(2 * t + 1) * length : (2 * t + 2) * length]
            start = (k * group_tiles + t) * LANES
            attended[:, start : start + LANES] = jnp.where(
                left, pltpu.roll(even, HEAD, 1), odd
            ).astype(jnp.bfloat16)
    first_side = side_ref[0] == 0
    half = own_ref.shape[0]
    for i, (start, size) in enumerate(chunks):
        copies[i].wait()
        if i + 2 < len(copies):
            copies[i + 2].start()
        projected = by_rows(attended[...], weight[start : start + size])
        top, bottom = projected[:half], projected[half:]
        own_ref[:, start : start + size] = jnp.where(first_side, top, bottom)
        other_ref[:, start : start + size] = jnp.where(first_side, bottom, top).astype(jnp.bfloat16)


def run_attention(side, expert, page_table, sink_logits, queries, keys_values, segments, out_weight):
    length, query_width = queries.shape
    width = out_weight.shape[1]
    half = length // 2
    inverse = np.float32(rope_base) ** (
        -(np.arange(LANES) % (HEAD // 2)).astype(np.float32) / np.float32(HEAD // 2)
    )
    smem = pl.BlockSpec(memory_space=pltpu.SMEM)
    return pl.pallas_call(
        attention_kernel,
        out_shape=[
            jax.ShapeDtypeStruct((half, width), jnp.float32),
            jax.ShapeDtypeStruct((half, width), jnp.bfloat16),
            jax.ShapeDtypeStruct(
                (length // PAGE_LEN, PAGE_LEN, keys_values.shape[1]), jnp.bfloat16
            ),
            jax.ShapeDtypeStruct((1,), jnp.int32),
        ],
        in_specs=[smem] * 4 + [vmem()] * 4 + [anywhere()],
        out_specs=[vmem()] * 3 + [smem],
        scratch_shapes=[
            pltpu.VMEM((width, query_width), jnp.bfloat16),
            pltpu.VMEM((length, query_width), jnp.bfloat16),
            pltpu.SemaphoreType.DMA((len(tiles(width, 512)),)),
        ],
        compiler_params=pltpu.CompilerParams(vmem_limit_bytes=VMEM_LIMIT),
        name="attention",
    )(
        side,
        expert,
        page_table,
        sink_logits,
        queries,
        keys_values,
        segments[None],
        jnp.asarray(inverse.astype(np.float32))[None],
        out_weight.T,
    )


def vmem():
    return pl.BlockSpec(memory_space=pltpu.VMEM)


def anywhere():
    return pl.BlockSpec(memory_space=pl.ANY)


def run_expert(
    expert, pieces, gate_rows, gate_bias, up_rows, up_bias, down_weight, signs, block, limit
):
    parts = len(pieces)
    piece, padded = pieces[0].shape
    hidden_units, width = down_weight.shape
    slots = parts * piece // block * limit
    return pl.pallas_call(
        functools.partial(expert_kernel, parts, block, limit, 512),
        out_shape=[jax.ShapeDtypeStruct((piece, width), jnp.bfloat16)] * parts,
        in_specs=[pl.BlockSpec(memory_space=pltpu.SMEM)] + [vmem()] * (parts + 5)
        + [anywhere()] * 3,
        out_specs=[vmem()] * parts,
        scratch_shapes=[
            pltpu.VMEM((slots, width), jnp.bfloat16),
            pltpu.VMEM((slots, hidden_units), jnp.bfloat16),
        ],
        compiler_params=pltpu.CompilerParams(vmem_limit_bytes=8 * 2**20),
        cost_estimate=pl.CostEstimate(
            flops=6 * slots * width * hidden_units,
            bytes_accessed=6 * width * hidden_units,
            transcendentals=slots * hidden_units,
        ),
        name="expert",
    )(expert, *pieces, gate_rows, up_rows, down_weight, gate_bias, up_bias, *signs)


AXES = ("req", "tp")


def moved(array, n_req, step):
    outer, mid, core, tp = step
    pairs = []
    for source in range(2 * n_req):
        req, side = divmod(source, 2)
        place = (req // 4 ^ outer) * 4 + (req // 2 % 2 ^ mid) * 2 + (req % 2 ^ core)
        pairs.append((source, place * 2 + (side ^ tp)))
    return lax.ppermute(array, AXES, pairs)


def crossed(array, n_req, by_core):
    pairs = []
    for source in range(2 * n_req):
        req, side = divmod(source, 2)
        if req % 2 == by_core:
            pairs.append((source, (req ^ 2) * 2 + side))
        else:
            pairs.append((source, req * 2 + (side ^ 1)))
    return lax.ppermute(array, AXES, pairs)


def gather_rows(rows, n_req, signs):
    signs = list(signs)
    outer = n_req // 4
    others = [moved(rows, n_req, (k, 0, 0, 0)) for k in range(1, outer)]
    line = jnp.concatenate([rows] + others)
    first = crossed(line, n_req, 0)
    second = crossed(line, n_req, 1)
    sent, signs[0], signs[1] = lax.optimization_barrier((first, signs[0], signs[1]))
    both = crossed(sent, n_req, 1)
    own = [line, first, second, both]
    sent, signs[2] = lax.optimization_barrier((both, signs[2]))
    pieces = own + [moved(piece, n_req, (0, 0, 1, 0)) for piece in (line, first, second, sent)]
    return pieces, signs


def add_rows(left, right):
    return (left.astype(jnp.float32) + right.astype(jnp.float32)).astype(jnp.bfloat16)


def scatter_rows(sums, n_req):
    own, other = sums[:4], sums[4:]
    line, first, second, both = [
        add_rows(mine, moved(theirs, n_req, (0, 0, 1, 0))) for mine, theirs in zip(own, other)
    ]
    first = add_rows(first, crossed(both, n_req, 1))
    line = add_rows(line, crossed(second, n_req, 1))
    line = add_rows(line, crossed(first, n_req, 0))
    outer = n_req // 4
    count = line.shape[0] // outer
    blocks = [line[k * count : (k + 1) * count] for k in range(outer)]
    return [blocks[0]] + [
        moved(block, n_req, (k, 0, 0, 0)) for k, block in enumerate(blocks) if k > 0
    ]


def gathered_body(
    n_req,
    queries,
    keys_values,
    segments,
    sink_logits,
    out_weight,
    out_bias,
    residual,
    norm_gain,
    route_ids,
    route_logits,
    gate_weight,
    gate_bias,
    up_weight,
    up_bias,
    down_weight,
    down_bias,
    page_table,
):
    tok_count, width = residual.shape
    side = lax.axis_index("tp")[None]
    expert = lax.axis_index("req")[None]
    own, other, page_pool, expert = run_attention(
        side, expert, page_table, sink_logits, queries, keys_values, segments, out_weight
    )
    got = moved(other, n_req, (0, 0, 0, 1))
    experts = down_bias.shape[0]
    base, rows = pl.pallas_call(
        mid_kernel,
        out_shape=[
            jax.ShapeDtypeStruct((tok_count, width), jnp.float32),
            jax.ShapeDtypeStruct((tok_count, width + 4 * experts), jnp.bfloat16),
        ],
        in_specs=[vmem()] * 8,
        out_specs=[vmem()] * 2,
        compiler_params=pltpu.CompilerParams(vmem_limit_bytes=4 * 2**20),
        name="norm_rows",
    )(
        own,
        got,
        residual,
        out_bias[None],
        norm_gain[None],
        route_ids.T,
        route_logits.T,
        down_bias,
    )
    signs = [None] * 3
    gate, signs[0] = load(gate_weight[0].T, 40 * 2**20)
    up, signs[1] = load(up_weight[0].T, 2 * 2**20)
    down, signs[2] = load(down_weight[0], 2 * 2**20)
    pieces, signs = gather_rows(rows, n_req, signs)
    sums = run_expert(
        expert,
        pieces,
        gate,
        gate_bias,
        up,
        up_bias,
        down,
        signs,
        tok_count,
        slot_limit(tok_count, route_ids.shape[1], experts),
    )
    mixed = base
    for part in scatter_rows(sums, n_req):
        mixed = mixed + part.astype(jnp.float32)
    return (mixed.astype(jnp.bfloat16), page_pool)


def solution(mesh):
    in_specs = (
        P("req", "tp"),
        P("req", "tp"),
        P("req"),
        P("tp"),
        P("tp", None),
        P(),
        P(("req", "tp"), None),
        P(),
        P(("req", "tp"), None),
        P(("req", "tp"), None),
        P("req", None, "tp"),
        P("req", "tp"),
        P("req", None, "tp"),
        P("req", "tp"),
        P("req", "tp", None),
        P(),
        P("req", None),
    )
    out_specs = (P(("req", "tp"), None), P("req", None, "tp"))
    n_req, n_tp = mesh.shape["req"], mesh.shape["tp"]
    chosen = functools.partial(gathered_body, n_req) if (n_req, n_tp) == (16, 2) else body
    return jax.shard_map(chosen, mesh=mesh, in_specs=in_specs, out_specs=out_specs, check_vma=False)
```

```python
import functools

import jax
import jax.numpy as jnp
import numpy as np
from jax import lax
from jax.experimental import pallas as pl
from jax.experimental.pallas import tpu as pltpu
from jax.sharding import PartitionSpec as P

HEAD = 64
PAGE_LEN = 16
LANES = 128
DOWN_STEP = 512
VMEM_LIMIT = 60 * 2**20
LOAD_ROWS = 480


rope_base = 150000.0
norm_eps = 1e-05
swiglu_limit = 7.0
glu_alpha = 1.702


def seg_positions(segment_ids):
    length = segment_ids.shape[0]
    indices = jnp.arange(length, dtype=jnp.int32)
    change = jnp.concatenate([jnp.ones((1,), dtype=bool), segment_ids[1:] != segment_ids[:-1]])
    starts = lax.cummax(jnp.where(change, indices, 0), axis=0)
    return indices - starts


def rotate(values, positions):
    half_dim = values.shape[-1] // 2
    inverse = rope_base ** (-jnp.arange(half_dim, dtype=jnp.float32) / half_dim)
    angles = positions.astype(jnp.float32)[:, None] * inverse[None, :]
    cosine = jnp.cos(angles)[:, None, :]
    sine_col = jnp.sin(angles)[:, None, :]
    first_half = values[..., :half_dim]
    second_half = values[..., half_dim:]
    return jnp.concatenate(
        [
            first_half * cosine - second_half * sine_col,
            second_half * cosine + first_half * sine_col,
        ],
        axis=-1,
    )


def attend_group(queries, keys_values, segment_ids, sink_logits):
    length = queries.shape[0]
    kv_heads = keys_values.shape[1] // (2 * HEAD)
    q_heads = queries.shape[1] // HEAD
    group_size = q_heads // kv_heads
    positions = seg_positions(segment_ids)
    q_rot = rotate(queries.astype(jnp.float32).reshape(length, q_heads, HEAD), positions).astype(
        jnp.bfloat16
    )
    q_rot = q_rot.reshape(length, kv_heads, group_size, HEAD)
    key_part = keys_values.reshape(length, kv_heads, 2, HEAD)
    k_rot = rotate(key_part[:, :, 0].astype(jnp.float32), positions).astype(jnp.bfloat16)
    values = key_part[:, :, 1]
    scores = jnp.einsum(
        "qkgd,skd->kgqs", q_rot, k_rot, preferred_element_type=jnp.float32
    ) * HEAD ** (-0.5)
    indices = jnp.arange(length, dtype=jnp.int32)
    visible = (segment_ids[:, None] == segment_ids[None, :]) & (
        indices[None, :] <= indices[:, None]
    )
    scores = jnp.where(visible, scores, -jnp.inf)
    sink_col = sink_logits.reshape(kv_heads, group_size)[:, :, None]
    highest = jnp.maximum(jnp.max(scores, axis=-1), sink_col)
    expo_terms = jnp.exp(scores - highest[..., None])
    denominator = jnp.sum(expo_terms, axis=-1) + jnp.exp(sink_col - highest)
    probabilities = (expo_terms / denominator[..., None]).astype(jnp.bfloat16)
    attended = jnp.einsum(
        "kgqs,skd->qkgd", probabilities, values, preferred_element_type=jnp.float32
    )
    attended = attended.astype(jnp.bfloat16).reshape(length, q_heads * HEAD)
    cached = jnp.stack([k_rot, values], axis=2).reshape(length, kv_heads * 2 * HEAD)
    return (attended, cached)


def slot_index(routes, experts, capacity):
    blocks, row_count, route_width = routes.shape
    flat_ids = routes.reshape(blocks, row_count * route_width)
    onehot = (flat_ids[:, :, None] == jnp.arange(experts, dtype=jnp.int32)[None, None, :]).astype(
        jnp.int32
    )
    earlier = jnp.cumsum(onehot, axis=1) - onehot
    position = jnp.sum(earlier * onehot, axis=2)
    block_ids = jnp.arange(blocks, dtype=jnp.int32)[:, None]
    slot_ids = flat_ids * (blocks * capacity) + block_ids * capacity + position
    return slot_ids.reshape(blocks * row_count, route_width).astype(jnp.int32)


def dispatch(tokens, slot_ids, slot_total):
    row_count = tokens.shape[0]
    owners = jnp.broadcast_to(jnp.arange(row_count, dtype=jnp.int32)[:, None], slot_ids.shape)
    member = (
        jnp.full((slot_total,), row_count, jnp.int32)
        .at[slot_ids.reshape(-1)]
        .set(owners.reshape(-1))
    )
    padded = jnp.concatenate([tokens, jnp.zeros((1, tokens.shape[1]), tokens.dtype)], axis=0)
    return padded[member]


def slot_limit(tok_count, route_width, experts):
    return max(2, 2 * tok_count * route_width // experts)


def body(
    queries,
    keys_values,
    segments,
    sink_logits,
    out_weight,
    out_bias,
    residual,
    norm_gain,
    route_ids,
    route_logits,
    gate_weight,
    gate_bias,
    up_weight,
    up_bias,
    down_weight,
    down_bias,
    page_table,
):
    attended, cached = attend_group(queries, keys_values, segments, sink_logits)
    projected = lax.psum_scatter(
        jnp.dot(attended, out_weight, preferred_element_type=jnp.float32).astype(jnp.bfloat16),
        "tp",
        scatter_dimension=0,
        tiled=True,
    ).astype(jnp.float32)
    hidden = (residual.astype(jnp.float32) + projected + out_bias.astype(jnp.float32)).astype(
        jnp.bfloat16
    )
    stream = hidden.astype(jnp.float32)
    normed = (
        stream
        * lax.rsqrt(jnp.mean(stream * stream, axis=-1, keepdims=True) + norm_eps)
        * norm_gain.astype(jnp.float32)
    ).astype(jnp.bfloat16)
    route_weights = jax.nn.softmax(route_logits, axis=-1)
    tok_count, route_width = route_ids.shape
    experts = down_bias.shape[0]
    model_width = residual.shape[1]
    capacity = slot_limit(tok_count, route_width, experts)
    own_slots = slot_index(route_ids[None], experts, capacity)
    group_rows, group_routes = (
        lax.all_gather(normed, "tp", axis=0, tiled=True),
        lax.all_gather(route_ids, "tp", axis=0, tiled=True),
    )
    tp_count = group_rows.shape[0] // tok_count
    all_slots = slot_index(
        group_routes.reshape(tp_count, tok_count, route_width), experts, capacity
    )
    dispatched = dispatch(group_rows, all_slots, experts * tp_count * capacity).reshape(
        experts, tp_count, capacity, model_width
    )
    received = lax.all_to_all(dispatched, "req", split_axis=0, concat_axis=0, tiled=True)
    slot_shape = received.shape
    flat_rows = received.reshape(-1, model_width)
    gate_act = jnp.dot(flat_rows, gate_weight[0], preferred_element_type=jnp.float32) + gate_bias[
        0
    ].astype(jnp.float32)
    up_act = jnp.dot(flat_rows, up_weight[0], preferred_element_type=jnp.float32) + up_bias[
        0
    ].astype(jnp.float32)
    gate_act = jnp.minimum(gate_act, swiglu_limit)
    up_act = jnp.clip(up_act, -swiglu_limit, swiglu_limit)
    active = (gate_act * jax.nn.sigmoid(glu_alpha * gate_act) * (up_act + 1.0)).astype(jnp.bfloat16)
    partial_value = jnp.dot(active, down_weight[0], preferred_element_type=jnp.float32).reshape(
        slot_shape
    )
    summed = lax.psum_scatter(
        partial_value.astype(jnp.bfloat16), "tp", scatter_dimension=1, tiled=True
    ).astype(jnp.float32)
    returned = lax.all_to_all(
        summed.astype(jnp.bfloat16), "req", split_axis=0, concat_axis=0, tiled=True
    ).astype(summed.dtype)
    returned = returned.reshape(experts * capacity, model_width)
    slot_onehot = (
        own_slots[:, :, None] == jnp.arange(experts * capacity, dtype=jnp.int32)[None, None, :]
    ).astype(jnp.float32)
    combiner = jnp.einsum("rk,rks->rs", route_weights, slot_onehot, precision=lax.Precision.HIGHEST)
    expert_onehot = (
        route_ids[:, :, None] == jnp.arange(experts, dtype=jnp.int32)[None, None, :]
    ).astype(jnp.float32)
    dense_weights = jnp.einsum(
        "rk,rke->re", route_weights, expert_onehot, precision=lax.Precision.HIGHEST
    )
    expert_mix = jnp.dot(
        combiner, returned, precision=lax.Precision.HIGHEST, preferred_element_type=jnp.float32
    )
    expert_mix = expert_mix + jnp.dot(
        dense_weights,
        down_bias.astype(jnp.float32),
        precision=lax.Precision.HIGHEST,
        preferred_element_type=jnp.float32,
    )
    mixed_out = (stream + expert_mix).astype(jnp.bfloat16)
    blocks = cached.reshape(-1, PAGE_LEN, cached.shape[1])
    page_pool = jnp.zeros_like(blocks).at[page_table[0]].set(blocks)
    return (mixed_out, page_pool)


def mid_kernel(
    own_ref,
    got_ref,
    residual_ref,
    out_bias_ref,
    gain_ref,
    ids_ref,
    logits_ref,
    down_bias_ref,
    base_ref,
    rows_ref,
):
    width = residual_ref.shape[1]
    experts = down_bias_ref.shape[0]
    hidden = (
        residual_ref[...].astype(jnp.float32)
        + own_ref[...].astype(jnp.float32)
        + got_ref[...].astype(jnp.float32)
        + out_bias_ref[...].astype(jnp.float32)
    ).astype(jnp.bfloat16)
    stream = hidden.astype(jnp.float32)
    normed = (
        stream
        * lax.rsqrt(jnp.mean(stream * stream, axis=-1, keepdims=True) + norm_eps)
        * gain_ref[...].astype(jnp.float32)
    ).astype(jnp.bfloat16)
    logits = logits_ref[...]
    expo = jnp.exp(logits - jnp.max(logits, axis=0, keepdims=True))
    weights = expo / jnp.sum(expo, axis=0, keepdims=True)
    high = weights.astype(jnp.bfloat16).astype(jnp.float32)
    low = (weights - high).astype(jnp.bfloat16).astype(jnp.float32)
    ids = ids_ref[...]
    column = lax.broadcasted_iota(jnp.int32, (LANES, ids.shape[1]), 0)
    high_cols = jnp.zeros(column.shape, jnp.float32)
    low_cols = jnp.zeros(column.shape, jnp.float32)
    first = width % LANES
    for k in range(ids.shape[0]):
        at = ids[k : k + 1] + first
        high_cols = high_cols + jnp.where(column == at, high[k : k + 1], 0.0)
        low_cols = low_cols + jnp.where(column == at + experts, low[k : k + 1], 0.0)
    high_cols = high_cols.T
    low_cols = low_cols.T
    high_dense = high_cols[:, first : first + experts].astype(jnp.bfloat16)
    low_dense = low_cols[:, first + experts : first + 2 * experts].astype(jnp.bfloat16)
    bias = down_bias_ref[...]
    base_ref[...] = (
        stream
        + jnp.dot(high_dense, bias, preferred_element_type=jnp.float32)
        + jnp.dot(low_dense, bias, preferred_element_type=jnp.float32)
    )
    rows_ref[:, :width] = normed
    rows_ref[:, width:] = (high_cols + low_cols)[:, first:].astype(jnp.bfloat16)


def tiles(total, step):
    return [(start, min(step, total - start)) for start in range(0, total, step)]


def by_rows(left, right):
    return lax.dot_general(
        left, right, (((1,), (1,)), ((), ())), preferred_element_type=jnp.float32
    )


def load_kernel(after_ref, source, target, sign, sems):
    copies = []
    for i, (start, size) in enumerate(tiles(source.shape[0], LOAD_ROWS)):
        here = pl.ds(start, size)
        copies.append(pltpu.make_async_copy(source.at[here], target.at[here], sems.at[i]))
    for copy in copies:
        copy.start()
    for copy in copies:
        copy.wait()
    sign[...] = target[: sign.shape[0], : sign.shape[1]]


def load(weight, after, reserve):
    return pl.pallas_call(
        load_kernel,
        out_shape=[
            jax.ShapeDtypeStruct(weight.shape, weight.dtype),
            jax.ShapeDtypeStruct((16, LANES), weight.dtype),
        ],
        in_specs=[anywhere()] * 2,
        out_specs=[vmem()] * 2,
        scratch_shapes=[pltpu.SemaphoreType.DMA((len(tiles(weight.shape[0], LOAD_ROWS)),))],
        compiler_params=pltpu.CompilerParams(vmem_limit_bytes=reserve),
        cost_estimate=pl.CostEstimate(
            flops=0, bytes_accessed=4 * weight.size, transcendentals=0
        ),
        name="load",
    )(after, weight)


def expert_kernel(parts, block, limit, step, expert_ref, *refs):
    pieces, refs = refs[:parts], refs[parts:]
    gate_w, up_w, down_w, gate_bias_ref, up_bias_ref = refs[:5]
    outs, (picked, active) = refs[8 : 8 + parts], refs[8 + parts :]
    piece, padded = pieces[0].shape
    total = parts * piece
    units, width = down_w.shape
    group = 2 * piece
    group_slots = group // block * limit
    up_bias = jnp.broadcast_to(up_bias_ref[...].astype(jnp.float32), (8, units)).T
    gate_bias = jnp.broadcast_to(gate_bias_ref[...].astype(jnp.float32), (8, units)).T

    expert = expert_ref[0]
    experts = (padded - width) // 4
    lane = lax.broadcasted_iota(jnp.int32, (16, LANES), 1)
    which = lax.broadcasted_iota(jnp.int32, (16, LANES), 0)
    choose = jnp.where(
        (lane == width % LANES + expert + which * experts) & (which < 2), 1.0, 0.0
    ).astype(jnp.bfloat16)
    found = by_rows(
        choose, jnp.concatenate([p[:, padded - LANES :] for p in pieces], axis=0)
    )
    share = jnp.broadcast_to(found[0:1] + found[1:2], (8, total))
    chosen = share > 0.0
    token = lax.broadcasted_iota(jnp.int32, (8, total), 1)
    count = jnp.where(chosen, 1, 0)
    reach = 1
    while reach < block:
        count = count + jnp.where(token % block >= reach, pltpu.roll(count, reach, 1), 0)
        reach *= 2
    slot = jnp.where(chosen, token // block * limit + count - 1, -1)
    spreads, shares = [], []
    for g in range(total // group):
        here = slice(g * group, (g + 1) * group)
        hit = (
            lax.broadcasted_iota(jnp.int32, (group_slots, group), 0) + g * group_slots
            == slot[0:1, here]
        )
        shares.append(jnp.sum(jnp.where(hit, share[0:1, here], 0.0), axis=1, keepdims=True))
        pick = jnp.where(hit, 1.0, 0.0)
        spreads.append(pick.T.astype(jnp.bfloat16))
        pick = pick.astype(jnp.bfloat16)
        for start, size in tiles(width, 2 * step):
            cols = slice(start, start + size)
            both = jnp.concatenate([pieces[2 * g][:, cols], pieces[2 * g + 1][:, cols]], axis=0)
            picked[g * group_slots : (g + 1) * group_slots, cols] = jnp.dot(
                pick, both, preferred_element_type=jnp.float32
            ).astype(jnp.bfloat16)
    slot_share = jnp.concatenate(shares, axis=0)

    def activate(start, size, gate, up):
        here = slice(start, start + size)
        gate = jnp.minimum(gate + gate_bias[here, 0:1], swiglu_limit)
        up = jnp.clip(up + up_bias[here, 0:1], -swiglu_limit, swiglu_limit)
        value = gate * (1.0 / (1.0 + jnp.exp(-glu_alpha * gate))) * (up + 1.0)
        active[:, here] = value.T.astype(jnp.bfloat16)

    def give(start, size, value):
        cols = slice(start, start + size)
        scaled = (value * slot_share).astype(jnp.bfloat16)
        for g, spread in enumerate(spreads):
            sums = jnp.dot(
                spread,
                scaled[g * group_slots : (g + 1) * group_slots],
                preferred_element_type=jnp.float32,
            ).astype(jnp.bfloat16)
            outs[2 * g][:, cols] = sums[:piece]
            outs[2 * g + 1][:, cols] = sums[piece:]

    last = None
    for start, size in tiles(units, step):
        here = slice(start, start + size)
        gate = by_rows(gate_w[here], picked[...])
        up = by_rows(up_w[here], picked[...])
        if last is not None:
            activate(*last)
        last = (start, size, gate, up)
    activate(*last)
    last = None
    for start, size in tiles(width, DOWN_STEP):
        cols = slice(start, start + size)
        value = jnp.dot(active[...], down_w[:, cols], preferred_element_type=jnp.float32)
        if last is not None:
            give(*last)
        last = (start, size, value)
    give(*last)


def attention_kernel(
    side_ref,
    expert_in_ref,
    pages_ref,
    sink_ref,
    queries_ref,
    keys_values_ref,
    segments_ref,
    inverse_ref,
    weight_hbm,
    own_ref,
    other_ref,
    cache_ref,
    expert_ref,
    weight,
    attended,
    sems,
):
    expert_ref[0] = expert_in_ref[0]
    length, query_width = queries_ref.shape
    width = weight.shape[0]
    kv_heads = keys_values_ref.shape[1] // LANES
    group_tiles = query_width // LANES // kv_heads
    chunks = tiles(width, 512)
    copies = [
        pltpu.make_async_copy(
            weight_hbm.at[pl.ds(start, size)], weight.at[pl.ds(start, size)], sems.at[i]
        )
        for i, (start, size) in enumerate(chunks)
    ]
    for copy in copies:
        copy.start()
    named = jnp.broadcast_to(segments_ref[...].astype(jnp.float32), (length, length))
    visible = (named == named.T) & (
        lax.broadcasted_iota(jnp.int32, (length, length), 1)
        <= lax.broadcasted_iota(jnp.int32, (length, length), 0)
    )
    positions = jnp.sum(jnp.where(visible, 1.0, 0.0), axis=1, keepdims=True) - 1.0
    angles = positions * inverse_ref[...]
    lane = lax.broadcasted_iota(jnp.int32, (length, LANES), 1)
    lower = lane % HEAD < HEAD // 2
    cosine = jnp.cos(angles)
    sine = jnp.sin(angles)
    sine = jnp.where(lower, -sine, sine)
    left = lane < HEAD

    def turned(tile):
        swapped = jnp.where(
            lower, pltpu.roll(tile, LANES - HEAD // 2, 1), pltpu.roll(tile, HEAD // 2, 1)
        )
        return tile * cosine + swapped * sine

    group_heads = 2 * group_tiles
    token = lax.broadcasted_iota(jnp.int32, (length, group_heads * length), 1)
    repeat = token % length == lax.broadcasted_iota(jnp.int32, token.shape, 0)
    seen = (
        jnp.dot(
            jnp.where(visible, 1.0, 0.0).T.astype(jnp.bfloat16),
            jnp.where(repeat, 1.0, 0.0).astype(jnp.bfloat16),
            preferred_element_type=jnp.float32,
        )
        > 0.5
    )
    head_of = lax.broadcasted_iota(jnp.int32, (1, group_heads * length), 1) // length
    for k in range(kv_heads):
        raw = keys_values_ref[:, k * LANES : (k + 1) * LANES].astype(jnp.float32)
        pair = jnp.where(left, turned(raw), raw).astype(jnp.bfloat16)
        for b in range(cache_ref.shape[0]):
            cache_ref[pages_ref[0, b], :, k * LANES : (k + 1) * LANES] = pair[
                b * PAGE_LEN : (b + 1) * PAGE_LEN
            ]
        heads = []
        sink = jnp.zeros(head_of.shape, jnp.float32)
        for h in range(group_heads):
            sink = jnp.where(head_of == h, sink_ref[k * group_heads + h], sink)
        for t in range(k * group_tiles, (k + 1) * group_tiles):
            tile = turned(queries_ref[:, t * LANES : (t + 1) * LANES].astype(jnp.float32))
            heads.append(jnp.where(left, tile, 0.0))
            heads.append(jnp.where(left, pltpu.roll(tile, HEAD, 1), 0.0))
        scores = by_rows(
            pair, jnp.concatenate(heads, axis=0).astype(jnp.bfloat16)
        ) * HEAD ** (-0.5)
        scores = jnp.where(seen, scores, -1e30)
        highest = jnp.maximum(jnp.max(scores, axis=0, keepdims=True), sink)
        expo = jnp.where(seen, jnp.exp(scores - highest), 0.0)
        denominator = jnp.sum(expo, axis=0, keepdims=True) + jnp.exp(sink - highest)
        probabilities = (expo / denominator).T.astype(jnp.bfloat16)
        mixed = jnp.dot(probabilities, pair, preferred_element_type=jnp.float32)
        for t in range(group_tiles):
            even = mixed[2 * t * length : (2 * t + 1) * length]
            odd = mixed[(2 * t + 1) * length : (2 * t + 2) * length]
            start = (k * group_tiles + t) * LANES
            attended[:, start : start + LANES] = jnp.where(
                left, pltpu.roll(even, HEAD, 1), odd
            ).astype(jnp.bfloat16)
    first_side = side_ref[0] == 0
    half = own_ref.shape[0]
    for i, (start, size) in enumerate(chunks):
        copies[i].wait()
        projected = by_rows(attended[...], weight[start : start + size])
        top, bottom = projected[:half], projected[half:]
        own_ref[:, start : start + size] = jnp.where(first_side, top, bottom)
        other_ref[:, start : start + size] = jnp.where(first_side, bottom, top).astype(jnp.bfloat16)


def run_attention(side, expert, page_table, sink_logits, queries, keys_values, segments, out_weight):
    length, query_width = queries.shape
    width = out_weight.shape[1]
    half = length // 2
    inverse = np.float32(rope_base) ** (
        -(np.arange(LANES) % (HEAD // 2)).astype(np.float32) / np.float32(HEAD // 2)
    )
    smem = pl.BlockSpec(memory_space=pltpu.SMEM)
    return pl.pallas_call(
        attention_kernel,
        out_shape=[
            jax.ShapeDtypeStruct((half, width), jnp.float32),
            jax.ShapeDtypeStruct((half, width), jnp.bfloat16),
            jax.ShapeDtypeStruct(
                (length // PAGE_LEN, PAGE_LEN, keys_values.shape[1]), jnp.bfloat16
            ),
            jax.ShapeDtypeStruct((1,), jnp.int32),
        ],
        in_specs=[smem] * 4 + [vmem()] * 4 + [anywhere()],
        out_specs=[vmem()] * 3 + [smem],
        scratch_shapes=[
            pltpu.VMEM((width, query_width), jnp.bfloat16),
            pltpu.VMEM((length, query_width), jnp.bfloat16),
            pltpu.SemaphoreType.DMA((len(tiles(width, 512)),)),
        ],
        compiler_params=pltpu.CompilerParams(vmem_limit_bytes=VMEM_LIMIT),
        name="attention",
    )(
        side,
        expert,
        page_table,
        sink_logits,
        queries,
        keys_values,
        segments[None],
        jnp.asarray(inverse.astype(np.float32))[None],
        out_weight.T,
    )


def vmem():
    return pl.BlockSpec(memory_space=pltpu.VMEM)


def anywhere():
    return pl.BlockSpec(memory_space=pl.ANY)


def run_expert(
    expert, pieces, gate_rows, gate_bias, up_rows, up_bias, down_weight, signs, block, limit
):
    parts = len(pieces)
    piece, padded = pieces[0].shape
    hidden_units, width = down_weight.shape
    slots = parts * piece // block * limit
    return pl.pallas_call(
        functools.partial(expert_kernel, parts, block, limit, 512),
        out_shape=[jax.ShapeDtypeStruct((piece, width), jnp.bfloat16)] * parts,
        in_specs=[pl.BlockSpec(memory_space=pltpu.SMEM)] + [vmem()] * (parts + 5)
        + [anywhere()] * 3,
        out_specs=[vmem()] * parts,
        scratch_shapes=[
            pltpu.VMEM((slots, width), jnp.bfloat16),
            pltpu.VMEM((slots, hidden_units), jnp.bfloat16),
        ],
        compiler_params=pltpu.CompilerParams(vmem_limit_bytes=8 * 2**20),
        cost_estimate=pl.CostEstimate(
            flops=6 * slots * width * hidden_units,
            bytes_accessed=6 * width * hidden_units,
            transcendentals=slots * hidden_units,
        ),
        name="expert",
    )(expert, *pieces, gate_rows, up_rows, down_weight, gate_bias, up_bias, *signs)


AXES = ("req", "tp")


def moved(array, n_req, step):
    outer, mid, core, tp = step
    pairs = []
    for source in range(2 * n_req):
        req, side = divmod(source, 2)
        place = (req // 4 ^ outer) * 4 + (req // 2 % 2 ^ mid) * 2 + (req % 2 ^ core)
        pairs.append((source, place * 2 + (side ^ tp)))
    return lax.ppermute(array, AXES, pairs)


def crossed(array, n_req, by_core):
    pairs = []
    for source in range(2 * n_req):
        req, side = divmod(source, 2)
        if req % 2 == by_core:
            pairs.append((source, (req ^ 2) * 2 + side))
        else:
            pairs.append((source, req * 2 + (side ^ 1)))
    return lax.ppermute(array, AXES, pairs)


def gather_rows(rows, n_req, weights, signs):
    outer = n_req // 4
    others = [moved(rows, n_req, (k, 0, 0, 0)) for k in range(1, outer)]
    weights[0], signs[0] = load(weights[0], rows, 40 * 2**20)
    others[0], signs[0] = lax.optimization_barrier((others[0], signs[0]))
    line = jnp.concatenate([rows] + others)
    first = crossed(line, n_req, 0)
    weights[1], signs[1] = load(weights[1], line, 2 * 2**20)
    late, signs[1] = lax.optimization_barrier((line, signs[1]))
    second = crossed(late, n_req, 1)
    both = crossed(first, n_req, 1)
    own = [line, first, second, both]
    sent = both
    weights[2], signs[2] = load(weights[2], line, 2 * 2**20)
    sent, signs[2] = lax.optimization_barrier((sent, signs[2]))
    pieces = own + [moved(piece, n_req, (0, 0, 1, 0)) for piece in (line, first, second, sent)]
    return pieces


def add_rows(left, right):
    return (left.astype(jnp.float32) + right.astype(jnp.float32)).astype(jnp.bfloat16)


def scatter_rows(sums, n_req):
    own, other = sums[:4], sums[4:]
    line, first, second, both = [
        add_rows(mine, moved(theirs, n_req, (0, 0, 1, 0))) for mine, theirs in zip(own, other)
    ]
    first = add_rows(first, crossed(both, n_req, 1))
    line = add_rows(line, crossed(second, n_req, 1))
    line = add_rows(line, crossed(first, n_req, 0))
    outer = n_req // 4
    count = line.shape[0] // outer
    blocks = [line[k * count : (k + 1) * count] for k in range(outer)]
    return [blocks[0]] + [
        moved(block, n_req, (k, 0, 0, 0)) for k, block in enumerate(blocks) if k > 0
    ]


def gathered_body(
    n_req,
    queries,
    keys_values,
    segments,
    sink_logits,
    out_weight,
    out_bias,
    residual,
    norm_gain,
    route_ids,
    route_logits,
    gate_weight,
    gate_bias,
    up_weight,
    up_bias,
    down_weight,
    down_bias,
    page_table,
):
    tok_count, width = residual.shape
    side = lax.axis_index("tp")[None]
    expert = lax.axis_index("req")[None]
    own, other, page_pool, expert = run_attention(
        side, expert, page_table, sink_logits, queries, keys_values, segments, out_weight
    )
    got = moved(other, n_req, (0, 0, 0, 1))
    weights = [gate_weight[0].T, up_weight[0].T, down_weight[0]]
    signs = [None] * len(weights)
    experts = down_bias.shape[0]
    base, rows = pl.pallas_call(
        mid_kernel,
        out_shape=[
            jax.ShapeDtypeStruct((tok_count, width), jnp.float32),
            jax.ShapeDtypeStruct((tok_count, width + 4 * experts), jnp.bfloat16),
        ],
        in_specs=[vmem()] * 8,
        out_specs=[vmem()] * 2,
        compiler_params=pltpu.CompilerParams(vmem_limit_bytes=4 * 2**20),
        name="norm_rows",
    )(
        own,
        got,
        residual,
        out_bias[None],
        norm_gain[None],
        route_ids.T,
        route_logits.T,
        down_bias,
    )
    pieces = gather_rows(rows, n_req, weights, signs)
    sums = run_expert(
        expert,
        pieces,
        weights[0],
        gate_bias,
        weights[1],
        up_bias,
        weights[2],
        signs,
        tok_count,
        slot_limit(tok_count, route_ids.shape[1], experts),
    )
    mixed = base
    for part in scatter_rows(sums, n_req):
        mixed = mixed + part.astype(jnp.float32)
    return (mixed.astype(jnp.bfloat16), page_pool)


def solution(mesh):
    in_specs = (
        P("req", "tp"),
        P("req", "tp"),
        P("req"),
        P("tp"),
        P("tp", None),
        P(),
        P(("req", "tp"), None),
        P(),
        P(("req", "tp"), None),
        P(("req", "tp"), None),
        P("req", None, "tp"),
        P("req", "tp"),
        P("req", None, "tp"),
        P("req", "tp"),
        P("req", "tp", None),
        P(),
        P("req", None),
    )
    out_specs = (P(("req", "tp"), None), P("req", None, "tp"))
    n_req, n_tp = mesh.shape["req"], mesh.shape["tp"]
    chosen = functools.partial(gathered_body, n_req) if (n_req, n_tp) == (16, 2) else body
    return jax.shard_map(chosen, mesh=mesh, in_specs=in_specs, out_specs=out_specs, check_vma=False)
```

```python
import functools

import jax
import jax.numpy as jnp
import numpy as np
from jax import lax
from jax.experimental import pallas as pl
from jax.experimental.pallas import tpu as pltpu
from jax.sharding import PartitionSpec as P

HEAD = 64
PAGE_LEN = 16
LANES = 128
DOWN_STEP = 512
VMEM_LIMIT = 60 * 2**20
LOAD_ROWS = 480


rope_base = 150000.0
norm_eps = 1e-05
swiglu_limit = 7.0
glu_alpha = 1.702


def seg_positions(segment_ids):
    length = segment_ids.shape[0]
    indices = jnp.arange(length, dtype=jnp.int32)
    change = jnp.concatenate([jnp.ones((1,), dtype=bool), segment_ids[1:] != segment_ids[:-1]])
    starts = lax.cummax(jnp.where(change, indices, 0), axis=0)
    return indices - starts


def rotate(values, positions):
    half_dim = values.shape[-1] // 2
    inverse = rope_base ** (-jnp.arange(half_dim, dtype=jnp.float32) / half_dim)
    angles = positions.astype(jnp.float32)[:, None] * inverse[None, :]
    cosine = jnp.cos(angles)[:, None, :]
    sine_col = jnp.sin(angles)[:, None, :]
    first_half = values[..., :half_dim]
    second_half = values[..., half_dim:]
    return jnp.concatenate(
        [
            first_half * cosine - second_half * sine_col,
            second_half * cosine + first_half * sine_col,
        ],
        axis=-1,
    )


def attend_group(queries, keys_values, segment_ids, sink_logits):
    length = queries.shape[0]
    kv_heads = keys_values.shape[1] // (2 * HEAD)
    q_heads = queries.shape[1] // HEAD
    group_size = q_heads // kv_heads
    positions = seg_positions(segment_ids)
    q_rot = rotate(queries.astype(jnp.float32).reshape(length, q_heads, HEAD), positions).astype(
        jnp.bfloat16
    )
    q_rot = q_rot.reshape(length, kv_heads, group_size, HEAD)
    key_part = keys_values.reshape(length, kv_heads, 2, HEAD)
    k_rot = rotate(key_part[:, :, 0].astype(jnp.float32), positions).astype(jnp.bfloat16)
    values = key_part[:, :, 1]
    scores = jnp.einsum(
        "qkgd,skd->kgqs", q_rot, k_rot, preferred_element_type=jnp.float32
    ) * HEAD ** (-0.5)
    indices = jnp.arange(length, dtype=jnp.int32)
    visible = (segment_ids[:, None] == segment_ids[None, :]) & (
        indices[None, :] <= indices[:, None]
    )
    scores = jnp.where(visible, scores, -jnp.inf)
    sink_col = sink_logits.reshape(kv_heads, group_size)[:, :, None]
    highest = jnp.maximum(jnp.max(scores, axis=-1), sink_col)
    expo_terms = jnp.exp(scores - highest[..., None])
    denominator = jnp.sum(expo_terms, axis=-1) + jnp.exp(sink_col - highest)
    probabilities = (expo_terms / denominator[..., None]).astype(jnp.bfloat16)
    attended = jnp.einsum(
        "kgqs,skd->qkgd", probabilities, values, preferred_element_type=jnp.float32
    )
    attended = attended.astype(jnp.bfloat16).reshape(length, q_heads * HEAD)
    cached = jnp.stack([k_rot, values], axis=2).reshape(length, kv_heads * 2 * HEAD)
    return (attended, cached)


def slot_index(routes, experts, capacity):
    blocks, row_count, route_width = routes.shape
    flat_ids = routes.reshape(blocks, row_count * route_width)
    onehot = (flat_ids[:, :, None] == jnp.arange(experts, dtype=jnp.int32)[None, None, :]).astype(
        jnp.int32
    )
    earlier = jnp.cumsum(onehot, axis=1) - onehot
    position = jnp.sum(earlier * onehot, axis=2)
    block_ids = jnp.arange(blocks, dtype=jnp.int32)[:, None]
    slot_ids = flat_ids * (blocks * capacity) + block_ids * capacity + position
    return slot_ids.reshape(blocks * row_count, route_width).astype(jnp.int32)


def dispatch(tokens, slot_ids, slot_total):
    row_count = tokens.shape[0]
    owners = jnp.broadcast_to(jnp.arange(row_count, dtype=jnp.int32)[:, None], slot_ids.shape)
    member = (
        jnp.full((slot_total,), row_count, jnp.int32)
        .at[slot_ids.reshape(-1)]
        .set(owners.reshape(-1))
    )
    padded = jnp.concatenate([tokens, jnp.zeros((1, tokens.shape[1]), tokens.dtype)], axis=0)
    return padded[member]


def slot_limit(tok_count, route_width, experts):
    return max(2, 2 * tok_count * route_width // experts)


def body(
    queries,
    keys_values,
    segments,
    sink_logits,
    out_weight,
    out_bias,
    residual,
    norm_gain,
    route_ids,
    route_logits,
    gate_weight,
    gate_bias,
    up_weight,
    up_bias,
    down_weight,
    down_bias,
    page_table,
):
    attended, cached = attend_group(queries, keys_values, segments, sink_logits)
    projected = lax.psum_scatter(
        jnp.dot(attended, out_weight, preferred_element_type=jnp.float32).astype(jnp.bfloat16),
        "tp",
        scatter_dimension=0,
        tiled=True,
    ).astype(jnp.float32)
    hidden = (residual.astype(jnp.float32) + projected + out_bias.astype(jnp.float32)).astype(
        jnp.bfloat16
    )
    stream = hidden.astype(jnp.float32)
    normed = (
        stream
        * lax.rsqrt(jnp.mean(stream * stream, axis=-1, keepdims=True) + norm_eps)
        * norm_gain.astype(jnp.float32)
    ).astype(jnp.bfloat16)
    route_weights = jax.nn.softmax(route_logits, axis=-1)
    tok_count, route_width = route_ids.shape
    experts = down_bias.shape[0]
    model_width = residual.shape[1]
    capacity = slot_limit(tok_count, route_width, experts)
    own_slots = slot_index(route_ids[None], experts, capacity)
    group_rows, group_routes = (
        lax.all_gather(normed, "tp", axis=0, tiled=True),
        lax.all_gather(route_ids, "tp", axis=0, tiled=True),
    )
    tp_count = group_rows.shape[0] // tok_count
    all_slots = slot_index(
        group_routes.reshape(tp_count, tok_count, route_width), experts, capacity
    )
    dispatched = dispatch(group_rows, all_slots, experts * tp_count * capacity).reshape(
        experts, tp_count, capacity, model_width
    )
    received = lax.all_to_all(dispatched, "req", split_axis=0, concat_axis=0, tiled=True)
    slot_shape = received.shape
    flat_rows = received.reshape(-1, model_width)
    gate_act = jnp.dot(flat_rows, gate_weight[0], preferred_element_type=jnp.float32) + gate_bias[
        0
    ].astype(jnp.float32)
    up_act = jnp.dot(flat_rows, up_weight[0], preferred_element_type=jnp.float32) + up_bias[
        0
    ].astype(jnp.float32)
    gate_act = jnp.minimum(gate_act, swiglu_limit)
    up_act = jnp.clip(up_act, -swiglu_limit, swiglu_limit)
    active = (gate_act * jax.nn.sigmoid(glu_alpha * gate_act) * (up_act + 1.0)).astype(jnp.bfloat16)
    partial_value = jnp.dot(active, down_weight[0], preferred_element_type=jnp.float32).reshape(
        slot_shape
    )
    summed = lax.psum_scatter(
        partial_value.astype(jnp.bfloat16), "tp", scatter_dimension=1, tiled=True
    ).astype(jnp.float32)
    returned = lax.all_to_all(
        summed.astype(jnp.bfloat16), "req", split_axis=0, concat_axis=0, tiled=True
    ).astype(summed.dtype)
    returned = returned.reshape(experts * capacity, model_width)
    slot_onehot = (
        own_slots[:, :, None] == jnp.arange(experts * capacity, dtype=jnp.int32)[None, None, :]
    ).astype(jnp.float32)
    combiner = jnp.einsum("rk,rks->rs", route_weights, slot_onehot, precision=lax.Precision.HIGHEST)
    expert_onehot = (
        route_ids[:, :, None] == jnp.arange(experts, dtype=jnp.int32)[None, None, :]
    ).astype(jnp.float32)
    dense_weights = jnp.einsum(
        "rk,rke->re", route_weights, expert_onehot, precision=lax.Precision.HIGHEST
    )
    expert_mix = jnp.dot(
        combiner, returned, precision=lax.Precision.HIGHEST, preferred_element_type=jnp.float32
    )
    expert_mix = expert_mix + jnp.dot(
        dense_weights,
        down_bias.astype(jnp.float32),
        precision=lax.Precision.HIGHEST,
        preferred_element_type=jnp.float32,
    )
    mixed_out = (stream + expert_mix).astype(jnp.bfloat16)
    blocks = cached.reshape(-1, PAGE_LEN, cached.shape[1])
    page_pool = jnp.zeros_like(blocks).at[page_table[0]].set(blocks)
    return (mixed_out, page_pool)


def mid_kernel(
    own_ref,
    got_ref,
    residual_ref,
    out_bias_ref,
    gain_ref,
    ids_ref,
    logits_ref,
    down_bias_ref,
    base_ref,
    rows_ref,
):
    width = residual_ref.shape[1]
    experts = down_bias_ref.shape[0]
    hidden = (
        residual_ref[...].astype(jnp.float32)
        + own_ref[...].astype(jnp.float32)
        + got_ref[...].astype(jnp.float32)
        + out_bias_ref[...].astype(jnp.float32)
    ).astype(jnp.bfloat16)
    stream = hidden.astype(jnp.float32)
    normed = (
        stream
        * lax.rsqrt(jnp.mean(stream * stream, axis=-1, keepdims=True) + norm_eps)
        * gain_ref[...].astype(jnp.float32)
    ).astype(jnp.bfloat16)
    logits = logits_ref[...]
    expo = jnp.exp(logits - jnp.max(logits, axis=0, keepdims=True))
    weights = expo / jnp.sum(expo, axis=0, keepdims=True)
    high = weights.astype(jnp.bfloat16).astype(jnp.float32)
    low = (weights - high).astype(jnp.bfloat16).astype(jnp.float32)
    ids = ids_ref[...]
    column = lax.broadcasted_iota(jnp.int32, (LANES, ids.shape[1]), 0)
    high_cols = jnp.zeros(column.shape, jnp.float32)
    low_cols = jnp.zeros(column.shape, jnp.float32)
    first = width % LANES
    for k in range(ids.shape[0]):
        at = ids[k : k + 1] + first
        high_cols = high_cols + jnp.where(column == at, high[k : k + 1], 0.0)
        low_cols = low_cols + jnp.where(column == at + experts, low[k : k + 1], 0.0)
    high_cols = high_cols.T
    low_cols = low_cols.T
    high_dense = high_cols[:, first : first + experts].astype(jnp.bfloat16)
    low_dense = low_cols[:, first + experts : first + 2 * experts].astype(jnp.bfloat16)
    bias = down_bias_ref[...]
    base_ref[...] = (
        stream
        + jnp.dot(high_dense, bias, preferred_element_type=jnp.float32)
        + jnp.dot(low_dense, bias, preferred_element_type=jnp.float32)
    )
    rows_ref[:, :width] = normed
    rows_ref[:, width:] = (high_cols + low_cols)[:, first:].astype(jnp.bfloat16)


def tiles(total, step):
    return [(start, min(step, total - start)) for start in range(0, total, step)]


def by_rows(left, right):
    return lax.dot_general(
        left, right, (((1,), (1,)), ((), ())), preferred_element_type=jnp.float32
    )


def load_kernel(after_ref, source, target, sign, sems):
    copies = []
    for i, (start, size) in enumerate(tiles(source.shape[0], LOAD_ROWS)):
        here = pl.ds(start, size)
        copies.append(pltpu.make_async_copy(source.at[here], target.at[here], sems.at[i]))
    for copy in copies:
        copy.start()
    for copy in copies:
        copy.wait()
    sign[...] = target[: sign.shape[0], : sign.shape[1]]


def load(weight, after, reserve):
    return pl.pallas_call(
        load_kernel,
        out_shape=[
            jax.ShapeDtypeStruct(weight.shape, weight.dtype),
            jax.ShapeDtypeStruct((16, LANES), weight.dtype),
        ],
        in_specs=[anywhere()] * 2,
        out_specs=[vmem()] * 2,
        scratch_shapes=[pltpu.SemaphoreType.DMA((len(tiles(weight.shape[0], LOAD_ROWS)),))],
        compiler_params=pltpu.CompilerParams(vmem_limit_bytes=reserve),
        cost_estimate=pl.CostEstimate(
            flops=0, bytes_accessed=4 * weight.size, transcendentals=0
        ),
        name="load",
    )(after, weight)


def expert_kernel(parts, block, limit, step, expert_ref, *refs):
    pieces, refs = refs[:parts], refs[parts:]
    gate_w, up_w, down_w, gate_bias_ref, up_bias_ref = refs[:5]
    outs, (picked, active) = refs[8 : 8 + parts], refs[8 + parts :]
    piece, padded = pieces[0].shape
    total = parts * piece
    units, width = down_w.shape
    group = 2 * piece
    half = piece // 2
    group_slots = group // block * limit
    up_bias = jnp.broadcast_to(up_bias_ref[...].astype(jnp.float32), (8, units)).T
    gate_bias = jnp.broadcast_to(gate_bias_ref[...].astype(jnp.float32), (8, units)).T

    expert = expert_ref[0]
    experts = (padded - width) // 4
    lane = lax.broadcasted_iota(jnp.int32, (16, LANES), 1)
    which = lax.broadcasted_iota(jnp.int32, (16, LANES), 0)
    choose = jnp.where(
        (lane == width % LANES + expert + which * experts) & (which < 2), 1.0, 0.0
    ).astype(jnp.bfloat16)
    found = by_rows(
        choose, jnp.concatenate([p[:, padded - LANES :] for p in pieces], axis=0)
    )
    share = jnp.broadcast_to(found[0:1] + found[1:2], (8, total))
    chosen = share > 0.0
    token = lax.broadcasted_iota(jnp.int32, (8, total), 1)
    count = jnp.where(chosen, 1, 0)
    reach = 1
    while reach < block:
        count = count + jnp.where(token % block >= reach, pltpu.roll(count, reach, 1), 0)
        reach *= 2
    slot = jnp.where(chosen, token // block * limit + count - 1, -1)
    spreads, shares = [], []
    for g in range(total // group):
        here = slice(g * group, (g + 1) * group)
        hit = (
            lax.broadcasted_iota(jnp.int32, (group_slots, group), 0) + g * group_slots
            == slot[0:1, here]
        )
        shares.append(jnp.sum(jnp.where(hit, share[0:1, here], 0.0), axis=1, keepdims=True))
        pick = jnp.where(hit, 1.0, 0.0)
        spreads.append(pick.T.astype(jnp.bfloat16))
        pick = pick.astype(jnp.bfloat16)
        for start, size in tiles(width, 2 * step):
            cols = slice(start, start + size)
            both = jnp.concatenate([pieces[2 * g][:, cols], pieces[2 * g + 1][:, cols]], axis=0)
            picked[g * group_slots : (g + 1) * group_slots, cols] = jnp.dot(
                pick, both, preferred_element_type=jnp.float32
            ).astype(jnp.bfloat16)
    slot_share = jnp.concatenate(shares, axis=0)

    def activate(start, size, gate, up):
        here = slice(start, start + size)
        gate = jnp.minimum(gate + gate_bias[here, 0:1], swiglu_limit)
        up = jnp.clip(up + up_bias[here, 0:1], -swiglu_limit, swiglu_limit)
        value = gate * (1.0 / (1.0 + jnp.exp(-glu_alpha * gate))) * (up + 1.0)
        active[:, here] = value.T.astype(jnp.bfloat16)

    def give(start, size, value):
        cols = slice(start, start + size)
        scaled = (value * slot_share).astype(jnp.bfloat16)
        for g, spread in enumerate(spreads):
            sums = jnp.dot(
                spread,
                scaled[g * group_slots : (g + 1) * group_slots],
                preferred_element_type=jnp.float32,
            ).astype(jnp.bfloat16)
            near, far = outs[g // 2 * 4 + g % 2], outs[g // 2 * 4 + g % 2 + 2]
            near[:half, cols] = sums[:half]
            far[:half, cols] = sums[half:piece]
            near[half:, cols] = sums[piece : piece + half]
            far[half:, cols] = sums[piece + half :]

    last = None
    for start, size in tiles(units, step):
        here = slice(start, start + size)
        gate = by_rows(gate_w[here], picked[...])
        up = by_rows(up_w[here], picked[...])
        if last is not None:
            activate(*last)
        last = (start, size, gate, up)
    activate(*last)
    last = None
    for start, size in tiles(width, DOWN_STEP):
        cols = slice(start, start + size)
        value = jnp.dot(active[...], down_w[:, cols], preferred_element_type=jnp.float32)
        if last is not None:
            give(*last)
        last = (start, size, value)
    give(*last)


def attention_kernel(
    side_ref,
    expert_in_ref,
    pages_ref,
    sink_ref,
    queries_ref,
    keys_values_ref,
    segments_ref,
    inverse_ref,
    weight_hbm,
    own_ref,
    other_ref,
    cache_ref,
    expert_ref,
    weight,
    attended,
    sems,
):
    expert_ref[0] = expert_in_ref[0]
    length, query_width = queries_ref.shape
    width = weight.shape[0]
    kv_heads = keys_values_ref.shape[1] // LANES
    group_tiles = query_width // LANES // kv_heads
    chunks = tiles(width, 512)
    copies = [
        pltpu.make_async_copy(
            weight_hbm.at[pl.ds(start, size)], weight.at[pl.ds(start, size)], sems.at[i]
        )
        for i, (start, size) in enumerate(chunks)
    ]
    for copy in copies:
        copy.start()
    named = jnp.broadcast_to(segments_ref[...].astype(jnp.float32), (length, length))
    visible = (named == named.T) & (
        lax.broadcasted_iota(jnp.int32, (length, length), 1)
        <= lax.broadcasted_iota(jnp.int32, (length, length), 0)
    )
    positions = jnp.sum(jnp.where(visible, 1.0, 0.0), axis=1, keepdims=True) - 1.0
    angles = positions * inverse_ref[...]
    lane = lax.broadcasted_iota(jnp.int32, (length, LANES), 1)
    lower = lane % HEAD < HEAD // 2
    cosine = jnp.cos(angles)
    sine = jnp.sin(angles)
    sine = jnp.where(lower, -sine, sine)
    left = lane < HEAD

    def turned(tile):
        swapped = jnp.where(
            lower, pltpu.roll(tile, LANES - HEAD // 2, 1), pltpu.roll(tile, HEAD // 2, 1)
        )
        return tile * cosine + swapped * sine

    group_heads = 2 * group_tiles
    token = lax.broadcasted_iota(jnp.int32, (length, group_heads * length), 1)
    repeat = token % length == lax.broadcasted_iota(jnp.int32, token.shape, 0)
    seen = (
        jnp.dot(
            jnp.where(visible, 1.0, 0.0).T.astype(jnp.bfloat16),
            jnp.where(repeat, 1.0, 0.0).astype(jnp.bfloat16),
            preferred_element_type=jnp.float32,
        )
        > 0.5
    )
    head_of = lax.broadcasted_iota(jnp.int32, (1, group_heads * length), 1) // length
    for k in range(kv_heads):
        raw = keys_values_ref[:, k * LANES : (k + 1) * LANES].astype(jnp.float32)
        pair = jnp.where(left, turned(raw), raw).astype(jnp.bfloat16)
        for b in range(cache_ref.shape[0]):
            cache_ref[pages_ref[0, b], :, k * LANES : (k + 1) * LANES] = pair[
                b * PAGE_LEN : (b + 1) * PAGE_LEN
            ]
        heads = []
        sink = jnp.zeros(head_of.shape, jnp.float32)
        for h in range(group_heads):
            sink = jnp.where(head_of == h, sink_ref[k * group_heads + h], sink)
        for t in range(k * group_tiles, (k + 1) * group_tiles):
            tile = turned(queries_ref[:, t * LANES : (t + 1) * LANES].astype(jnp.float32))
            heads.append(jnp.where(left, tile, 0.0))
            heads.append(jnp.where(left, pltpu.roll(tile, HEAD, 1), 0.0))
        scores = by_rows(
            pair, jnp.concatenate(heads, axis=0).astype(jnp.bfloat16)
        ) * HEAD ** (-0.5)
        scores = jnp.where(seen, scores, -1e30)
        highest = jnp.maximum(jnp.max(scores, axis=0, keepdims=True), sink)
        expo = jnp.where(seen, jnp.exp(scores - highest), 0.0)
        denominator = jnp.sum(expo, axis=0, keepdims=True) + jnp.exp(sink - highest)
        probabilities = (expo / denominator).T.astype(jnp.bfloat16)
        mixed = jnp.dot(probabilities, pair, preferred_element_type=jnp.float32)
        for t in range(group_tiles):
            even = mixed[2 * t * length : (2 * t + 1) * length]
            odd = mixed[(2 * t + 1) * length : (2 * t + 2) * length]
            start = (k * group_tiles + t) * LANES
            attended[:, start : start + LANES] = jnp.where(
                left, pltpu.roll(even, HEAD, 1), odd
            ).astype(jnp.bfloat16)
    first_side = side_ref[0] == 0
    half = own_ref.shape[0]
    for i, (start, size) in enumerate(chunks):
        copies[i].wait()
        projected = by_rows(attended[...], weight[start : start + size])
        top, bottom = projected[:half], projected[half:]
        own_ref[:, start : start + size] = jnp.where(first_side, top, bottom)
        other_ref[:, start : start + size] = jnp.where(first_side, bottom, top).astype(jnp.bfloat16)


def run_attention(side, expert, page_table, sink_logits, queries, keys_values, segments, out_weight):
    length, query_width = queries.shape
    width = out_weight.shape[1]
    half = length // 2
    inverse = np.float32(rope_base) ** (
        -(np.arange(LANES) % (HEAD // 2)).astype(np.float32) / np.float32(HEAD // 2)
    )
    smem = pl.BlockSpec(memory_space=pltpu.SMEM)
    return pl.pallas_call(
        attention_kernel,
        out_shape=[
            jax.ShapeDtypeStruct((half, width), jnp.float32),
            jax.ShapeDtypeStruct((half, width), jnp.bfloat16),
            jax.ShapeDtypeStruct(
                (length // PAGE_LEN, PAGE_LEN, keys_values.shape[1]), jnp.bfloat16
            ),
            jax.ShapeDtypeStruct((1,), jnp.int32),
        ],
        in_specs=[smem] * 4 + [vmem()] * 4 + [anywhere()],
        out_specs=[vmem()] * 3 + [smem],
        scratch_shapes=[
            pltpu.VMEM((width, query_width), jnp.bfloat16),
            pltpu.VMEM((length, query_width), jnp.bfloat16),
            pltpu.SemaphoreType.DMA((len(tiles(width, 512)),)),
        ],
        compiler_params=pltpu.CompilerParams(vmem_limit_bytes=VMEM_LIMIT),
        name="attention",
    )(
        side,
        expert,
        page_table,
        sink_logits,
        queries,
        keys_values,
        segments[None],
        jnp.asarray(inverse.astype(np.float32))[None],
        out_weight.T,
    )


def vmem():
    return pl.BlockSpec(memory_space=pltpu.VMEM)


def anywhere():
    return pl.BlockSpec(memory_space=pl.ANY)


def run_expert(
    expert, pieces, gate_rows, gate_bias, up_rows, up_bias, down_weight, signs, block, limit
):
    parts = len(pieces)
    piece, padded = pieces[0].shape
    hidden_units, width = down_weight.shape
    slots = parts * piece // block * limit
    return pl.pallas_call(
        functools.partial(expert_kernel, parts, block, limit, 512),
        out_shape=[jax.ShapeDtypeStruct((piece, width), jnp.bfloat16)] * parts,
        in_specs=[pl.BlockSpec(memory_space=pltpu.SMEM)] + [vmem()] * (parts + 5)
        + [anywhere()] * 3,
        out_specs=[vmem()] * parts,
        scratch_shapes=[
            pltpu.VMEM((slots, width), jnp.bfloat16),
            pltpu.VMEM((slots, hidden_units), jnp.bfloat16),
        ],
        compiler_params=pltpu.CompilerParams(vmem_limit_bytes=8 * 2**20),
        cost_estimate=pl.CostEstimate(
            flops=6 * slots * width * hidden_units,
            bytes_accessed=6 * width * hidden_units,
            transcendentals=slots * hidden_units,
        ),
        name="expert",
    )(expert, *pieces, gate_rows, up_rows, down_weight, gate_bias, up_bias, *signs)


AXES = ("req", "tp")


def moved(array, n_req, step):
    outer, mid, core, tp = step
    pairs = []
    for source in range(2 * n_req):
        req, side = divmod(source, 2)
        place = (req // 4 ^ outer) * 4 + (req // 2 % 2 ^ mid) * 2 + (req % 2 ^ core)
        pairs.append((source, place * 2 + (side ^ tp)))
    return lax.ppermute(array, AXES, pairs)


def crossed(array, n_req, by_core):
    pairs = []
    for source in range(2 * n_req):
        req, side = divmod(source, 2)
        if req % 2 == by_core:
            pairs.append((source, (req ^ 2) * 2 + side))
        else:
            pairs.append((source, req * 2 + (side ^ 1)))
    return lax.ppermute(array, AXES, pairs)


def gather_rows(rows, n_req, weights, signs):
    outer = n_req // 4
    others = [moved(rows, n_req, (k, 0, 0, 0)) for k in range(1, outer)]
    weights[0], signs[0] = load(weights[0], rows, 40 * 2**20)
    others[0], signs[0] = lax.optimization_barrier((others[0], signs[0]))
    line = jnp.concatenate([rows] + others)
    first = crossed(line, n_req, 0)
    weights[1], signs[1] = load(weights[1], line, 2 * 2**20)
    late, signs[1] = lax.optimization_barrier((line, signs[1]))
    second = crossed(late, n_req, 1)
    both = crossed(first, n_req, 1)
    own = [line, first, second, both]
    sent = both
    weights[2], signs[2] = load(weights[2], line, 2 * 2**20)
    sent, signs[2] = lax.optimization_barrier((sent, signs[2]))
    pieces = own + [moved(piece, n_req, (0, 0, 1, 0)) for piece in (line, first, second, sent)]
    return pieces


def add_rows(left, right):
    return (left.astype(jnp.float32) + right.astype(jnp.float32)).astype(jnp.bfloat16)


def scatter_rows(sums, n_req):
    own, other = sums[:4], sums[4:]
    outer = n_req // 4
    half = outer // 2
    parts = []
    for side in (1, 0):
        here, beyond = [
            add_rows(own[i], moved(other[i], n_req, (0, 0, 1, 0)))
            for i in (2 * side, 2 * side + 1)
        ]
        here = add_rows(here, crossed(beyond, n_req, 1))
        middle = here.shape[0] // 2
        line = add_rows(here[:middle], crossed(here[middle:], n_req, 0))
        count = middle // half
        for i in range(half):
            block = line[i * count : (i + 1) * count]
            step = half * side + i
            parts.append(moved(block, n_req, (step, 0, 0, 0)) if step > 0 else block)
    return parts


def gathered_body(
    n_req,
    queries,
    keys_values,
    segments,
    sink_logits,
    out_weight,
    out_bias,
    residual,
    norm_gain,
    route_ids,
    route_logits,
    gate_weight,
    gate_bias,
    up_weight,
    up_bias,
    down_weight,
    down_bias,
    page_table,
):
    tok_count, width = residual.shape
    side = lax.axis_index("tp")[None]
    expert = lax.axis_index("req")[None]
    own, other, page_pool, expert = run_attention(
        side, expert, page_table, sink_logits, queries, keys_values, segments, out_weight
    )
    got = moved(other, n_req, (0, 0, 0, 1))
    weights = [gate_weight[0].T, up_weight[0].T, down_weight[0]]
    signs = [None] * len(weights)
    experts = down_bias.shape[0]
    base, rows = pl.pallas_call(
        mid_kernel,
        out_shape=[
            jax.ShapeDtypeStruct((tok_count, width), jnp.float32),
            jax.ShapeDtypeStruct((tok_count, width + 4 * experts), jnp.bfloat16),
        ],
        in_specs=[vmem()] * 8,
        out_specs=[vmem()] * 2,
        compiler_params=pltpu.CompilerParams(vmem_limit_bytes=4 * 2**20),
        name="norm_rows",
    )(
        own,
        got,
        residual,
        out_bias[None],
        norm_gain[None],
        route_ids.T,
        route_logits.T,
        down_bias,
    )
    pieces = gather_rows(rows, n_req, weights, signs)
    sums = run_expert(
        expert,
        pieces,
        weights[0],
        gate_bias,
        weights[1],
        up_bias,
        weights[2],
        signs,
        tok_count,
        slot_limit(tok_count, route_ids.shape[1], experts),
    )
    mixed = base
    for part in scatter_rows(sums, n_req):
        mixed = mixed + part.astype(jnp.float32)
    return (mixed.astype(jnp.bfloat16), page_pool)


def solution(mesh):
    in_specs = (
        P("req", "tp"),
        P("req", "tp"),
        P("req"),
        P("tp"),
        P("tp", None),
        P(),
        P(("req", "tp"), None),
        P(),
        P(("req", "tp"), None),
        P(("req", "tp"), None),
        P("req", None, "tp"),
        P("req", "tp"),
        P("req", None, "tp"),
        P("req", "tp"),
        P("req", "tp", None),
        P(),
        P("req", None),
    )
    out_specs = (P(("req", "tp"), None), P("req", None, "tp"))
    n_req, n_tp = mesh.shape["req"], mesh.shape["tp"]
    chosen = functools.partial(gathered_body, n_req) if (n_req, n_tp) == (16, 2) else body
    return jax.shard_map(chosen, mesh=mesh, in_specs=in_specs, out_specs=out_specs, check_vma=False)
```

```python
import functools

import jax
import jax.numpy as jnp
import numpy as np
from jax import lax
from jax.experimental import pallas as pl
from jax.experimental.pallas import tpu as pltpu
from jax.sharding import PartitionSpec as P

HEAD = 64
PAGE_LEN = 16
LANES = 128
DOWN_STEP = 512
VMEM_LIMIT = 60 * 2**20
LOAD_ROWS = 480


rope_base = 150000.0
norm_eps = 1e-05
swiglu_limit = 7.0
glu_alpha = 1.702


def seg_positions(segment_ids):
    length = segment_ids.shape[0]
    indices = jnp.arange(length, dtype=jnp.int32)
    change = jnp.concatenate([jnp.ones((1,), dtype=bool), segment_ids[1:] != segment_ids[:-1]])
    starts = lax.cummax(jnp.where(change, indices, 0), axis=0)
    return indices - starts


def rotate(values, positions):
    half_dim = values.shape[-1] // 2
    inverse = rope_base ** (-jnp.arange(half_dim, dtype=jnp.float32) / half_dim)
    angles = positions.astype(jnp.float32)[:, None] * inverse[None, :]
    cosine = jnp.cos(angles)[:, None, :]
    sine_col = jnp.sin(angles)[:, None, :]
    first_half = values[..., :half_dim]
    second_half = values[..., half_dim:]
    return jnp.concatenate(
        [
            first_half * cosine - second_half * sine_col,
            second_half * cosine + first_half * sine_col,
        ],
        axis=-1,
    )


def attend_group(queries, keys_values, segment_ids, sink_logits):
    length = queries.shape[0]
    kv_heads = keys_values.shape[1] // (2 * HEAD)
    q_heads = queries.shape[1] // HEAD
    group_size = q_heads // kv_heads
    positions = seg_positions(segment_ids)
    q_rot = rotate(queries.astype(jnp.float32).reshape(length, q_heads, HEAD), positions).astype(
        jnp.bfloat16
    )
    q_rot = q_rot.reshape(length, kv_heads, group_size, HEAD)
    key_part = keys_values.reshape(length, kv_heads, 2, HEAD)
    k_rot = rotate(key_part[:, :, 0].astype(jnp.float32), positions).astype(jnp.bfloat16)
    values = key_part[:, :, 1]
    scores = jnp.einsum(
        "qkgd,skd->kgqs", q_rot, k_rot, preferred_element_type=jnp.float32
    ) * HEAD ** (-0.5)
    indices = jnp.arange(length, dtype=jnp.int32)
    visible = (segment_ids[:, None] == segment_ids[None, :]) & (
        indices[None, :] <= indices[:, None]
    )
    scores = jnp.where(visible, scores, -jnp.inf)
    sink_col = sink_logits.reshape(kv_heads, group_size)[:, :, None]
    highest = jnp.maximum(jnp.max(scores, axis=-1), sink_col)
    expo_terms = jnp.exp(scores - highest[..., None])
    denominator = jnp.sum(expo_terms, axis=-1) + jnp.exp(sink_col - highest)
    probabilities = (expo_terms / denominator[..., None]).astype(jnp.bfloat16)
    attended = jnp.einsum(
        "kgqs,skd->qkgd", probabilities, values, preferred_element_type=jnp.float32
    )
    attended = attended.astype(jnp.bfloat16).reshape(length, q_heads * HEAD)
    cached = jnp.stack([k_rot, values], axis=2).reshape(length, kv_heads * 2 * HEAD)
    return (attended, cached)


def slot_index(routes, experts, capacity):
    blocks, row_count, route_width = routes.shape
    flat_ids = routes.reshape(blocks, row_count * route_width)
    onehot = (flat_ids[:, :, None] == jnp.arange(experts, dtype=jnp.int32)[None, None, :]).astype(
        jnp.int32
    )
    earlier = jnp.cumsum(onehot, axis=1) - onehot
    position = jnp.sum(earlier * onehot, axis=2)
    block_ids = jnp.arange(blocks, dtype=jnp.int32)[:, None]
    slot_ids = flat_ids * (blocks * capacity) + block_ids * capacity + position
    return slot_ids.reshape(blocks * row_count, route_width).astype(jnp.int32)


def dispatch(tokens, slot_ids, slot_total):
    row_count = tokens.shape[0]
    owners = jnp.broadcast_to(jnp.arange(row_count, dtype=jnp.int32)[:, None], slot_ids.shape)
    member = (
        jnp.full((slot_total,), row_count, jnp.int32)
        .at[slot_ids.reshape(-1)]
        .set(owners.reshape(-1))
    )
    padded = jnp.concatenate([tokens, jnp.zeros((1, tokens.shape[1]), tokens.dtype)], axis=0)
    return padded[member]


def slot_limit(tok_count, route_width, experts):
    return max(2, 2 * tok_count * route_width // experts)


def body(
    queries,
    keys_values,
    segments,
    sink_logits,
    out_weight,
    out_bias,
    residual,
    norm_gain,
    route_ids,
    route_logits,
    gate_weight,
    gate_bias,
    up_weight,
    up_bias,
    down_weight,
    down_bias,
    page_table,
):
    attended, cached = attend_group(queries, keys_values, segments, sink_logits)
    projected = lax.psum_scatter(
        jnp.dot(attended, out_weight, preferred_element_type=jnp.float32).astype(jnp.bfloat16),
        "tp",
        scatter_dimension=0,
        tiled=True,
    ).astype(jnp.float32)
    hidden = (residual.astype(jnp.float32) + projected + out_bias.astype(jnp.float32)).astype(
        jnp.bfloat16
    )
    stream = hidden.astype(jnp.float32)
    normed = (
        stream
        * lax.rsqrt(jnp.mean(stream * stream, axis=-1, keepdims=True) + norm_eps)
        * norm_gain.astype(jnp.float32)
    ).astype(jnp.bfloat16)
    route_weights = jax.nn.softmax(route_logits, axis=-1)
    tok_count, route_width = route_ids.shape
    experts = down_bias.shape[0]
    model_width = residual.shape[1]
    capacity = slot_limit(tok_count, route_width, experts)
    own_slots = slot_index(route_ids[None], experts, capacity)
    group_rows, group_routes = (
        lax.all_gather(normed, "tp", axis=0, tiled=True),
        lax.all_gather(route_ids, "tp", axis=0, tiled=True),
    )
    tp_count = group_rows.shape[0] // tok_count
    all_slots = slot_index(
        group_routes.reshape(tp_count, tok_count, route_width), experts, capacity
    )
    dispatched = dispatch(group_rows, all_slots, experts * tp_count * capacity).reshape(
        experts, tp_count, capacity, model_width
    )
    received = lax.all_to_all(dispatched, "req", split_axis=0, concat_axis=0, tiled=True)
    slot_shape = received.shape
    flat_rows = received.reshape(-1, model_width)
    gate_act = jnp.dot(flat_rows, gate_weight[0], preferred_element_type=jnp.float32) + gate_bias[
        0
    ].astype(jnp.float32)
    up_act = jnp.dot(flat_rows, up_weight[0], preferred_element_type=jnp.float32) + up_bias[
        0
    ].astype(jnp.float32)
    gate_act = jnp.minimum(gate_act, swiglu_limit)
    up_act = jnp.clip(up_act, -swiglu_limit, swiglu_limit)
    active = (gate_act * jax.nn.sigmoid(glu_alpha * gate_act) * (up_act + 1.0)).astype(jnp.bfloat16)
    partial_value = jnp.dot(active, down_weight[0], preferred_element_type=jnp.float32).reshape(
        slot_shape
    )
    summed = lax.psum_scatter(
        partial_value.astype(jnp.bfloat16), "tp", scatter_dimension=1, tiled=True
    ).astype(jnp.float32)
    returned = lax.all_to_all(
        summed.astype(jnp.bfloat16), "req", split_axis=0, concat_axis=0, tiled=True
    ).astype(summed.dtype)
    returned = returned.reshape(experts * capacity, model_width)
    slot_onehot = (
        own_slots[:, :, None] == jnp.arange(experts * capacity, dtype=jnp.int32)[None, None, :]
    ).astype(jnp.float32)
    combiner = jnp.einsum("rk,rks->rs", route_weights, slot_onehot, precision=lax.Precision.HIGHEST)
    expert_onehot = (
        route_ids[:, :, None] == jnp.arange(experts, dtype=jnp.int32)[None, None, :]
    ).astype(jnp.float32)
    dense_weights = jnp.einsum(
        "rk,rke->re", route_weights, expert_onehot, precision=lax.Precision.HIGHEST
    )
    expert_mix = jnp.dot(
        combiner, returned, precision=lax.Precision.HIGHEST, preferred_element_type=jnp.float32
    )
    expert_mix = expert_mix + jnp.dot(
        dense_weights,
        down_bias.astype(jnp.float32),
        precision=lax.Precision.HIGHEST,
        preferred_element_type=jnp.float32,
    )
    mixed_out = (stream + expert_mix).astype(jnp.bfloat16)
    blocks = cached.reshape(-1, PAGE_LEN, cached.shape[1])
    page_pool = jnp.zeros_like(blocks).at[page_table[0]].set(blocks)
    return (mixed_out, page_pool)


def mid_kernel(
    own_ref,
    got_ref,
    gain_ref,
    ids_ref,
    logits_ref,
    down_bias_ref,
    base_ref,
    rows_ref,
):
    width = own_ref.shape[1]
    experts = down_bias_ref.shape[0]
    hidden = (own_ref[...] + got_ref[...].astype(jnp.float32)).astype(jnp.bfloat16)
    stream = hidden.astype(jnp.float32)
    normed = (
        stream
        * lax.rsqrt(jnp.mean(stream * stream, axis=-1, keepdims=True) + norm_eps)
        * gain_ref[...].astype(jnp.float32)
    ).astype(jnp.bfloat16)
    logits = logits_ref[...]
    expo = jnp.exp(logits - jnp.max(logits, axis=0, keepdims=True))
    weights = expo / jnp.sum(expo, axis=0, keepdims=True)
    high = weights.astype(jnp.bfloat16).astype(jnp.float32)
    low = (weights - high).astype(jnp.bfloat16).astype(jnp.float32)
    ids = ids_ref[...]
    column = lax.broadcasted_iota(jnp.int32, (LANES, ids.shape[1]), 0)
    high_cols = jnp.zeros(column.shape, jnp.float32)
    low_cols = jnp.zeros(column.shape, jnp.float32)
    first = width % LANES
    for k in range(ids.shape[0]):
        at = ids[k : k + 1] + first
        high_cols = high_cols + jnp.where(column == at, high[k : k + 1], 0.0)
        low_cols = low_cols + jnp.where(column == at + experts, low[k : k + 1], 0.0)
    high_cols = high_cols.T
    low_cols = low_cols.T
    high_dense = high_cols[:, first : first + experts].astype(jnp.bfloat16)
    low_dense = low_cols[:, first + experts : first + 2 * experts].astype(jnp.bfloat16)
    bias = down_bias_ref[...]
    base_ref[...] = (
        stream
        + jnp.dot(high_dense, bias, preferred_element_type=jnp.float32)
        + jnp.dot(low_dense, bias, preferred_element_type=jnp.float32)
    )
    rows_ref[:, :width] = normed
    rows_ref[:, width:] = (high_cols + low_cols)[:, first:].astype(jnp.bfloat16)


def tiles(total, step):
    return [(start, min(step, total - start)) for start in range(0, total, step)]


def by_rows(left, right):
    return lax.dot_general(
        left, right, (((1,), (1,)), ((), ())), preferred_element_type=jnp.float32
    )


def load_kernel(after_ref, source, target, sign, sems):
    copies = []
    for i, (start, size) in enumerate(tiles(source.shape[0], LOAD_ROWS)):
        here = pl.ds(start, size)
        copies.append(pltpu.make_async_copy(source.at[here], target.at[here], sems.at[i]))
    for copy in copies:
        copy.start()
    for copy in copies:
        copy.wait()
    sign[...] = target[: sign.shape[0], : sign.shape[1]]


def load(weight, after, reserve):
    return pl.pallas_call(
        load_kernel,
        out_shape=[
            jax.ShapeDtypeStruct(weight.shape, weight.dtype),
            jax.ShapeDtypeStruct((16, LANES), weight.dtype),
        ],
        in_specs=[anywhere()] * 2,
        out_specs=[vmem()] * 2,
        scratch_shapes=[pltpu.SemaphoreType.DMA((len(tiles(weight.shape[0], LOAD_ROWS)),))],
        compiler_params=pltpu.CompilerParams(vmem_limit_bytes=reserve),
        cost_estimate=pl.CostEstimate(
            flops=0, bytes_accessed=4 * weight.size, transcendentals=0
        ),
        name="load",
    )(after, weight)


def expert_kernel(parts, block, limit, step, expert_ref, *refs):
    pieces, refs = refs[:parts], refs[parts:]
    gate_w, up_w, down_w, gate_bias_ref, up_bias_ref = refs[:5]
    outs, (picked, active) = refs[8 : 8 + parts], refs[8 + parts :]
    piece, padded = pieces[0].shape
    total = parts * piece
    units, width = down_w.shape
    group = 2 * piece
    half = piece // 2
    group_slots = group // block * limit
    up_bias = jnp.broadcast_to(up_bias_ref[...].astype(jnp.float32), (8, units)).T
    gate_bias = jnp.broadcast_to(gate_bias_ref[...].astype(jnp.float32), (8, units)).T

    expert = expert_ref[0]
    experts = (padded - width) // 4
    lane = lax.broadcasted_iota(jnp.int32, (16, LANES), 1)
    which = lax.broadcasted_iota(jnp.int32, (16, LANES), 0)
    choose = jnp.where(
        (lane == width % LANES + expert + which * experts) & (which < 2), 1.0, 0.0
    ).astype(jnp.bfloat16)
    found = by_rows(
        choose, jnp.concatenate([p[:, padded - LANES :] for p in pieces], axis=0)
    )
    share = jnp.broadcast_to(found[0:1] + found[1:2], (8, total))
    chosen = share > 0.0
    token = lax.broadcasted_iota(jnp.int32, (8, total), 1)
    count = jnp.where(chosen, 1, 0)
    reach = 1
    while reach < block:
        count = count + jnp.where(token % block >= reach, pltpu.roll(count, reach, 1), 0)
        reach *= 2
    slot = jnp.where(chosen, token // block * limit + count - 1, -1)
    spreads, shares = [], []
    for g in range(total // group):
        here = slice(g * group, (g + 1) * group)
        hit = (
            lax.broadcasted_iota(jnp.int32, (group_slots, group), 0) + g * group_slots
            == slot[0:1, here]
        )
        shares.append(jnp.sum(jnp.where(hit, share[0:1, here], 0.0), axis=1, keepdims=True))
        pick = jnp.where(hit, 1.0, 0.0)
        spreads.append(pick.T.astype(jnp.bfloat16))
        pick = pick.astype(jnp.bfloat16)
        for start, size in tiles(width, 2 * step):
            cols = slice(start, start + size)
            both = jnp.concatenate([pieces[2 * g][:, cols], pieces[2 * g + 1][:, cols]], axis=0)
            picked[g * group_slots : (g + 1) * group_slots, cols] = jnp.dot(
                pick, both, preferred_element_type=jnp.float32
            ).astype(jnp.bfloat16)
    slot_share = jnp.concatenate(shares, axis=0)

    def activate(start, size, gate, up):
        here = slice(start, start + size)
        gate = jnp.minimum(gate + gate_bias[here, 0:1], swiglu_limit)
        up = jnp.clip(up + up_bias[here, 0:1], -swiglu_limit, swiglu_limit)
        value = gate * (1.0 / (1.0 + jnp.exp(-glu_alpha * gate))) * (up + 1.0)
        active[:, here] = value.T.astype(jnp.bfloat16)

    def give(start, size, value):
        cols = slice(start, start + size)
        scaled = (value * slot_share).astype(jnp.bfloat16)
        for g, spread in enumerate(spreads):
            sums = jnp.dot(
                spread,
                scaled[g * group_slots : (g + 1) * group_slots],
                preferred_element_type=jnp.float32,
            ).astype(jnp.bfloat16)
            near, far = outs[g // 2 * 4 + g % 2], outs[g // 2 * 4 + g % 2 + 2]
            near[:half, cols] = sums[:half]
            far[:half, cols] = sums[half:piece]
            near[half:, cols] = sums[piece : piece + half]
            far[half:, cols] = sums[piece + half :]

    last = None
    for start, size in tiles(units, step):
        here = slice(start, start + size)
        gate = by_rows(gate_w[here], picked[...])
        up = by_rows(up_w[here], picked[...])
        if last is not None:
            activate(*last)
        last = (start, size, gate, up)
    activate(*last)
    last = None
    for start, size in tiles(width, DOWN_STEP):
        cols = slice(start, start + size)
        value = jnp.dot(active[...], down_w[:, cols], preferred_element_type=jnp.float32)
        if last is not None:
            give(*last)
        last = (start, size, value)
    give(*last)


def attention_kernel(
    side_ref,
    expert_in_ref,
    pages_ref,
    sink_ref,
    queries_ref,
    keys_values_ref,
    segments_ref,
    inverse_ref,
    weight_hbm,
    own_ref,
    other_ref,
    cache_ref,
    expert_ref,
    weight,
    attended,
    sems,
):
    expert_ref[0] = expert_in_ref[0]
    length, query_width = queries_ref.shape
    width = weight.shape[0]
    kv_heads = keys_values_ref.shape[1] // LANES
    group_tiles = query_width // LANES // kv_heads
    chunks = tiles(width, 512)
    copies = [
        pltpu.make_async_copy(
            weight_hbm.at[pl.ds(start, size)], weight.at[pl.ds(start, size)], sems.at[i]
        )
        for i, (start, size) in enumerate(chunks)
    ]
    for copy in copies:
        copy.start()
    named = jnp.broadcast_to(segments_ref[...].astype(jnp.float32), (length, length))
    visible = (named == named.T) & (
        lax.broadcasted_iota(jnp.int32, (length, length), 1)
        <= lax.broadcasted_iota(jnp.int32, (length, length), 0)
    )
    positions = jnp.sum(jnp.where(visible, 1.0, 0.0), axis=1, keepdims=True) - 1.0
    angles = positions * inverse_ref[...]
    lane = lax.broadcasted_iota(jnp.int32, (length, LANES), 1)
    lower = lane % HEAD < HEAD // 2
    cosine = jnp.cos(angles)
    sine = jnp.sin(angles)
    sine = jnp.where(lower, -sine, sine)
    left = lane < HEAD

    def turned(tile):
        swapped = jnp.where(
            lower, pltpu.roll(tile, LANES - HEAD // 2, 1), pltpu.roll(tile, HEAD // 2, 1)
        )
        return tile * cosine + swapped * sine

    group_heads = 2 * group_tiles
    token = lax.broadcasted_iota(jnp.int32, (length, group_heads * length), 1)
    repeat = token % length == lax.broadcasted_iota(jnp.int32, token.shape, 0)
    seen = (
        jnp.dot(
            jnp.where(visible, 1.0, 0.0).T.astype(jnp.bfloat16),
            jnp.where(repeat, 1.0, 0.0).astype(jnp.bfloat16),
            preferred_element_type=jnp.float32,
        )
        > 0.5
    )
    head_of = lax.broadcasted_iota(jnp.int32, (1, group_heads * length), 1) // length
    for k in range(kv_heads):
        raw = keys_values_ref[:, k * LANES : (k + 1) * LANES].astype(jnp.float32)
        pair = jnp.where(left, turned(raw), raw).astype(jnp.bfloat16)
        for b in range(cache_ref.shape[0]):
            cache_ref[pages_ref[0, b], :, k * LANES : (k + 1) * LANES] = pair[
                b * PAGE_LEN : (b + 1) * PAGE_LEN
            ]
        heads = []
        sink = jnp.zeros(head_of.shape, jnp.float32)
        for h in range(group_heads):
            sink = jnp.where(head_of == h, sink_ref[k * group_heads + h], sink)
        for t in range(k * group_tiles, (k + 1) * group_tiles):
            tile = turned(queries_ref[:, t * LANES : (t + 1) * LANES].astype(jnp.float32))
            heads.append(jnp.where(left, tile, 0.0))
            heads.append(jnp.where(left, pltpu.roll(tile, HEAD, 1), 0.0))
        scores = by_rows(
            pair, jnp.concatenate(heads, axis=0).astype(jnp.bfloat16)
        ) * HEAD ** (-0.5)
        scores = jnp.where(seen, scores, -1e30)
        highest = jnp.maximum(jnp.max(scores, axis=0, keepdims=True), sink)
        expo = jnp.where(seen, jnp.exp(scores - highest), 0.0)
        denominator = jnp.sum(expo, axis=0, keepdims=True) + jnp.exp(sink - highest)
        probabilities = (expo / denominator).T.astype(jnp.bfloat16)
        mixed = jnp.dot(probabilities, pair, preferred_element_type=jnp.float32)
        for t in range(group_tiles):
            even = mixed[2 * t * length : (2 * t + 1) * length]
            odd = mixed[(2 * t + 1) * length : (2 * t + 2) * length]
            start = (k * group_tiles + t) * LANES
            attended[:, start : start + LANES] = jnp.where(
                left, pltpu.roll(even, HEAD, 1), odd
            ).astype(jnp.bfloat16)
    first_side = side_ref[0] == 0
    half = own_ref.shape[0]
    for i, (start, size) in enumerate(chunks):
        copies[i].wait()
        projected = by_rows(attended[...], weight[start : start + size])
        top, bottom = projected[:half], projected[half:]
        own_ref[:, start : start + size] = jnp.where(first_side, top, bottom)
        other_ref[:, start : start + size] = jnp.where(first_side, bottom, top).astype(jnp.bfloat16)


def run_attention(side, expert, page_table, sink_logits, queries, keys_values, segments, out_weight):
    length, query_width = queries.shape
    width = out_weight.shape[1]
    half = length // 2
    inverse = np.float32(rope_base) ** (
        -(np.arange(LANES) % (HEAD // 2)).astype(np.float32) / np.float32(HEAD // 2)
    )
    smem = pl.BlockSpec(memory_space=pltpu.SMEM)
    return pl.pallas_call(
        attention_kernel,
        out_shape=[
            jax.ShapeDtypeStruct((half, width), jnp.float32),
            jax.ShapeDtypeStruct((half, width), jnp.bfloat16),
            jax.ShapeDtypeStruct(
                (length // PAGE_LEN, PAGE_LEN, keys_values.shape[1]), jnp.bfloat16
            ),
            jax.ShapeDtypeStruct((1,), jnp.int32),
        ],
        in_specs=[smem] * 4 + [vmem()] * 4 + [anywhere()],
        out_specs=[vmem()] * 3 + [smem],
        scratch_shapes=[
            pltpu.VMEM((width, query_width), jnp.bfloat16),
            pltpu.VMEM((length, query_width), jnp.bfloat16),
            pltpu.SemaphoreType.DMA((len(tiles(width, 512)),)),
        ],
        compiler_params=pltpu.CompilerParams(vmem_limit_bytes=VMEM_LIMIT),
        name="attention",
    )(
        side,
        expert,
        page_table,
        sink_logits,
        queries,
        keys_values,
        segments[None],
        jnp.asarray(inverse.astype(np.float32))[None],
        out_weight.T,
    )


def vmem():
    return pl.BlockSpec(memory_space=pltpu.VMEM)


def anywhere():
    return pl.BlockSpec(memory_space=pl.ANY)


def run_expert(
    expert, pieces, gate_rows, gate_bias, up_rows, up_bias, down_weight, signs, block, limit
):
    parts = len(pieces)
    piece, padded = pieces[0].shape
    hidden_units, width = down_weight.shape
    slots = parts * piece // block * limit
    return pl.pallas_call(
        functools.partial(expert_kernel, parts, block, limit, 512),
        out_shape=[jax.ShapeDtypeStruct((piece, width), jnp.bfloat16)] * parts,
        in_specs=[pl.BlockSpec(memory_space=pltpu.SMEM)] + [vmem()] * (parts + 5)
        + [anywhere()] * 3,
        out_specs=[vmem()] * parts,
        scratch_shapes=[
            pltpu.VMEM((slots, width), jnp.bfloat16),
            pltpu.VMEM((slots, hidden_units), jnp.bfloat16),
        ],
        compiler_params=pltpu.CompilerParams(vmem_limit_bytes=8 * 2**20),
        cost_estimate=pl.CostEstimate(
            flops=6 * slots * width * hidden_units,
            bytes_accessed=6 * width * hidden_units,
            transcendentals=slots * hidden_units,
        ),
        name="expert",
    )(expert, *pieces, gate_rows, up_rows, down_weight, gate_bias, up_bias, *signs)


AXES = ("req", "tp")


def moved(array, n_req, step):
    outer, mid, core, tp = step
    pairs = []
    for source in range(2 * n_req):
        req, side = divmod(source, 2)
        place = (req // 4 ^ outer) * 4 + (req // 2 % 2 ^ mid) * 2 + (req % 2 ^ core)
        pairs.append((source, place * 2 + (side ^ tp)))
    return lax.ppermute(array, AXES, pairs)


def crossed(array, n_req, by_core):
    pairs = []
    for source in range(2 * n_req):
        req, side = divmod(source, 2)
        if req % 2 == by_core:
            pairs.append((source, (req ^ 2) * 2 + side))
        else:
            pairs.append((source, req * 2 + (side ^ 1)))
    return lax.ppermute(array, AXES, pairs)


def gather_rows(rows, n_req, weights, signs):
    outer = n_req // 4
    others = [moved(rows, n_req, (k, 0, 0, 0)) for k in range(1, outer)]
    weights[0], signs[0] = load(weights[0], rows, 40 * 2**20)
    others[0], signs[0] = lax.optimization_barrier((others[0], signs[0]))
    line = jnp.concatenate([rows] + others)
    first = crossed(line, n_req, 0)
    weights[1], signs[1] = load(weights[1], line, 2 * 2**20)
    late, signs[1] = lax.optimization_barrier((line, signs[1]))
    second = crossed(late, n_req, 1)
    both = crossed(first, n_req, 1)
    own = [line, first, second, both]
    sent = both
    weights[2], signs[2] = load(weights[2], line, 2 * 2**20)
    sent, signs[2] = lax.optimization_barrier((sent, signs[2]))
    pieces = own + [moved(piece, n_req, (0, 0, 1, 0)) for piece in (line, first, second, sent)]
    return pieces


def add_rows(left, right):
    return (left.astype(jnp.float32) + right.astype(jnp.float32)).astype(jnp.bfloat16)


def scatter_rows(sums, n_req):
    own, other = sums[:4], sums[4:]
    outer = n_req // 4
    half = outer // 2
    parts = []
    for side in (1, 0):
        here, beyond = [
            add_rows(own[i], moved(other[i], n_req, (0, 0, 1, 0)))
            for i in (2 * side, 2 * side + 1)
        ]
        here = add_rows(here, crossed(beyond, n_req, 1))
        middle = here.shape[0] // 2
        line = add_rows(here[:middle], crossed(here[middle:], n_req, 0))
        count = middle // half
        for i in range(half):
            block = line[i * count : (i + 1) * count]
            step = half * side + i
            parts.append(moved(block, n_req, (step, 0, 0, 0)) if step > 0 else block)
    return parts


def gathered_body(
    n_req,
    queries,
    keys_values,
    segments,
    sink_logits,
    out_weight,
    out_bias,
    residual,
    norm_gain,
    route_ids,
    route_logits,
    gate_weight,
    gate_bias,
    up_weight,
    up_bias,
    down_weight,
    down_bias,
    page_table,
):
    tok_count, width = residual.shape
    side = lax.axis_index("tp")[None]
    expert = lax.axis_index("req")[None]
    own, other, page_pool, expert = run_attention(
        side, expert, page_table, sink_logits, queries, keys_values, segments, out_weight
    )
    got = moved(other, n_req, (0, 0, 0, 1))
    weights = [gate_weight[0].T, up_weight[0].T, down_weight[0]]
    signs = [None] * len(weights)
    experts = down_bias.shape[0]
    base, rows = pl.pallas_call(
        mid_kernel,
        out_shape=[
            jax.ShapeDtypeStruct((tok_count, width), jnp.float32),
            jax.ShapeDtypeStruct((tok_count, width + 4 * experts), jnp.bfloat16),
        ],
        in_specs=[vmem()] * 6,
        out_specs=[vmem()] * 2,
        compiler_params=pltpu.CompilerParams(vmem_limit_bytes=4 * 2**20),
        name="norm_rows",
    )(
        own + residual.astype(jnp.float32) + out_bias.astype(jnp.float32),
        got,
        norm_gain[None],
        route_ids.T,
        route_logits.T,
        down_bias,
    )
    pieces = gather_rows(rows, n_req, weights, signs)
    sums = run_expert(
        expert,
        pieces,
        weights[0],
        gate_bias,
        weights[1],
        up_bias,
        weights[2],
        signs,
        tok_count,
        slot_limit(tok_count, route_ids.shape[1], experts),
    )
    mixed = base
    for part in scatter_rows(sums, n_req):
        mixed = mixed + part.astype(jnp.float32)
    return (mixed.astype(jnp.bfloat16), page_pool)


def solution(mesh):
    in_specs = (
        P("req", "tp"),
        P("req", "tp"),
        P("req"),
        P("tp"),
        P("tp", None),
        P(),
        P(("req", "tp"), None),
        P(),
        P(("req", "tp"), None),
        P(("req", "tp"), None),
        P("req", None, "tp"),
        P("req", "tp"),
        P("req", None, "tp"),
        P("req", "tp"),
        P("req", "tp", None),
        P(),
        P("req", None),
    )
    out_specs = (P(("req", "tp"), None), P("req", None, "tp"))
    n_req, n_tp = mesh.shape["req"], mesh.shape["tp"]
    chosen = functools.partial(gathered_body, n_req) if (n_req, n_tp) == (16, 2) else body
    return jax.shard_map(chosen, mesh=mesh, in_specs=in_specs, out_specs=out_specs, check_vma=False)
```

```python
import functools

import jax
import jax.numpy as jnp
import numpy as np
from jax import lax
from jax.experimental import pallas as pl
from jax.experimental.pallas import tpu as pltpu
from jax.sharding import PartitionSpec as P

HEAD = 64
PAGE_LEN = 16
LANES = 128
DOWN_STEP = 768
VMEM_LIMIT = 60 * 2**20
LOAD_ROWS = 480


rope_base = 150000.0
norm_eps = 1e-05
swiglu_limit = 7.0
glu_alpha = 1.702


def seg_positions(segment_ids):
    length = segment_ids.shape[0]
    indices = jnp.arange(length, dtype=jnp.int32)
    change = jnp.concatenate([jnp.ones((1,), dtype=bool), segment_ids[1:] != segment_ids[:-1]])
    starts = lax.cummax(jnp.where(change, indices, 0), axis=0)
    return indices - starts


def rotate(values, positions):
    half_dim = values.shape[-1] // 2
    inverse = rope_base ** (-jnp.arange(half_dim, dtype=jnp.float32) / half_dim)
    angles = positions.astype(jnp.float32)[:, None] * inverse[None, :]
    cosine = jnp.cos(angles)[:, None, :]
    sine_col = jnp.sin(angles)[:, None, :]
    first_half = values[..., :half_dim]
    second_half = values[..., half_dim:]
    return jnp.concatenate(
        [
            first_half * cosine - second_half * sine_col,
            second_half * cosine + first_half * sine_col,
        ],
        axis=-1,
    )


def attend_group(queries, keys_values, segment_ids, sink_logits):
    length = queries.shape[0]
    kv_heads = keys_values.shape[1] // (2 * HEAD)
    q_heads = queries.shape[1] // HEAD
    group_size = q_heads // kv_heads
    positions = seg_positions(segment_ids)
    q_rot = rotate(queries.astype(jnp.float32).reshape(length, q_heads, HEAD), positions).astype(
        jnp.bfloat16
    )
    q_rot = q_rot.reshape(length, kv_heads, group_size, HEAD)
    key_part = keys_values.reshape(length, kv_heads, 2, HEAD)
    k_rot = rotate(key_part[:, :, 0].astype(jnp.float32), positions).astype(jnp.bfloat16)
    values = key_part[:, :, 1]
    scores = jnp.einsum(
        "qkgd,skd->kgqs", q_rot, k_rot, preferred_element_type=jnp.float32
    ) * HEAD ** (-0.5)
    indices = jnp.arange(length, dtype=jnp.int32)
    visible = (segment_ids[:, None] == segment_ids[None, :]) & (
        indices[None, :] <= indices[:, None]
    )
    scores = jnp.where(visible, scores, -jnp.inf)
    sink_col = sink_logits.reshape(kv_heads, group_size)[:, :, None]
    highest = jnp.maximum(jnp.max(scores, axis=-1), sink_col)
    expo_terms = jnp.exp(scores - highest[..., None])
    denominator = jnp.sum(expo_terms, axis=-1) + jnp.exp(sink_col - highest)
    probabilities = (expo_terms / denominator[..., None]).astype(jnp.bfloat16)
    attended = jnp.einsum(
        "kgqs,skd->qkgd", probabilities, values, preferred_element_type=jnp.float32
    )
    attended = attended.astype(jnp.bfloat16).reshape(length, q_heads * HEAD)
    cached = jnp.stack([k_rot, values], axis=2).reshape(length, kv_heads * 2 * HEAD)
    return (attended, cached)


def slot_index(routes, experts, capacity):
    blocks, row_count, route_width = routes.shape
    flat_ids = routes.reshape(blocks, row_count * route_width)
    onehot = (flat_ids[:, :, None] == jnp.arange(experts, dtype=jnp.int32)[None, None, :]).astype(
        jnp.int32
    )
    earlier = jnp.cumsum(onehot, axis=1) - onehot
    position = jnp.sum(earlier * onehot, axis=2)
    block_ids = jnp.arange(blocks, dtype=jnp.int32)[:, None]
    slot_ids = flat_ids * (blocks * capacity) + block_ids * capacity + position
    return slot_ids.reshape(blocks * row_count, route_width).astype(jnp.int32)


def dispatch(tokens, slot_ids, slot_total):
    row_count = tokens.shape[0]
    owners = jnp.broadcast_to(jnp.arange(row_count, dtype=jnp.int32)[:, None], slot_ids.shape)
    member = (
        jnp.full((slot_total,), row_count, jnp.int32)
        .at[slot_ids.reshape(-1)]
        .set(owners.reshape(-1))
    )
    padded = jnp.concatenate([tokens, jnp.zeros((1, tokens.shape[1]), tokens.dtype)], axis=0)
    return padded[member]


def slot_limit(tok_count, route_width, experts):
    return max(2, 2 * tok_count * route_width // experts)


def body(
    queries,
    keys_values,
    segments,
    sink_logits,
    out_weight,
    out_bias,
    residual,
    norm_gain,
    route_ids,
    route_logits,
    gate_weight,
    gate_bias,
    up_weight,
    up_bias,
    down_weight,
    down_bias,
    page_table,
):
    attended, cached = attend_group(queries, keys_values, segments, sink_logits)
    projected = lax.psum_scatter(
        jnp.dot(attended, out_weight, preferred_element_type=jnp.float32).astype(jnp.bfloat16),
        "tp",
        scatter_dimension=0,
        tiled=True,
    ).astype(jnp.float32)
    hidden = (residual.astype(jnp.float32) + projected + out_bias.astype(jnp.float32)).astype(
        jnp.bfloat16
    )
    stream = hidden.astype(jnp.float32)
    normed = (
        stream
        * lax.rsqrt(jnp.mean(stream * stream, axis=-1, keepdims=True) + norm_eps)
        * norm_gain.astype(jnp.float32)
    ).astype(jnp.bfloat16)
    route_weights = jax.nn.softmax(route_logits, axis=-1)
    tok_count, route_width = route_ids.shape
    experts = down_bias.shape[0]
    model_width = residual.shape[1]
    capacity = slot_limit(tok_count, route_width, experts)
    own_slots = slot_index(route_ids[None], experts, capacity)
    group_rows, group_routes = (
        lax.all_gather(normed, "tp", axis=0, tiled=True),
        lax.all_gather(route_ids, "tp", axis=0, tiled=True),
    )
    tp_count = group_rows.shape[0] // tok_count
    all_slots = slot_index(
        group_routes.reshape(tp_count, tok_count, route_width), experts, capacity
    )
    dispatched = dispatch(group_rows, all_slots, experts * tp_count * capacity).reshape(
        experts, tp_count, capacity, model_width
    )
    received = lax.all_to_all(dispatched, "req", split_axis=0, concat_axis=0, tiled=True)
    slot_shape = received.shape
    flat_rows = received.reshape(-1, model_width)
    gate_act = jnp.dot(flat_rows, gate_weight[0], preferred_element_type=jnp.float32) + gate_bias[
        0
    ].astype(jnp.float32)
    up_act = jnp.dot(flat_rows, up_weight[0], preferred_element_type=jnp.float32) + up_bias[
        0
    ].astype(jnp.float32)
    gate_act = jnp.minimum(gate_act, swiglu_limit)
    up_act = jnp.clip(up_act, -swiglu_limit, swiglu_limit)
    active = (gate_act * jax.nn.sigmoid(glu_alpha * gate_act) * (up_act + 1.0)).astype(jnp.bfloat16)
    partial_value = jnp.dot(active, down_weight[0], preferred_element_type=jnp.float32).reshape(
        slot_shape
    )
    summed = lax.psum_scatter(
        partial_value.astype(jnp.bfloat16), "tp", scatter_dimension=1, tiled=True
    ).astype(jnp.float32)
    returned = lax.all_to_all(
        summed.astype(jnp.bfloat16), "req", split_axis=0, concat_axis=0, tiled=True
    ).astype(summed.dtype)
    returned = returned.reshape(experts * capacity, model_width)
    slot_onehot = (
        own_slots[:, :, None] == jnp.arange(experts * capacity, dtype=jnp.int32)[None, None, :]
    ).astype(jnp.float32)
    combiner = jnp.einsum("rk,rks->rs", route_weights, slot_onehot, precision=lax.Precision.HIGHEST)
    expert_onehot = (
        route_ids[:, :, None] == jnp.arange(experts, dtype=jnp.int32)[None, None, :]
    ).astype(jnp.float32)
    dense_weights = jnp.einsum(
        "rk,rke->re", route_weights, expert_onehot, precision=lax.Precision.HIGHEST
    )
    expert_mix = jnp.dot(
        combiner, returned, precision=lax.Precision.HIGHEST, preferred_element_type=jnp.float32
    )
    expert_mix = expert_mix + jnp.dot(
        dense_weights,
        down_bias.astype(jnp.float32),
        precision=lax.Precision.HIGHEST,
        preferred_element_type=jnp.float32,
    )
    mixed_out = (stream + expert_mix).astype(jnp.bfloat16)
    blocks = cached.reshape(-1, PAGE_LEN, cached.shape[1])
    page_pool = jnp.zeros_like(blocks).at[page_table[0]].set(blocks)
    return (mixed_out, page_pool)


def mid_kernel(
    own_ref,
    got_ref,
    gain_ref,
    ids_ref,
    logits_ref,
    down_bias_ref,
    base_ref,
    rows_ref,
):
    width = own_ref.shape[1]
    experts = down_bias_ref.shape[0]
    hidden = (own_ref[...] + got_ref[...].astype(jnp.float32)).astype(jnp.bfloat16)
    stream = hidden.astype(jnp.float32)
    normed = (
        stream
        * lax.rsqrt(jnp.mean(stream * stream, axis=-1, keepdims=True) + norm_eps)
        * gain_ref[...].astype(jnp.float32)
    ).astype(jnp.bfloat16)
    logits = logits_ref[...]
    expo = jnp.exp(logits - jnp.max(logits, axis=0, keepdims=True))
    weights = expo / jnp.sum(expo, axis=0, keepdims=True)
    high = weights.astype(jnp.bfloat16).astype(jnp.float32)
    low = (weights - high).astype(jnp.bfloat16).astype(jnp.float32)
    ids = ids_ref[...]
    column = lax.broadcasted_iota(jnp.int32, (LANES, ids.shape[1]), 0)
    high_cols = jnp.zeros(column.shape, jnp.float32)
    low_cols = jnp.zeros(column.shape, jnp.float32)
    first = width % LANES
    for k in range(ids.shape[0]):
        at = ids[k : k + 1] + first
        high_cols = high_cols + jnp.where(column == at, high[k : k + 1], 0.0)
        low_cols = low_cols + jnp.where(column == at + experts, low[k : k + 1], 0.0)
    high_cols = high_cols.T
    low_cols = low_cols.T
    high_dense = high_cols[:, first : first + experts].astype(jnp.bfloat16)
    low_dense = low_cols[:, first + experts : first + 2 * experts].astype(jnp.bfloat16)
    bias = down_bias_ref[...]
    base_ref[...] = (
        stream
        + jnp.dot(high_dense, bias, preferred_element_type=jnp.float32)
        + jnp.dot(low_dense, bias, preferred_element_type=jnp.float32)
    )
    rows_ref[:, :width] = normed
    rows_ref[:, width:] = (high_cols + low_cols)[:, first:].astype(jnp.bfloat16)


def tiles(total, step):
    return [(start, min(step, total - start)) for start in range(0, total, step)]


def by_rows(left, right):
    return lax.dot_general(
        left, right, (((1,), (1,)), ((), ())), preferred_element_type=jnp.float32
    )


def load_kernel(after_ref, source, target, sign, sems):
    copies = []
    for i, (start, size) in enumerate(tiles(source.shape[0], LOAD_ROWS)):
        here = pl.ds(start, size)
        copies.append(pltpu.make_async_copy(source.at[here], target.at[here], sems.at[i]))
    for copy in copies:
        copy.start()
    for copy in copies:
        copy.wait()
    sign[...] = target[: sign.shape[0], : sign.shape[1]]


def load(weight, after, reserve):
    return pl.pallas_call(
        load_kernel,
        out_shape=[
            jax.ShapeDtypeStruct(weight.shape, weight.dtype),
            jax.ShapeDtypeStruct((16, LANES), weight.dtype),
        ],
        in_specs=[anywhere()] * 2,
        out_specs=[vmem()] * 2,
        scratch_shapes=[pltpu.SemaphoreType.DMA((len(tiles(weight.shape[0], LOAD_ROWS)),))],
        compiler_params=pltpu.CompilerParams(vmem_limit_bytes=reserve),
        cost_estimate=pl.CostEstimate(
            flops=0, bytes_accessed=4 * weight.size, transcendentals=0
        ),
        name="load",
    )(after, weight)


def expert_kernel(parts, block, limit, step, expert_ref, *refs):
    pieces, refs = refs[:parts], refs[parts:]
    gate_w, up_w, down_w, gate_bias_ref, up_bias_ref = refs[:5]
    outs, (picked, active) = refs[8 : 8 + parts], refs[8 + parts :]
    piece, padded = pieces[0].shape
    total = parts * piece
    units, width = down_w.shape
    group = 2 * piece
    half = piece // 2
    group_slots = group // block * limit
    up_bias = jnp.broadcast_to(up_bias_ref[...].astype(jnp.float32), (8, units)).T
    gate_bias = jnp.broadcast_to(gate_bias_ref[...].astype(jnp.float32), (8, units)).T

    expert = expert_ref[0]
    experts = (padded - width) // 4
    lane = lax.broadcasted_iota(jnp.int32, (16, LANES), 1)
    which = lax.broadcasted_iota(jnp.int32, (16, LANES), 0)
    choose = jnp.where(
        (lane == width % LANES + expert + which * experts) & (which < 2), 1.0, 0.0
    ).astype(jnp.bfloat16)
    found = by_rows(
        choose, jnp.concatenate([p[:, padded - LANES :] for p in pieces], axis=0)
    )
    share = jnp.broadcast_to(found[0:1] + found[1:2], (8, total))
    chosen = share > 0.0
    token = lax.broadcasted_iota(jnp.int32, (8, total), 1)
    count = jnp.where(chosen, 1, 0)
    reach = 1
    while reach < block:
        count = count + jnp.where(token % block >= reach, pltpu.roll(count, reach, 1), 0)
        reach *= 2
    slot = jnp.where(chosen, token // block * limit + count - 1, -1)
    spreads, shares = [], []
    for g in range(total // group):
        here = slice(g * group, (g + 1) * group)
        hit = (
            lax.broadcasted_iota(jnp.int32, (group_slots, group), 0) + g * group_slots
            == slot[0:1, here]
        )
        shares.append(jnp.sum(jnp.where(hit, share[0:1, here], 0.0), axis=1, keepdims=True))
        pick = jnp.where(hit, 1.0, 0.0)
        spreads.append(pick.T.astype(jnp.bfloat16))
        pick = pick.astype(jnp.bfloat16)
        for start, size in tiles(width, 2 * step):
            cols = slice(start, start + size)
            both = jnp.concatenate([pieces[2 * g][:, cols], pieces[2 * g + 1][:, cols]], axis=0)
            picked[g * group_slots : (g + 1) * group_slots, cols] = jnp.dot(
                pick, both, preferred_element_type=jnp.float32
            ).astype(jnp.bfloat16)
    slot_share = jnp.concatenate(shares, axis=0)

    def activate(start, size, gate, up):
        here = slice(start, start + size)
        gate = jnp.minimum(gate + gate_bias[here, 0:1], swiglu_limit)
        up = jnp.clip(up + up_bias[here, 0:1], -swiglu_limit, swiglu_limit)
        value = gate * (1.0 / (1.0 + jnp.exp(-glu_alpha * gate))) * (up + 1.0)
        active[:, here] = value.T.astype(jnp.bfloat16)

    def give(start, size, value):
        cols = slice(start, start + size)
        scaled = (value * slot_share).astype(jnp.bfloat16)
        for g, spread in enumerate(spreads):
            sums = jnp.dot(
                spread,
                scaled[g * group_slots : (g + 1) * group_slots],
                preferred_element_type=jnp.float32,
            ).astype(jnp.bfloat16)
            near, far = outs[g // 2 * 4 + g % 2], outs[g // 2 * 4 + g % 2 + 2]
            near[:half, cols] = sums[:half]
            far[:half, cols] = sums[half:piece]
            near[half:, cols] = sums[piece : piece + half]
            far[half:, cols] = sums[piece + half :]

    last = None
    for start, size in tiles(units, step):
        here = slice(start, start + size)
        gate = by_rows(gate_w[here], picked[...])
        up = by_rows(up_w[here], picked[...])
        if last is not None:
            activate(*last)
        last = (start, size, gate, up)
    activate(*last)
    last = None
    for start, size in tiles(width, DOWN_STEP):
        cols = slice(start, start + size)
        value = jnp.dot(active[...], down_w[:, cols], preferred_element_type=jnp.float32)
        if last is not None:
            give(*last)
        last = (start, size, value)
    give(*last)


def attention_kernel(
    side_ref,
    expert_in_ref,
    pages_ref,
    sink_ref,
    queries_ref,
    keys_values_ref,
    segments_ref,
    inverse_ref,
    weight_hbm,
    own_ref,
    other_ref,
    cache_ref,
    expert_ref,
    weight,
    attended,
    sems,
):
    expert_ref[0] = expert_in_ref[0]
    length, query_width = queries_ref.shape
    width = weight.shape[0]
    kv_heads = keys_values_ref.shape[1] // LANES
    group_tiles = query_width // LANES // kv_heads
    chunks = tiles(width, 512)
    copies = [
        pltpu.make_async_copy(
            weight_hbm.at[pl.ds(start, size)], weight.at[pl.ds(start, size)], sems.at[i]
        )
        for i, (start, size) in enumerate(chunks)
    ]
    for copy in copies:
        copy.start()
    named = jnp.broadcast_to(segments_ref[...].astype(jnp.float32), (length, length))
    visible = (named == named.T) & (
        lax.broadcasted_iota(jnp.int32, (length, length), 1)
        <= lax.broadcasted_iota(jnp.int32, (length, length), 0)
    )
    positions = jnp.sum(jnp.where(visible, 1.0, 0.0), axis=1, keepdims=True) - 1.0
    angles = positions * inverse_ref[...]
    lane = lax.broadcasted_iota(jnp.int32, (length, LANES), 1)
    lower = lane % HEAD < HEAD // 2
    cosine = jnp.cos(angles)
    sine = jnp.sin(angles)
    sine = jnp.where(lower, -sine, sine)
    left = lane < HEAD

    def turned(tile):
        swapped = jnp.where(
            lower, pltpu.roll(tile, LANES - HEAD // 2, 1), pltpu.roll(tile, HEAD // 2, 1)
        )
        return tile * cosine + swapped * sine

    group_heads = 2 * group_tiles
    token = lax.broadcasted_iota(jnp.int32, (length, group_heads * length), 1)
    repeat = token % length == lax.broadcasted_iota(jnp.int32, token.shape, 0)
    seen = (
        jnp.dot(
            jnp.where(visible, 1.0, 0.0).T.astype(jnp.bfloat16),
            jnp.where(repeat, 1.0, 0.0).astype(jnp.bfloat16),
            preferred_element_type=jnp.float32,
        )
        > 0.5
    )
    head_of = lax.broadcasted_iota(jnp.int32, (1, group_heads * length), 1) // length
    for k in range(kv_heads):
        raw = keys_values_ref[:, k * LANES : (k + 1) * LANES].astype(jnp.float32)
        pair = jnp.where(left, turned(raw), raw).astype(jnp.bfloat16)
        for b in range(cache_ref.shape[0]):
            cache_ref[pages_ref[0, b], :, k * LANES : (k + 1) * LANES] = pair[
                b * PAGE_LEN : (b + 1) * PAGE_LEN
            ]
        heads = []
        sink = jnp.zeros(head_of.shape, jnp.float32)
        for h in range(group_heads):
            sink = jnp.where(head_of == h, sink_ref[k * group_heads + h], sink)
        for t in range(k * group_tiles, (k + 1) * group_tiles):
            tile = turned(queries_ref[:, t * LANES : (t + 1) * LANES].astype(jnp.float32))
            heads.append(jnp.where(left, tile, 0.0))
            heads.append(jnp.where(left, pltpu.roll(tile, HEAD, 1), 0.0))
        scores = by_rows(
            pair, jnp.concatenate(heads, axis=0).astype(jnp.bfloat16)
        ) * HEAD ** (-0.5)
        scores = jnp.where(seen, scores, -1e30)
        highest = jnp.maximum(jnp.max(scores, axis=0, keepdims=True), sink)
        expo = jnp.where(seen, jnp.exp(scores - highest), 0.0)
        denominator = jnp.sum(expo, axis=0, keepdims=True) + jnp.exp(sink - highest)
        probabilities = (expo / denominator).T.astype(jnp.bfloat16)
        mixed = jnp.dot(probabilities, pair, preferred_element_type=jnp.float32)
        for t in range(group_tiles):
            even = mixed[2 * t * length : (2 * t + 1) * length]
            odd = mixed[(2 * t + 1) * length : (2 * t + 2) * length]
            start = (k * group_tiles + t) * LANES
            attended[:, start : start + LANES] = jnp.where(
                left, pltpu.roll(even, HEAD, 1), odd
            ).astype(jnp.bfloat16)
    first_side = side_ref[0] == 0
    half = own_ref.shape[0]
    for i, (start, size) in enumerate(chunks):
        copies[i].wait()
        projected = by_rows(attended[...], weight[start : start + size])
        top, bottom = projected[:half], projected[half:]
        own_ref[:, start : start + size] = jnp.where(first_side, top, bottom)
        other_ref[:, start : start + size] = jnp.where(first_side, bottom, top).astype(jnp.bfloat16)


def run_attention(side, expert, page_table, sink_logits, queries, keys_values, segments, out_weight):
    length, query_width = queries.shape
    width = out_weight.shape[1]
    half = length // 2
    inverse = np.float32(rope_base) ** (
        -(np.arange(LANES) % (HEAD // 2)).astype(np.float32) / np.float32(HEAD // 2)
    )
    smem = pl.BlockSpec(memory_space=pltpu.SMEM)
    return pl.pallas_call(
        attention_kernel,
        out_shape=[
            jax.ShapeDtypeStruct((half, width), jnp.float32),
            jax.ShapeDtypeStruct((half, width), jnp.bfloat16),
            jax.ShapeDtypeStruct(
                (length // PAGE_LEN, PAGE_LEN, keys_values.shape[1]), jnp.bfloat16
            ),
            jax.ShapeDtypeStruct((1,), jnp.int32),
        ],
        in_specs=[smem] * 4 + [vmem()] * 4 + [anywhere()],
        out_specs=[vmem()] * 3 + [smem],
        scratch_shapes=[
            pltpu.VMEM((width, query_width), jnp.bfloat16),
            pltpu.VMEM((length, query_width), jnp.bfloat16),
            pltpu.SemaphoreType.DMA((len(tiles(width, 512)),)),
        ],
        compiler_params=pltpu.CompilerParams(vmem_limit_bytes=VMEM_LIMIT),
        name="attention",
    )(
        side,
        expert,
        page_table,
        sink_logits,
        queries,
        keys_values,
        segments[None],
        jnp.asarray(inverse.astype(np.float32))[None],
        out_weight.T,
    )


def vmem():
    return pl.BlockSpec(memory_space=pltpu.VMEM)


def anywhere():
    return pl.BlockSpec(memory_space=pl.ANY)


def run_expert(
    expert, pieces, gate_rows, gate_bias, up_rows, up_bias, down_weight, signs, block, limit
):
    parts = len(pieces)
    piece, padded = pieces[0].shape
    hidden_units, width = down_weight.shape
    slots = parts * piece // block * limit
    return pl.pallas_call(
        functools.partial(expert_kernel, parts, block, limit, 512),
        out_shape=[jax.ShapeDtypeStruct((piece, width), jnp.bfloat16)] * parts,
        in_specs=[pl.BlockSpec(memory_space=pltpu.SMEM)] + [vmem()] * (parts + 5)
        + [anywhere()] * 3,
        out_specs=[vmem()] * parts,
        scratch_shapes=[
            pltpu.VMEM((slots, width), jnp.bfloat16),
            pltpu.VMEM((slots, hidden_units), jnp.bfloat16),
        ],
        compiler_params=pltpu.CompilerParams(vmem_limit_bytes=8 * 2**20),
        cost_estimate=pl.CostEstimate(
            flops=6 * slots * width * hidden_units,
            bytes_accessed=6 * width * hidden_units,
            transcendentals=slots * hidden_units,
        ),
        name="expert",
    )(expert, *pieces, gate_rows, up_rows, down_weight, gate_bias, up_bias, *signs)


AXES = ("req", "tp")


def moved(array, n_req, step):
    outer, mid, core, tp = step
    pairs = []
    for source in range(2 * n_req):
        req, side = divmod(source, 2)
        place = (req // 4 ^ outer) * 4 + (req // 2 % 2 ^ mid) * 2 + (req % 2 ^ core)
        pairs.append((source, place * 2 + (side ^ tp)))
    return lax.ppermute(array, AXES, pairs)


def crossed(array, n_req, by_core):
    pairs = []
    for source in range(2 * n_req):
        req, side = divmod(source, 2)
        if req % 2 == by_core:
            pairs.append((source, (req ^ 2) * 2 + side))
        else:
            pairs.append((source, req * 2 + (side ^ 1)))
    return lax.ppermute(array, AXES, pairs)


def gather_rows(rows, n_req, weights, signs):
    outer = n_req // 4
    others = [moved(rows, n_req, (k, 0, 0, 0)) for k in range(1, outer)]
    weights[0], signs[0] = load(weights[0], rows, 40 * 2**20)
    others[0], signs[0] = lax.optimization_barrier((others[0], signs[0]))
    line = jnp.concatenate([rows] + others)
    first = crossed(line, n_req, 0)
    weights[1], signs[1] = load(weights[1], line, 2 * 2**20)
    late, signs[1] = lax.optimization_barrier((line, signs[1]))
    second = crossed(late, n_req, 1)
    both = crossed(first, n_req, 1)
    own = [line, first, second, both]
    sent = both
    weights[2], signs[2] = load(weights[2], line, 2 * 2**20)
    sent, signs[2] = lax.optimization_barrier((sent, signs[2]))
    pieces = own + [moved(piece, n_req, (0, 0, 1, 0)) for piece in (line, first, second, sent)]
    return pieces


def add_rows(left, right):
    return (left.astype(jnp.float32) + right.astype(jnp.float32)).astype(jnp.bfloat16)


def scatter_rows(sums, n_req):
    own, other = sums[:4], sums[4:]
    outer = n_req // 4
    half = outer // 2
    parts = []
    for side in (1, 0):
        here, beyond = [
            add_rows(own[i], moved(other[i], n_req, (0, 0, 1, 0)))
            for i in (2 * side, 2 * side + 1)
        ]
        here = add_rows(here, crossed(beyond, n_req, 1))
        middle = here.shape[0] // 2
        line = add_rows(here[:middle], crossed(here[middle:], n_req, 0))
        count = middle // half
        for i in range(half):
            block = line[i * count : (i + 1) * count]
            step = half * side + i
            parts.append(moved(block, n_req, (step, 0, 0, 0)) if step > 0 else block)
    return parts


def gathered_body(
    n_req,
    queries,
    keys_values,
    segments,
    sink_logits,
    out_weight,
    out_bias,
    residual,
    norm_gain,
    route_ids,
    route_logits,
    gate_weight,
    gate_bias,
    up_weight,
    up_bias,
    down_weight,
    down_bias,
    page_table,
):
    tok_count, width = residual.shape
    side = lax.axis_index("tp")[None]
    expert = lax.axis_index("req")[None]
    own, other, page_pool, expert = run_attention(
        side, expert, page_table, sink_logits, queries, keys_values, segments, out_weight
    )
    got = moved(other, n_req, (0, 0, 0, 1))
    weights = [gate_weight[0].T, up_weight[0].T, down_weight[0]]
    signs = [None] * len(weights)
    experts = down_bias.shape[0]
    base, rows = pl.pallas_call(
        mid_kernel,
        out_shape=[
            jax.ShapeDtypeStruct((tok_count, width), jnp.float32),
            jax.ShapeDtypeStruct((tok_count, width + 4 * experts), jnp.bfloat16),
        ],
        in_specs=[vmem()] * 6,
        out_specs=[vmem()] * 2,
        compiler_params=pltpu.CompilerParams(vmem_limit_bytes=4 * 2**20),
        name="norm_rows",
    )(
        own + residual.astype(jnp.float32) + out_bias.astype(jnp.float32),
        got,
        norm_gain[None],
        route_ids.T,
        route_logits.T,
        down_bias,
    )
    pieces = gather_rows(rows, n_req, weights, signs)
    sums = run_expert(
        expert,
        pieces,
        weights[0],
        gate_bias,
        weights[1],
        up_bias,
        weights[2],
        signs,
        tok_count,
        slot_limit(tok_count, route_ids.shape[1], experts),
    )
    mixed = base
    for part in scatter_rows(sums, n_req):
        mixed = mixed + part.astype(jnp.float32)
    return (mixed.astype(jnp.bfloat16), page_pool)


def solution(mesh):
    in_specs = (
        P("req", "tp"),
        P("req", "tp"),
        P("req"),
        P("tp"),
        P("tp", None),
        P(),
        P(("req", "tp"), None),
        P(),
        P(("req", "tp"), None),
        P(("req", "tp"), None),
        P("req", None, "tp"),
        P("req", "tp"),
        P("req", None, "tp"),
        P("req", "tp"),
        P("req", "tp", None),
        P(),
        P("req", None),
    )
    out_specs = (P(("req", "tp"), None), P("req", None, "tp"))
    n_req, n_tp = mesh.shape["req"], mesh.shape["tp"]
    chosen = functools.partial(gathered_body, n_req) if (n_req, n_tp) == (16, 2) else body
    return jax.shard_map(chosen, mesh=mesh, in_specs=in_specs, out_specs=out_specs, check_vma=False)
```
